512 devices in a mesh: ctx: 16 (over y, x), exp: 32 (over z, core).
Axes of the slice: x: 4, y: 4, z: 16, core: 2. Of those that a mesh axis runs over, the one named last changes fastest.
Arguments:
- features: bfloat16 [2048, 65536], P('exp', 'ctx'), may hold values from -36 to 36
- write_vectors: bfloat16 [128, 65536], P(None, 'ctx'), may hold values from -0.5 to 0.5
- read_vectors: bfloat16 [128, 65536], P(None, 'ctx'), may hold values from -6 to 6
- log_decay: float32 [64, 65536], P('exp', 'ctx'), may hold values from -0.8 to 0, as said below
- doc_lengths: int32 [8], replicated, may hold values from 1 to 16384, 65536 in all
- expert_ids: int32 [65536, 2], P(('ctx', 'exp')), may hold values from 0 to 31, all different within a row; in each aligned block of 128 rows (0 to 127, 128 to 255, ...) at most 10 rows name the same one
- route_weights: float32 [65536, 2], P(('ctx', 'exp')), may hold values from 0.2 to 1
- norm_gain: float32 [2048], replicated, may hold values from 0.1 to 1.9
- expert_in: bfloat16 [32, 2048, 1536], P('exp', 'ctx'), may hold values from -0.125 to 0.125
- expert_out: bfloat16 [32, 2048, 768], P('exp', 'ctx'), may hold values from -0.21875 to 0.21875
- out_grad: bfloat16 [2048, 65536], P(None, ('ctx', 'exp')), may hold values from -6 to 6
Outputs:
- block_out: bfloat16 [2048, 65536], P(None, ('ctx', 'exp'))
- input_grad: bfloat16 [2048, 65536], P('exp', 'ctx')
The draws below stay inside these ranges and needn't reach their ends.
Inputs may be any that keep to these rules, and one draw needn't show every extreme that they name: `expert_ids`: over the 128 rows of one device no expert is named more than 10 times; the ids of a row differ. `log_decay`: strictly negative.
All inputs are finite; a program needn't handle non-finite values.
Results may differ from the reference program's by a relative error of at most 0.017.
Values may be sent and summed in bfloat16 or wider, within the bound.
No kernel may reach another device: no remote copies, remote signals or barrier semaphores. Data moves between devices by JAX's collectives and lax.ppermute only.
A program may use at most 128 MiB of HBM per device.

```python
import math
import jax
import jax.numpy as jnp
import numpy as np
from jax import lax

HEADS = 64
STATE = 128
FF = 768
TOPK = 2
DOCS = 8
TOK_DEV = 128
D = 2048
EXPERTS = 32
TOKEN_COUNT = 65536
CAP = 10


def draw_features(key, part):
    key = jax.random.fold_in(key, 11)
    key_noise, key_rows, key_cols = jax.random.split(key, 3)
    row_scale = jnp.exp(jax.random.uniform(key_rows, (D, 1), jnp.float32, math.log(0.3), math.log(3.0)))
    col_scale = jnp.exp(jax.random.uniform(key_cols, (1, TOKEN_COUNT), jnp.float32, math.log(0.3), math.log(3.0)))
    base_value = jnp.clip(jax.random.normal(key_noise, (D, TOKEN_COUNT), jnp.float32), -4.0, 4.0)
    return (base_value * row_scale * col_scale).astype(jnp.bfloat16)


def draw_log_decay(key, part):
    key = jax.random.fold_in(key, 23)
    key_variety, key_quick, key_gradual, key_jagged, key_spike, key_objective = jax.random.split(key, 6)
    slow_share = 0.5
    slow_heads = jax.random.uniform(key_variety, (HEADS, 1), jnp.float32) < slow_share
    fast_rate = jnp.exp(jax.random.uniform(key_quick, (HEADS, 1), jnp.float32, math.log(1.0 / 50.0), math.log(1.0 / 30.0)))
    slow_rate = jnp.exp(jax.random.uniform(key_gradual, (HEADS, 1), jnp.float32, math.log(0.0001), math.log(0.001)))
    decay_speed = jnp.where(slow_heads, slow_rate, fast_rate)
    jaggedness = jax.random.uniform(key_jagged, (HEADS, TOKEN_COUNT), jnp.float32, 0.5, 1.5)
    spike_mask = jax.random.uniform(key_spike, (1, TOKEN_COUNT), jnp.float32) < 4.0 / TOKEN_COUNT
    spike_loss = jax.random.uniform(key_objective, (1, TOKEN_COUNT), jnp.float32, 0.22, 0.69)
    return -(decay_speed * jaggedness) - jnp.where(spike_mask, spike_loss, 0.0)


def steps_of(key, dims, shards, low, high):
    factor_of, own = 1.0, jax.random.fold_in(key, 6)
    for dim, shards_of in shards:
        draws = jnp.exp(jax.random.uniform(jax.random.fold_in(own, dim), (shards_of,), jnp.float32, low / len(shards), high / len(shards)))
        factor_of = factor_of * jnp.repeat(draws, dims[dim] // shards_of).reshape([-1 if axis == dim else 1 for axis in range(len(dims))])
    return factor_of


def split_up(number_of, total, limit, lean):
    portions = [(1 << 20) // math.isqrt(standing ** lean) + 1 for standing in range(2, number_of + 1)]
    surplus, counts = total - limit - (number_of - 1), [1] * (number_of - 1)
    while surplus > 0:
        free = [i for i in range(number_of - 1) if counts[i] < limit]
        pool, left = sum([portions[i] for i in free]), surplus
        for i in free:
            more = min(limit - counts[i], max(1, left * portions[i] // pool), surplus)
            counts[i] = counts[i] + more
            surplus = surplus - more
    return np.array([limit] + counts)


def ragged(own_key, count, total, bound, lean):
    if count == 2:
        one = jax.random.randint(own_key, (), max(1, total - bound), min(bound, total - 1) + 1)
        return jnp.stack([one, total - one])
    sizes = jnp.asarray(split_up(count, total, bound, lean), jnp.int32)
    twos = (count - 1) // 2
    source_of, receiver = sizes[1:1 + 2 * twos:2], sizes[2:2 + 2 * twos:2]
    room = jnp.minimum(source_of - 1, bound - receiver)
    shifted = jax.random.randint(jax.random.fold_in(own_key, 1), (twos,), 0, 1 << 20) % (room + 1)
    sizes = sizes.at[1:1 + 2 * twos:2].set(source_of - shifted).at[2:2 + 2 * twos:2].set(receiver + shifted)
    return sizes[jax.random.permutation(jax.random.fold_in(own_key, 2), count)]


def shared_out(key, own, number, rows, number_of, top, bound, slope):
    ranking = jax.random.permutation(key, number_of)
    packed, common = shares(number_of, rows * top, bound, slope, True), shares(number_of, rows * top, bound, slope, False)
    places = jnp.arange(number_of)

    def named(sizes, turn):
        used = int((sizes > 0).sum())
        fixed = max(1, used // 4)
        shifted = fixed + (places - fixed + turn * (used - fixed)) % max(1, number_of - fixed)
        return jnp.zeros((number_of,), jnp.int32).at[ranking[jnp.where(places < fixed, places, shifted)]].set(jnp.asarray(sizes, jnp.int32))

    sizes = jnp.where(number % 4 == 0, named(packed, number // 4), named(common, number - number // 4 - 1))
    mixed = jax.random.permutation(jax.random.fold_in(own, 3), number_of)
    giver, taker = mixed[0:number_of // 2 * 2:2], mixed[1:number_of // 2 * 2:2]
    slack = jnp.minimum(sizes[giver] - 1, bound - sizes[taker]) // 2
    slack = jnp.where((giver == ranking[0]) | (taker == ranking[0]) | (sizes[taker] == 0), 0, jnp.maximum(slack, 0))
    shifted = jax.random.randint(jax.random.fold_in(own, 4), (number_of // 2,), 0, 1 << 20) % (slack + 1)
    sizes = sizes.at[giver].add(-shifted).at[taker].add(shifted)
    members = jnp.searchsorted(jnp.cumsum(sizes), jnp.arange(rows * top), side="right").astype(jnp.int32)
    grid = members.reshape(top, rows).T
    grid = grid[jax.random.permutation(jax.random.fold_in(own, 1), rows)]
    turn = jax.random.randint(jax.random.fold_in(own, 2), (rows, 1), 0, top)
    return jnp.take_along_axis(grid, (jnp.arange(top)[None, :] + turn) % top, axis=1)


def shares(count, total, limit, skew, full):
    portions = [(1 << 20) // math.isqrt(rank ** skew) + 1 for rank in range(1, count + 1)]
    largest = limit if full else min(limit, max(-(-total // count), total * portions[0] // sum(portions)))
    least = 1 if total - largest >= count - 1 else 0
    holding, rest = [largest] + [least] * (count - 1), total - largest - least * (count - 1)
    while rest > 0:
        movable = [i for i in range(1, count) if holding[i] < largest] or [i for i in range(1, count) if holding[i] < limit]
        mass, left = sum([portions[i] for i in movable]), rest
        for i in movable:
            extra = min(limit - holding[i], max(1, left * portions[i] // mass), rest)
            holding[i] = holding[i] + extra
            rest = rest - extra
    return np.array(holding)


def scatter_about(stream_key, shape, spread, bound, shards=(), kind=jnp.bfloat16):
    array = jax.random.normal(stream_key, shape, jnp.float32) * spread
    if len(shards) > 0:
        array = steps_of(stream_key, shape, shards, -0.22, 0.18) * array
    return jnp.clip(array, min=-bound, max=bound).astype(kind)


def setup_inputs(seed: int = 0) -> dict:
    streams_of = jax.random.split(jax.random.key(seed), 12)
    features = draw_features(jax.random.fold_in(streams_of[11], 71), 0)
    write_vectors = scatter_about(streams_of[1], (STATE, TOKEN_COUNT), STATE ** -0.5, 0.5, ((1, 16),))
    read_vectors = scatter_about(streams_of[2], (STATE, TOKEN_COUNT), 1.0, 6.0, ((1, 16),))
    log_decay = draw_log_decay(jax.random.fold_in(streams_of[11], 71), 0)
    doc_lengths = ragged(streams_of[4], DOCS, TOKEN_COUNT, TOKEN_COUNT // 4, 1).astype(jnp.int32)
    expert_ids_keys = jax.random.split(jax.random.fold_in(streams_of[5], 1), TOKEN_COUNT // TOK_DEV)
    expert_ids_turns = jax.random.permutation(jax.random.fold_in(streams_of[5], 3), TOKEN_COUNT // TOK_DEV)
    expert_ids = jax.vmap(lambda own, number: shared_out(jax.random.fold_in(streams_of[5], 2), own, number, TOK_DEV, EXPERTS, TOPK, CAP, 1))(expert_ids_keys, expert_ids_turns).reshape((TOKEN_COUNT, TOPK))
    route_weights = jnp.clip(jnp.exp(math.log(1.0) - 1.609438 * jax.random.uniform(streams_of[6], (TOKEN_COUNT, TOPK), jnp.float32) ** steps_of(streams_of[6], (TOKEN_COUNT, TOPK), ((0, 512),), -0.2, 0.2)), 0.2, 1.0)
    norm_gain = jnp.clip(1.0 + 0.18 * jax.random.normal(streams_of[7], (D,), jnp.float32), 0.1, 1.9)
    expert_in = scatter_about(streams_of[8], (EXPERTS, D, 2 * FF), D ** -0.5, 0.125, ((0, 32), (1, 16)))
    expert_out = scatter_about(streams_of[9], (EXPERTS, D, FF), FF ** -0.5, 0.21875, ((0, 32), (1, 16)))
    out_grad = scatter_about(streams_of[10], (D, TOKEN_COUNT), 1.0, 6.0, ((1, 512),))
    return {"features": features, "write_vectors": write_vectors, "read_vectors": read_vectors, "log_decay": log_decay, "doc_lengths": doc_lengths, "expert_ids": expert_ids, "route_weights": route_weights, "norm_gain": norm_gain, "expert_in": expert_in, "expert_out": expert_out, "out_grad": out_grad}


precise = lax.Precision.HIGHEST

def block_weights(decay_block, flag_block):
    cumulative = jnp.cumsum(decay_block, axis=1)
    starts_upto = jnp.cumsum(flag_block)
    position = jnp.arange(flag_block.shape[0], dtype=jnp.int32)
    lower_mask = position[:, None] >= position[None, :]
    same_doc = lower_mask & (starts_upto[:, None] == starts_upto[None, :])
    log_gap = cumulative[:, :, None] - cumulative[:, None, :]
    pair_weight = jnp.where(same_doc[None], jnp.exp(jnp.where(same_doc[None], log_gap, 0.0)), 0.0)
    entering = jnp.where(starts_upto[None, :] == 0, jnp.exp(cumulative), 0.0)
    leaving = jnp.where(starts_upto[None, :] == starts_upto[-1], jnp.exp(cumulative[:, -1:] - cumulative), 0.0)
    through_all = jnp.where(starts_upto[-1] == 0, jnp.exp(cumulative[:, -1]), 0.0)
    return (pair_weight, entering, leaving, through_all)

def doc_flags(doc_lengths, offset, span_count):
    doc_ends = jnp.cumsum(doc_lengths)
    starts = (doc_ends - doc_lengths).astype(jnp.int32)
    position = offset + jnp.arange(span_count, dtype=jnp.int32)
    return lax.optimization_barrier(jnp.sum((position[:, None] == starts[None, :]).astype(jnp.float32), axis=1))

def split_blocks(features, write_vectors, read_vectors, log_decay, flags, block_size):
    feature_count, token_count = features.shape
    head_count = log_decay.shape[0]
    num_blocks = token_count // block_size
    x_blocks = features.reshape(head_count, feature_count // head_count, num_blocks, block_size).transpose(2, 0, 1, 3)
    write_blocks = write_vectors.reshape(-1, num_blocks, block_size).transpose(1, 0, 2)
    read_blocks = read_vectors.reshape(-1, num_blocks, block_size).transpose(1, 0, 2)
    decay_blocks = log_decay.reshape(head_count, num_blocks, block_size).transpose(1, 0, 2)
    flag_blocks = flags.reshape(num_blocks, block_size)
    return (x_blocks, write_blocks, read_blocks, decay_blocks, flag_blocks)

def ssd_forward(features, write_vectors, read_vectors, log_decay, flags, block_size):
    feature_count, token_count = features.shape
    head_count = log_decay.shape[0]
    head_size = feature_count // head_count
    parts = split_blocks(features, write_vectors, read_vectors, log_decay, flags, block_size)

    def forward_step(state_now, inputs):
        x_block, write_block, read_block, decay_block, flag_block = inputs
        pair_weight, entering, leaving, through_all = block_weights(decay_block, flag_block)
        x_float = x_block.astype(jnp.float32)
        write_float = write_block.astype(jnp.float32)
        read_float = read_block.astype(jnp.float32)
        scores = jnp.dot(read_block.T, write_block, preferred_element_type=jnp.float32)
        inside = jnp.einsum('hts,hps->hpt', pair_weight * scores[None], x_float, precision=precise)
        carried = jnp.einsum('nt,hnp->hpt', read_float, state_now, precision=precise) * entering[:, None, :]
        state_next = through_all[:, None, None] * state_now + jnp.einsum('ns,hs,hps->hnp', write_float, leaving, x_float, precision=precise)
        return (state_next, inside + carried)
    initial = jnp.zeros((head_count, write_vectors.shape[0], head_size), jnp.float32)
    final_state, outputs = lax.scan(forward_step, initial, parts)
    return outputs.transpose(1, 2, 0, 3).reshape(feature_count, token_count)

def ssd_backward(y_grad, write_vectors, read_vectors, log_decay, flags, block_size):
    feature_count, token_count = y_grad.shape
    head_count = log_decay.shape[0]
    head_size = feature_count // head_count
    parts = split_blocks(y_grad, write_vectors, read_vectors, log_decay, flags, block_size)

    def backward_step(adjoint_now, inputs):
        grad_block, write_block, read_block, decay_block, flag_block = inputs
        pair_weight, entering, leaving, through_all = block_weights(decay_block, flag_block)
        grad_float = grad_block.astype(jnp.float32)
        write_float = write_block.astype(jnp.float32)
        read_float = read_block.astype(jnp.float32)
        scores = jnp.dot(read_block.T, write_block, preferred_element_type=jnp.float32)
        inside = jnp.einsum('hts,hpt->hps', pair_weight * scores[None], grad_float, precision=precise)
        carried = jnp.einsum('ns,hnp->hps', write_float, adjoint_now, precision=precise) * leaving[:, None, :]
        adjoint_next = through_all[:, None, None] * adjoint_now + jnp.einsum('nt,ht,hpt->hnp', read_float, entering, grad_float, precision=precise)
        return (adjoint_next, inside + carried)
    initial = jnp.zeros((head_count, write_vectors.shape[0], head_size), jnp.float32)
    final_adjoint, outputs = lax.scan(backward_step, initial, parts, reverse=True)
    return outputs.transpose(1, 2, 0, 3).reshape(feature_count, token_count)

def reference(features, write_vectors, read_vectors, log_decay, doc_lengths, expert_ids, route_weights, norm_gain, expert_in, expert_out, out_grad):
    flags = doc_flags(doc_lengths, jnp.int32(0), TOKEN_COUNT)
    y_value = ssd_forward(features, write_vectors, read_vectors, log_decay, flags, 256).astype(jnp.bfloat16)
    y_float = y_value.astype(jnp.float32)
    rscale = lax.rsqrt(lax.optimization_barrier(jnp.mean(y_float * y_float, axis=0)) + 1e-06)
    normed = (y_float * rscale[None, :] * norm_gain[:, None]).astype(jnp.bfloat16)
    num_blocks = TOKEN_COUNT // TOK_DEV
    per_block = TOK_DEV * TOPK
    block_ids = expert_ids.reshape(num_blocks, per_block)
    picked = (block_ids[:, :, None] == jnp.arange(EXPERTS, dtype=jnp.int32)[None, None, :]).astype(jnp.int32)
    earlier = jnp.cumsum(picked, axis=1) - picked
    slot_rank = lax.optimization_barrier(jnp.sum(earlier * picked, axis=2)).astype(jnp.int32)
    token_index = jnp.repeat(jnp.arange(TOKEN_COUNT, dtype=jnp.int32), TOPK).reshape(num_blocks, per_block)
    block_index = jnp.broadcast_to(jnp.arange(num_blocks, dtype=jnp.int32)[:, None], (num_blocks, per_block))
    slot_table = jnp.full((EXPERTS, num_blocks, CAP), TOKEN_COUNT, jnp.int32).at[block_ids, block_index, slot_rank].set(token_index)
    weight_table = jnp.zeros((EXPERTS, num_blocks, CAP), jnp.float32).at[block_ids, block_index, slot_rank].set(route_weights.reshape(num_blocks, per_block))
    normed_rows = jnp.concatenate([normed.T, jnp.zeros((1, D), jnp.bfloat16)], axis=0)
    grad_rows = jnp.concatenate([out_grad.T, jnp.zeros((1, D), jnp.bfloat16)], axis=0)
    contract_last = (((1,), (1,)), ((), ()))

    def expert_step(carry, inputs):
        moe_sum, back_sum = carry
        weight_in, weight_out, rows_index, rows_weight = inputs
        row_index = rows_index.reshape(-1)
        row_weight = rows_weight.reshape(-1)
        taken_rows = normed_rows[row_index]
        projected = jnp.dot(taken_rows, weight_in, preferred_element_type=jnp.float32)
        gate_part = projected[:, :FF]
        up_part = projected[:, FF:]
        hidden = (jax.nn.silu(gate_part) * up_part).astype(jnp.bfloat16)
        expert_y = lax.dot_general(hidden, weight_out, contract_last, preferred_element_type=jnp.float32).astype(jnp.bfloat16)
        moe_sum = moe_sum.at[row_index].add(row_weight[:, None] * expert_y.astype(jnp.float32))
        back_in = (row_weight[:, None] * grad_rows[row_index].astype(jnp.float32)).astype(jnp.bfloat16)
        d_hidden = jnp.dot(back_in, weight_out, preferred_element_type=jnp.float32)
        sigmoid_gate = jax.nn.sigmoid(gate_part)
        d_gate = (d_hidden * up_part * sigmoid_gate * (1.0 + gate_part * (1.0 - sigmoid_gate))).astype(jnp.bfloat16)
        d_up = (d_hidden * gate_part * sigmoid_gate).astype(jnp.bfloat16)
        back_out = lax.dot_general(jnp.concatenate([d_gate, d_up], axis=1), weight_in, contract_last, preferred_element_type=jnp.float32).astype(jnp.bfloat16)
        back_sum = back_sum.at[row_index].add(back_out.astype(jnp.float32))
        return ((moe_sum, back_sum), None)
    start_sums = (jnp.zeros((TOKEN_COUNT + 1, D), jnp.float32), jnp.zeros((TOKEN_COUNT + 1, D), jnp.float32))
    (moe_sum, back_sum), nothing_out = lax.scan(expert_step, start_sums, (expert_in, expert_out, slot_table, weight_table))
    block_out = (normed.astype(jnp.float32) + moe_sum[:TOKEN_COUNT].T).astype(jnp.bfloat16)
    d_normed = out_grad.astype(jnp.float32) + back_sum[:TOKEN_COUNT].T
    scaled_grad = norm_gain[:, None] * d_normed
    mean_term = lax.optimization_barrier(jnp.mean(y_float * scaled_grad, axis=0))
    y_grad = (rscale[None, :] * scaled_grad - y_float * (rscale ** 3)[None, :] * mean_term[None, :]).astype(jnp.bfloat16)
    input_grad = ssd_backward(y_grad, write_vectors, read_vectors, log_decay, flags, 256).astype(jnp.bfloat16)
    return (block_out, input_grad)
```

```python
import jax
import jax.numpy as jnp
from jax import lax
from jax.experimental import pallas as pl
from jax.experimental.pallas import tpu as pltpu
from jax.sharding import PartitionSpec as P

f32 = jnp.float32
bf16 = jnp.bfloat16
i32 = jnp.int32

LANES = 128
SEQ = 4096
CHUNKS = SEQ // LANES
PAIRS = CHUNKS // 2
HP = 64
HEAD = 32
EXPERTS = 32
CAP = 10
SLOTS = EXPERTS * CAP
BLOCK = CAP * PAIRS
ROWS = EXPERTS * BLOCK
WIDTH = 2048
FF = 768
FBLOCKS = WIDTH // LANES
REACH = 4
VMEM_SMALL = 32 * 1024 * 1024
VMEM_LARGE = 48 * 1024 * 1024

LAST = (((1,), (1,)), ((), ()))
FIRST = (((0,), (0,)), ((), ()))


def dot(a, b):
    return jnp.dot(a, b, preferred_element_type=f32)


def dot_last(a, b):
    return lax.dot_general(a, b, LAST, preferred_element_type=f32)


def dot_first(a, b):
    return lax.dot_general(a, b, FIRST, preferred_element_type=f32)


def split3(value):
    high = value.astype(bf16)
    rest = value - high.astype(f32)
    middle = rest.astype(bf16)
    low = (rest - middle.astype(f32)).astype(bf16)
    return high, middle, low


def rows_of(first, second):
    return jnp.concatenate(
        [jnp.broadcast_to(first, (HEAD, LANES)), jnp.broadcast_to(second, (HEAD, LANES))], axis=0
    )


def earlier_mask():
    row = lax.broadcasted_iota(i32, (LANES, LANES), 0)
    col = lax.broadcasted_iota(i32, (LANES, LANES), 1)
    return jnp.where(row < col, 1.0, 0.0).astype(bf16)


def rank_table(first_ids, second_ids, earlier):
    expert = lax.broadcasted_iota(i32, (EXPERTS, LANES), 0).astype(f32)
    picked = (expert == first_ids) | (expert == second_ids)
    rank = dot(jnp.where(picked, 1.0, 0.0).astype(bf16), earlier)
    return jnp.where(picked, rank, -1.0)


def slot_onehot(ranks):
    return jnp.concatenate(
        [jnp.where(ranks == float(c), 1.0, 0.0).astype(bf16) for c in range(CAP)], axis=0
    )


def round_rows(dst_ref, src_ref):
    def step(i, carry):
        at = pl.ds(pl.multiple_of(i * BLOCK, BLOCK), BLOCK)
        dst_ref[at, :] = src_ref[at, :].astype(dst_ref.dtype)
        return carry

    lax.fori_loop(0, ROWS // BLOCK, step, 0)


def call(kernel, outs, args, in_specs, scratch=(), vmem=VMEM_SMALL, flops=0, moved=0, name=None):
    vm = pl.BlockSpec(memory_space=pltpu.VMEM)
    return pl.pallas_call(
        kernel,
        out_shape=tuple(jax.ShapeDtypeStruct(shape, kind) for shape, kind in outs),
        in_specs=in_specs,
        out_specs=tuple(vm for _ in outs),
        scratch_shapes=list(scratch),
        compiler_params=pltpu.CompilerParams(vmem_limit_bytes=vmem),
        cost_estimate=pl.CostEstimate(flops=flops, bytes_accessed=moved, transcendentals=0),
        name=name,
    )(*args)


VM = pl.BlockSpec(memory_space=pltpu.VMEM)
SM = pl.BlockSpec(memory_space=pltpu.SMEM)
HBM = pl.BlockSpec(memory_space=pl.ANY)


def grad_rows_kernel(ids_ref, grad_ref, out_ref, wide_ref):
    ranks = rank_table(ids_ref[0:1, :], ids_ref[1:2, :], earlier_mask())
    select = slot_onehot(ranks)

    def step(fb, carry):
        at = pl.multiple_of(fb * LANES, LANES)
        rows = dot_last(select, grad_ref[pl.ds(at, LANES), :])
        for c in range(CAP):
            wide_ref[pl.ds(c * FBLOCKS + fb, EXPERTS, stride=BLOCK), :] = rows[
                c * EXPERTS : (c + 1) * EXPERTS
            ]
        return carry

    lax.fori_loop(0, FBLOCKS, step, 0)
    round_rows(out_ref, wide_ref)


def tables_kernel(docs_ref, base_ref, decay_ref, x_ref, write_ref, rt_ref, dt_ref, msg_ref):
    decay = decay_ref[...]
    row_i = lax.broadcasted_iota(i32, (LANES, LANES), 0)
    col_i = lax.broadcasted_iota(i32, (LANES, LANES), 1)
    upto = jnp.where(row_i <= col_i, 1.0, 0.0).astype(bf16)
    cum = sum(dot(part, upto) for part in split3(decay))
    rows = 2 * CHUNKS
    chunk_end = jnp.broadcast_to(cum[:, LANES - 1 : LANES], (rows, LANES))
    row_j = lax.broadcasted_iota(i32, (rows, rows), 0)
    col_j = lax.broadcasted_iota(i32, (rows, rows), 1)
    same_head = (row_j >= CHUNKS) == (col_j >= CHUNKS)
    before = jnp.where(same_head & (col_j < row_j), 1.0, 0.0).astype(bf16)
    after = jnp.where(same_head & (col_j > row_j), 1.0, 0.0).astype(bf16)
    parts = split3(chunk_end)
    prefix = sum(dot(before, part) for part in parts)
    suffix = sum(dot(after, part) for part in parts)
    chunk = lax.broadcasted_iota(i32, (rows, LANES), 0)
    chunk = jnp.where(chunk >= CHUNKS, chunk - CHUNKS, chunk)
    token = lax.broadcasted_iota(i32, (rows, LANES), 1)
    place = chunk * LANES + token
    base = base_ref[0]
    doc_start = jnp.full((rows, LANES), -(1 << 20), i32)
    last_start = jnp.int32(-(1 << 20))
    start = -base
    for j in range(docs_ref.shape[0]):
        doc_start = jnp.where(place >= start, jnp.maximum(doc_start, start), doc_start)
        last_start = jnp.where(start <= SEQ - 1, jnp.maximum(last_start, start), last_start)
        start = start + docs_ref[j]
    inner_start = jnp.maximum(doc_start - chunk * LANES, -1)
    inner_float = inner_start.astype(f32)
    inner_last = jnp.broadcast_to(inner_float[:, LANES - 1 : LANES], (rows, LANES))
    to_end = chunk_end - cum
    entering = jnp.where(inner_start < 0, jnp.exp(cum), 0.0)
    leaving = jnp.where(token.astype(f32) >= inner_last, jnp.exp(to_end), 0.0)
    dev_entering = jnp.where(doc_start < 0, jnp.exp(prefix + cum), 0.0)
    dev_leaving = jnp.where(place >= last_start, jnp.exp(to_end + suffix), 0.0)
    for r, value in enumerate(
        (
            cum[:CHUNKS],
            cum[CHUNKS:],
            entering[:CHUNKS],
            entering[CHUNKS:],
            leaving[:CHUNKS],
            leaving[CHUNKS:],
            inner_float[:CHUNKS],
            inner_float[CHUNKS:],
        )
    ):
        rt_ref[pl.ds(r, CHUNKS, stride=8), :] = value
    zero = jnp.zeros((CHUNKS, LANES), f32)
    for r, value in enumerate(
        (
            dev_entering[:CHUNKS],
            dev_entering[CHUNKS:],
            dev_leaving[:CHUNKS],
            dev_leaving[CHUNKS:],
            zero,
            zero,
            zero,
            zero,
        )
    ):
        dt_ref[pl.ds(r, CHUNKS, stride=8), :] = value

    def step(k, acc):
        lanes = pl.ds(pl.multiple_of(k * LANES, LANES), LANES)
        rows_k = dt_ref[pl.ds(pl.multiple_of(k * 8, 8), 8), :]
        scaled = x_ref[:, lanes].astype(f32) * rows_of(rows_k[2:3], rows_k[3:4])
        return acc + dot_last(scaled.astype(bf16), write_ref[:, lanes])

    acc = lax.fori_loop(0, CHUNKS, step, jnp.zeros((HP, LANES), f32), unroll=4)
    msg_ref[0:HP, :] = acc
    through = jnp.concatenate(
        [
            jnp.broadcast_to(dev_entering[CHUNKS - 1 : CHUNKS, LANES - 1 : LANES], (1, LANES)),
            jnp.broadcast_to(dev_entering[rows - 1 : rows, LANES - 1 : LANES], (1, LANES)),
            jnp.zeros((6, LANES), f32),
        ],
        axis=0,
    )
    msg_ref[HP : HP + 8, :] = through


def chained(refs):
    state = refs[-1][0:HP, :]
    for ref in refs[-2::-1]:
        state = ref[0:HP, :] + rows_of(ref[HP : HP + 1, :], ref[HP + 1 : HP + 2, :]) * state
    return state


def forward_kernel(
    expert_ref,
    m1_ref,
    m2_ref,
    m3_ref,
    m4_ref,
    rt_ref,
    x_ref,
    write_ref,
    read_ref,
    ids_ref,
    y_ref,
    pair_ref,
    msg_ref,
    rank_ref,
    weight_ref,
    first_ref,
    wide_ref,
):
    earlier = earlier_mask()
    mine = expert_ref[0].astype(f32)
    is_first = ids_ref[0] == mine
    is_second = ids_ref[1] == mine
    picked = is_first | is_second
    rank = dot(jnp.where(picked, 1.0, 0.0).astype(bf16), earlier)
    rank = jnp.where(picked, rank, -1.0)
    route = jnp.where(is_first, ids_ref[2], jnp.where(is_second, ids_ref[3], 0.0))
    first = jnp.where(is_first, 1.0, 0.0)
    for c in range(CAP):
        here = rank == float(c)
        route_c = jnp.sum(jnp.where(here, route, 0.0), axis=1, keepdims=True)
        first_c = jnp.sum(jnp.where(here, first, 0.0), axis=1, keepdims=True)
        for par in range(2):
            at = (par * CAP + c) * PAIRS
            part = slice(par * PAIRS, (par + 1) * PAIRS)
            weight_ref[at : at + PAIRS, :] = jnp.broadcast_to(route_c[part], (PAIRS, LANES))
            first_ref[at : at + PAIRS, :] = jnp.broadcast_to(first_c[part], (PAIRS, LANES))

    row_i = lax.broadcasted_iota(i32, (LANES, LANES), 0)
    col_i = lax.broadcasted_iota(i32, (LANES, LANES), 1)
    causal = row_i <= col_i
    row_f = row_i.astype(f32)

    def step(k, state):
        lanes = pl.ds(pl.multiple_of(k * LANES, LANES), LANES)
        rows = rt_ref[pl.ds(pl.multiple_of(k * 8, 8), 8), :]
        cols = rows.T
        x = x_ref[:, lanes]
        write = write_ref[:, lanes]
        read = read_ref[:, lanes]
        scores = dot_first(write, read)
        valid = causal & (row_f >= rows[6:7, :])
        inside = []
        for h in range(2):
            gap = rows[h : h + 1, :] - cols[:, h : h + 1]
            pair = jnp.where(valid, jnp.exp(gap) * scores, 0.0).astype(bf16)
            pair_ref[pl.ds(pl.multiple_of((2 * k + h) * LANES, LANES), LANES), :] = pair
            inside.append(dot(x[h * HEAD : (h + 1) * HEAD, :], pair))
        carried = dot(state.astype(bf16), read) * rows_of(rows[2:3], rows[3:4])
        y_ref[:, lanes] = (jnp.concatenate(inside, axis=0) + carried).astype(bf16)
        scaled = (x.astype(f32) * rows_of(rows[4:5], rows[5:6])).astype(bf16)
        through = rows_of(
            jnp.broadcast_to(rows[2:3, LANES - 1 : LANES], (1, LANES)),
            jnp.broadcast_to(rows[3:4, LANES - 1 : LANES], (1, LANES)),
        )
        return through * state + dot_last(scaled, write)

    lax.fori_loop(0, CHUNKS, step, chained((m1_ref, m2_ref, m3_ref, m4_ref)), unroll=4)

    zero = jnp.zeros((HP, LANES), bf16)

    def dispatch(jp, carry):
        tables = []
        for par in range(2):
            j = par * PAIRS + jp
            table = rank_table(
                ids_ref[0, pl.ds(j, 1), :], ids_ref[1, pl.ds(j, 1), :], earlier
            )
            at = pl.multiple_of(jp * 64 + par * EXPERTS, EXPERTS)
            rank_ref[pl.ds(at, EXPERTS), :] = table
            tables.append(table)
        select = slot_onehot(jnp.concatenate(tables, axis=1))
        even = y_ref[:, pl.ds(pl.multiple_of(jp * 2 * LANES, LANES), LANES)]
        odd = y_ref[:, pl.ds(pl.multiple_of(jp * 2 * LANES + LANES, LANES), LANES)]
        both = jnp.concatenate(
            [jnp.concatenate([even, zero], axis=1), jnp.concatenate([zero, odd], axis=1)], axis=0
        )
        rows = dot_last(select, both)
        for c in range(CAP):
            wide_ref[pl.ds(c * PAIRS + jp, EXPERTS, stride=BLOCK), :] = rows[
                c * EXPERTS : (c + 1) * EXPERTS
            ]
        return carry

    lax.fori_loop(0, PAIRS, dispatch, 0)
    round_rows(msg_ref, wide_ref)


def arrived_grad_kernel(
    rows_ref, weight_ref, out_hbm, grad_ref, dhid_ref, wide_ref, scaled_ref, out_ref, sem
):
    fetch = pltpu.make_async_copy(out_hbm, out_ref, sem)
    fetch.start()
    round_rows(wide_ref, rows_ref)

    def unpack(fb, carry):
        lanes = pl.ds(pl.multiple_of(fb * LANES, LANES), LANES)
        for par in range(2):
            for c in range(CAP):
                at = (par * CAP + c) * PAIRS
                rows = wide_ref[
                    pl.ds(par * BLOCK + c * FBLOCKS + fb, PAIRS, stride=2 * BLOCK), :
                ]
                grad_ref[at : at + PAIRS, lanes] = rows.astype(bf16)
                scaled_ref[at : at + PAIRS, lanes] = (
                    rows * weight_ref[at : at + PAIRS, :]
                ).astype(bf16)
        return carry

    lax.fori_loop(0, FBLOCKS, unpack, 0)
    fetch.wait()

    def matmul(i, carry):
        lanes = pl.ds(pl.multiple_of(i * 256, 256), 256)
        dhid_ref[:, lanes] = dot(scaled_ref[...], out_ref[:, lanes])
        return carry

    lax.fori_loop(0, FF // 256, matmul, 0)


def expert_kernel(
    rows_ref,
    gain_ref,
    first_ref,
    grad_ref,
    dhid_ref,
    in_hbm,
    msg_ref,
    normed_ref,
    hidden_ref,
    stats_ref,
    y_ref,
    dcat_ref,
    in_ref,
    sem,
):
    fetch = pltpu.make_async_copy(in_hbm, in_ref, sem)
    fetch.start()
    lane = lax.broadcasted_iota(i32, (BLOCK, LANES), 1)
    low = lane < 64

    def unpack(k, squares):
        lanes = pl.ds(pl.multiple_of(k * LANES, LANES), LANES)
        at = pl.multiple_of(k * 2 * BLOCK, BLOCK)
        a = rows_ref[pl.ds(at, BLOCK), :].astype(f32)
        b = rows_ref[pl.ds(at + BLOCK, BLOCK), :].astype(f32)
        even = jnp.where(low, a, pltpu.roll(b, 64, 1))
        odd = jnp.where(low, pltpu.roll(a, 64, 1), b)
        both = jnp.concatenate([even, odd], axis=0)
        y_ref[:, lanes] = both
        return squares + both * both

    squares = lax.fori_loop(0, FBLOCKS, unpack, jnp.zeros((SLOTS, LANES), f32))
    mean = jnp.sum(squares, axis=1, keepdims=True) * (1.0 / WIDTH)
    rscale = lax.rsqrt(mean + 1e-06)
    rscale_b = jnp.broadcast_to(rscale, (SLOTS, LANES))

    def scale(k, carry):
        lanes = pl.ds(pl.multiple_of(k * LANES, LANES), LANES)
        scaled = y_ref[:, lanes] * gain_ref[:, lanes]
        y_ref[:, lanes] = scaled
        normed_ref[:, lanes] = (scaled * rscale_b).astype(bf16)
        return carry

    lax.fori_loop(0, FBLOCKS, scale, 0)
    fetch.wait()

    def project(i, carry):
        lanes = pl.ds(pl.multiple_of(i * 256, 256), 256)
        lanes_up = pl.ds(pl.multiple_of(FF + i * 256, 256), 256)
        gate = dot(normed_ref[...], in_ref[:, lanes])
        up = dot(normed_ref[...], in_ref[:, lanes_up])
        sigmoid = 1.0 / (1.0 + jnp.exp(-gate))
        swish = gate * sigmoid
        hidden_ref[:, lanes] = (swish * up).astype(bf16)
        dhid = dhid_ref[:, lanes]
        dcat_ref[:, lanes] = (dhid * up * sigmoid * (1.0 + gate * (1.0 - sigmoid))).astype(bf16)
        dcat_ref[:, lanes_up] = (dhid * swish).astype(bf16)
        return carry

    lax.fori_loop(0, FF // 256, project, 0)
    first = first_ref[...]
    first2 = jnp.concatenate([first, first], axis=1)

    def back(i, acc):
        at = pl.multiple_of(i * 256, 256)
        lanes = pl.ds(at, 256)
        grad = dot_last(dcat_ref[...], in_ref[lanes, :]) + first2 * grad_ref[:, lanes].astype(f32)
        product = grad * y_ref[:, lanes]
        for half in range(2):
            part = grad[:, half * LANES : (half + 1) * LANES]
            even, odd = part[:BLOCK], part[BLOCK:]
            row = pl.multiple_of((2 * i + half) * 2 * BLOCK, BLOCK)
            msg_ref[pl.ds(row, BLOCK), :] = jnp.where(low, even, pltpu.roll(odd, 64, 1)).astype(
                bf16
            )
            msg_ref[pl.ds(row + BLOCK, BLOCK), :] = jnp.where(
                low, pltpu.roll(even, 64, 1), odd
            ).astype(bf16)
        return acc + product[:, :LANES] + product[:, LANES:]

    acc = lax.fori_loop(0, WIDTH // 256, back, jnp.zeros((SLOTS, LANES), f32))
    total = jnp.broadcast_to(jnp.sum(acc, axis=1, keepdims=True), (SLOTS, LANES))
    stat_lane = lax.broadcasted_iota(i32, (SLOTS, LANES), 1)
    stats_ref[...] = jnp.where(stat_lane == 0, rscale_b, total)


def expert_out_kernel(
    hidden_ref, normed_ref, weight_ref, first_ref, out_hbm, msg_ref, wide_ref, out_ref, sem
):
    fetch = pltpu.make_async_copy(out_hbm, out_ref, sem)
    fetch.start()
    weight = weight_ref[...]
    weight2 = jnp.concatenate([weight, weight], axis=1)
    first = first_ref[...]
    first2 = jnp.concatenate([first, first], axis=1)
    fetch.wait()

    def matmul(i, carry):
        lanes = pl.ds(pl.multiple_of(i * 256, 256), 256)
        result = dot_last(hidden_ref[...], out_ref[lanes, :])
        result = weight2 * result + first2 * normed_ref[:, lanes].astype(f32)
        for half in range(2):
            part = result[:, half * LANES : (half + 1) * LANES]
            fb = 2 * i + half
            for par in range(2):
                for c in range(CAP):
                    at = (par * CAP + c) * PAIRS
                    wide_ref[
                        pl.ds(par * BLOCK + c * FBLOCKS + fb, PAIRS, stride=2 * BLOCK), :
                    ] = part[at : at + PAIRS]
        return carry

    lax.fori_loop(0, WIDTH // 256, matmul, 0)
    round_rows(msg_ref, wide_ref)


def combine_kernel(ids_ref, rows_ref, out_ref, wide_ref):
    round_rows(wide_ref, rows_ref)
    select = slot_onehot(rank_table(ids_ref[0:1, :], ids_ref[1:2, :], earlier_mask()))

    def step(fb, carry):
        rows = jnp.concatenate(
            [
                wide_ref[pl.ds(c * FBLOCKS + fb, EXPERTS, stride=BLOCK), :].astype(bf16)
                for c in range(CAP)
            ],
            axis=0,
        )
        at = pl.multiple_of(fb * LANES, LANES)
        out_ref[pl.ds(at, LANES), :] = dot_first(rows, select).astype(bf16)
        return carry

    lax.fori_loop(0, FBLOCKS, step, 0)


def grad_kernel(
    rows_ref, rank_ref, stats_ref, y_ref, gain_ref, read_ref, dt_ref, out_ref, msg_ref, wide_ref
):
    round_rows(wide_ref, rows_ref)
    gain = gain_ref[...]

    def step(jp, acc):
        at = pl.multiple_of(jp * 64, 64)
        ranks = rank_ref[pl.ds(at, 64), :]
        select = slot_onehot(jnp.concatenate([ranks[:EXPERTS], ranks[EXPERTS:]], axis=1))
        rows = jnp.concatenate(
            [
                wide_ref[pl.ds(c * PAIRS + jp, EXPERTS, stride=BLOCK), :].astype(bf16)
                for c in range(CAP)
            ],
            axis=0,
        )
        d_both = dot_first(rows, select)
        stats = stats_ref[jp]
        stats_high = stats.astype(bf16)
        stats_low = (stats - stats_high.astype(f32)).astype(bf16)
        per_token = dot(stats_high, select) + dot(stats_low, select)
        for par in range(2):
            lanes = pl.ds(pl.multiple_of((2 * jp + par) * LANES, LANES), LANES)
            part = slice(par * LANES, (par + 1) * LANES)
            rscale = 0.5 * per_token[2 * par : 2 * par + 1, part]
            mean = per_token[2 * par + 1 : 2 * par + 2, part] * (1.0 / WIDTH)
            scaled = gain * d_both[par * HP : (par + 1) * HP, part]
            y = y_ref[:, lanes].astype(f32)
            grad = (rscale * scaled - y * (rscale * rscale * rscale * mean)).astype(bf16)
            out_ref[:, lanes] = grad
            rows_k = dt_ref[pl.ds(pl.multiple_of((2 * jp + par) * 8, 8), 8), :]
            weighted = (grad.astype(f32) * rows_of(rows_k[0:1], rows_k[1:2])).astype(bf16)
            acc = acc + dot_last(weighted, read_ref[:, lanes])
        return acc

    msg_ref[0:HP, :] = lax.fori_loop(0, PAIRS, step, jnp.zeros((HP, LANES), f32))
    last = dt_ref[(CHUNKS - 1) * 8 : CHUNKS * 8, :]
    msg_ref[HP : HP + 8, :] = jnp.broadcast_to(last[:, LANES - 1 : LANES], (8, LANES))


def backward_kernel(
    m1_ref, m2_ref, m3_ref, m4_ref, rt_ref, grad_ref, write_ref, read_ref, pair_ref, out_ref
):
    def step(i, state):
        k = CHUNKS - 1 - i
        lanes = pl.ds(pl.multiple_of(k * LANES, LANES), LANES)
        rows = rt_ref[pl.ds(pl.multiple_of(k * 8, 8), 8), :]
        grad = grad_ref[:, lanes]
        write = write_ref[:, lanes]
        read = read_ref[:, lanes]
        inside = []
        for h in range(2):
            pair = pair_ref[pl.ds(pl.multiple_of((2 * k + h) * LANES, LANES), LANES), :]
            inside.append(dot_last(grad[h * HEAD : (h + 1) * HEAD, :], pair))
        carried = dot(state.astype(bf16), write) * rows_of(rows[4:5], rows[5:6])
        out_ref[:, lanes] = (jnp.concatenate(inside, axis=0) + carried).astype(bf16)
        scaled = (grad.astype(f32) * rows_of(rows[2:3], rows[3:4])).astype(bf16)
        through = rows_of(
            jnp.broadcast_to(rows[2:3, LANES - 1 : LANES], (1, LANES)),
            jnp.broadcast_to(rows[3:4, LANES - 1 : LANES], (1, LANES)),
        )
        return through * state + dot_last(scaled, read)

    lax.fori_loop(0, CHUNKS, step, chained((m1_ref, m2_ref, m3_ref, m4_ref)), unroll=4)


def sent_along(value, by):
    size = lax.axis_size("ctx")
    pairs = [(i, i + by) for i in range(size) if 0 <= i + by < size]
    return lax.ppermute(value, "ctx", pairs)


def exchanged(rows):
    blocks = rows.reshape(EXPERTS, BLOCK, LANES)
    return lax.all_to_all(blocks, "exp", split_axis=0, concat_axis=0, tiled=True).reshape(
        ROWS, LANES
    )


def per_device(
    features,
    write_vectors,
    read_vectors,
    log_decay,
    doc_lengths,
    expert_ids,
    route_weights,
    norm_gain,
    expert_in,
    expert_out,
    out_grad,
):
    me_ctx = lax.axis_index("ctx")
    me_exp = lax.axis_index("exp")
    wide = pltpu.VMEM((ROWS, LANES), f32)
    ids_own = expert_ids.T.astype(f32)
    tokens_own = jnp.concatenate([ids_own, route_weights.T], axis=0)

    (grad_out_rows,) = call(
        grad_rows_kernel,
        [((ROWS, LANES), bf16)],
        (ids_own, out_grad),
        [VM, VM],
        [wide],
        flops=2 * SLOTS * LANES * WIDTH,
        moved=4 << 20,
        name="grad_rows",
    )
    grad_in_rows = exchanged(grad_out_rows)

    weight_in = lax.all_gather(expert_in, "ctx", axis=1, tiled=True)[0]
    weight_out = lax.all_gather(expert_out, "ctx", axis=1, tiled=True)[0]
    tokens = lax.all_gather(tokens_own, "exp", axis=0, tiled=False)
    tokens = tokens.reshape(PAIRS, 2, 4, LANES).transpose(2, 1, 0, 3).reshape(4, CHUNKS, LANES)

    rt, dt, message = call(
        tables_kernel,
        [((CHUNKS * 8, LANES), f32), ((CHUNKS * 8, LANES), f32), ((HP + 8, LANES), f32)],
        (
            doc_lengths,
            (me_ctx * SEQ).astype(i32).reshape(1),
            log_decay.reshape(2 * CHUNKS, LANES),
            features,
            write_vectors,
        ),
        [SM, SM, VM, VM, VM],
        flops=2 * HP * LANES * SEQ,
        moved=3 << 20,
        name="shard_state",
    )
    before = [sent_along(message, d) for d in range(1, REACH + 1)]
    y_heads, pairs, y_out_rows, ranks, slot_weight, slot_first = call(
        forward_kernel,
        [
            ((HP, SEQ), bf16),
            ((2 * CHUNKS * LANES, LANES), bf16),
            ((ROWS, LANES), bf16),
            ((2 * CHUNKS // 2 * EXPERTS, LANES), f32),
            ((SLOTS, LANES), f32),
            ((SLOTS, LANES), f32),
        ],
        (
            me_exp.astype(i32).reshape(1),
            *before,
            rt,
            features,
            write_vectors,
            read_vectors,
            tokens,
        ),
        [SM] + [VM] * 9,
        [wide],
        flops=8 * HP * LANES * SEQ,
        moved=9 << 20,
        name="mixer_forward",
    )
    y_in_rows = exchanged(y_out_rows)

    grad_slots, d_hidden = call(
        arrived_grad_kernel,
        [((SLOTS, WIDTH), bf16), ((SLOTS, FF), f32)],
        (grad_in_rows, slot_weight, weight_out),
        [VM, VM, HBM],
        [wide, pltpu.VMEM((SLOTS, WIDTH), bf16), pltpu.VMEM((WIDTH, FF), bf16), pltpu.SemaphoreType.DMA],
        vmem=VMEM_LARGE,
        flops=2 * SLOTS * FF * WIDTH,
        moved=8 << 20,
        name="hidden_grad",
    )
    back_out_rows, normed, hidden, stats = call(
        expert_kernel,
        [
            ((ROWS, LANES), bf16),
            ((SLOTS, WIDTH), bf16),
            ((SLOTS, FF), bf16),
            ((SLOTS, LANES), f32),
        ],
        (y_in_rows, norm_gain.reshape(1, WIDTH), slot_first, grad_slots, d_hidden, weight_in),
        [VM, VM, VM, VM, VM, HBM],
        [
            pltpu.VMEM((SLOTS, WIDTH), f32),
            pltpu.VMEM((SLOTS, 2 * FF), bf16),
            pltpu.VMEM((WIDTH, 2 * FF), bf16),
            pltpu.SemaphoreType.DMA,
        ],
        vmem=VMEM_LARGE,
        flops=8 * SLOTS * FF * WIDTH,
        moved=14 << 20,
        name="expert",
    )
    back_in_rows = exchanged(back_out_rows)
    all_stats = lax.all_gather(stats[:, :2].T, "exp", axis=0, tiled=False)
    all_stats = all_stats.reshape(EXPERTS, 2, 2, CAP, PAIRS).transpose(4, 2, 1, 3, 0)
    all_stats = jnp.pad(all_stats.reshape(PAIRS, 4, SLOTS), ((0, 0), (0, 4), (0, 0)))

    (result_rows,) = call(
        expert_out_kernel,
        [((ROWS, LANES), bf16)],
        (hidden, normed, slot_weight, slot_first, weight_out),
        [VM, VM, VM, VM, HBM],
        [wide, pltpu.VMEM((WIDTH, FF), bf16), pltpu.SemaphoreType.DMA],
        vmem=VMEM_LARGE,
        flops=2 * SLOTS * FF * WIDTH,
        moved=8 << 20,
        name="expert_out",
    )
    result_rows, back_in_rows = lax.optimization_barrier((result_rows, back_in_rows))
    returned_rows = exchanged(result_rows)

    gain_own = lax.dynamic_slice(norm_gain, (me_exp * HP,), (HP,))
    y_grad, back_message = call(
        grad_kernel,
        [((HP, SEQ), bf16), ((HP + 8, LANES), f32)],
        (
            back_in_rows,
            ranks,
            all_stats,
            y_heads,
            jnp.broadcast_to(gain_own[:, None], (HP, LANES)),
            read_vectors,
            dt,
        ),
        [VM] * 7,
        [wide],
        flops=8 * HP * LANES * SEQ,
        moved=6 << 20,
        name="mixer_grad",
    )
    after = [sent_along(back_message, -d) for d in range(1, REACH + 1)]
    (input_grad,) = call(
        backward_kernel,
        [((HP, SEQ), bf16)],
        (*after, rt, y_grad, write_vectors, read_vectors, pairs),
        [VM] * 9,
        flops=8 * HP * LANES * SEQ,
        moved=6 << 20,
        name="mixer_backward",
    )
    (block_out,) = call(
        combine_kernel,
        [((WIDTH, LANES), bf16)],
        (ids_own, returned_rows),
        [VM, VM],
        [wide],
        flops=2 * SLOTS * LANES * WIDTH,
        moved=4 << 20,
        name="combine",
    )
    return (block_out, input_grad)


def solution(mesh):
    placed = (
        P("exp", "ctx"),
        P(None, "ctx"),
        P(None, "ctx"),
        P("exp", "ctx"),
        P(),
        P(("ctx", "exp"), None),
        P(("ctx", "exp"), None),
        P(),
        P("exp", "ctx", None),
        P("exp", "ctx", None),
        P(None, ("ctx", "exp")),
    )
    return jax.shard_map(
        per_device,
        mesh=mesh,
        in_specs=placed,
        out_specs=(P(None, ("ctx", "exp")), P("exp", "ctx")),
        check_vma=False,
    )
```

```python
import jax
import jax.numpy as jnp
from jax import lax
from jax.experimental import pallas as pl
from jax.experimental.pallas import tpu as pltpu
from jax.sharding import PartitionSpec as P

f32 = jnp.float32
bf16 = jnp.bfloat16
i32 = jnp.int32

LANES = 128
SEQ = 4096
CHUNKS = SEQ // LANES
PAIRS = CHUNKS // 2
HP = 64
HEAD = 32
EXPERTS = 32
CAP = 10
SLOTS = EXPERTS * CAP
BLOCK = CAP * PAIRS
ROWS = EXPERTS * BLOCK
WIDTH = 2048
FF = 768
FBLOCKS = WIDTH // LANES
REACH = 4
VMEM = 60 * 1024 * 1024

LAST = (((1,), (1,)), ((), ()))
FIRST = (((0,), (0,)), ((), ()))


def dot(a, b):
    return jnp.dot(a, b, preferred_element_type=f32)


def dot_last(a, b):
    return lax.dot_general(a, b, LAST, preferred_element_type=f32)


def dot_first(a, b):
    return lax.dot_general(a, b, FIRST, preferred_element_type=f32)


def split3(value):
    high = value.astype(bf16)
    rest = value - high.astype(f32)
    middle = rest.astype(bf16)
    low = (rest - middle.astype(f32)).astype(bf16)
    return high, middle, low


def rows_of(first, second):
    return jnp.concatenate(
        [jnp.broadcast_to(first, (HEAD, LANES)), jnp.broadcast_to(second, (HEAD, LANES))], axis=0
    )


def earlier_mask():
    row = lax.broadcasted_iota(i32, (LANES, LANES), 0)
    col = lax.broadcasted_iota(i32, (LANES, LANES), 1)
    return jnp.where(row < col, 1.0, 0.0).astype(bf16)


def rank_table(first_ids, second_ids, earlier):
    expert = lax.broadcasted_iota(i32, (EXPERTS, LANES), 0).astype(f32)
    picked = (expert == first_ids) | (expert == second_ids)
    rank = dot(jnp.where(picked, 1.0, 0.0).astype(bf16), earlier)
    return jnp.where(picked, rank, -1.0)


def slot_onehot(ranks):
    return jnp.concatenate(
        [jnp.where(ranks == float(c), 1.0, 0.0).astype(bf16) for c in range(CAP)], axis=0
    )


def round_rows(dst_ref, src_ref):
    def step(i, carry):
        at = pl.ds(pl.multiple_of(i * BLOCK, BLOCK), BLOCK)
        dst_ref[at, :] = src_ref[at, :].astype(dst_ref.dtype)
        return carry

    lax.fori_loop(0, ROWS // BLOCK, step, 0, unroll=4)


def call(kernel, outs, args, in_specs, scratch=(), flops=0, moved=0, name=None):
    vm = pl.BlockSpec(memory_space=pltpu.VMEM)
    return pl.pallas_call(
        kernel,
        out_shape=tuple(jax.ShapeDtypeStruct(shape, kind) for shape, kind in outs),
        in_specs=in_specs,
        out_specs=tuple(vm for _ in outs),
        scratch_shapes=list(scratch),
        compiler_params=pltpu.CompilerParams(vmem_limit_bytes=VMEM),
        cost_estimate=pl.CostEstimate(flops=flops, bytes_accessed=moved, transcendentals=0),
        name=name,
    )(*args)


VM = pl.BlockSpec(memory_space=pltpu.VMEM)
SM = pl.BlockSpec(memory_space=pltpu.SMEM)
HBM = pl.BlockSpec(memory_space=pl.ANY)


def grad_rows_kernel(ids_ref, grad_ref, out_ref, wide_ref):
    ranks = rank_table(ids_ref[0:1, :], ids_ref[1:2, :], earlier_mask())
    select = slot_onehot(ranks)

    def step(fb, carry):
        at = pl.multiple_of(fb * LANES, LANES)
        rows = dot_last(select, grad_ref[pl.ds(at, LANES), :])
        for c in range(CAP):
            wide_ref[pl.ds(c * FBLOCKS + fb, EXPERTS, stride=BLOCK), :] = rows[
                c * EXPERTS : (c + 1) * EXPERTS
            ]
        return carry

    lax.fori_loop(0, FBLOCKS, step, 0, unroll=4)
    round_rows(out_ref, wide_ref)


def tables_kernel(docs_ref, base_ref, decay_ref, x_ref, write_ref, rt_ref, dt_ref, msg_ref):
    decay = decay_ref[...]
    row_i = lax.broadcasted_iota(i32, (LANES, LANES), 0)
    col_i = lax.broadcasted_iota(i32, (LANES, LANES), 1)
    upto = jnp.where(row_i <= col_i, 1.0, 0.0).astype(bf16)
    cum = sum(dot(part, upto) for part in split3(decay))
    rows = 2 * CHUNKS
    chunk_end = jnp.broadcast_to(cum[:, LANES - 1 : LANES], (rows, LANES))
    row_j = lax.broadcasted_iota(i32, (rows, rows), 0)
    col_j = lax.broadcasted_iota(i32, (rows, rows), 1)
    same_head = (row_j >= CHUNKS) == (col_j >= CHUNKS)
    before = jnp.where(same_head & (col_j < row_j), 1.0, 0.0).astype(bf16)
    after = jnp.where(same_head & (col_j > row_j), 1.0, 0.0).astype(bf16)
    parts = split3(chunk_end)
    prefix = sum(dot(before, part) for part in parts)
    suffix = sum(dot(after, part) for part in parts)
    chunk = lax.broadcasted_iota(i32, (rows, LANES), 0)
    chunk = jnp.where(chunk >= CHUNKS, chunk - CHUNKS, chunk)
    token = lax.broadcasted_iota(i32, (rows, LANES), 1)
    place = chunk * LANES + token
    base = base_ref[0]
    doc_start = jnp.full((rows, LANES), -(1 << 20), i32)
    last_start = jnp.int32(-(1 << 20))
    start = -base
    for j in range(docs_ref.shape[0]):
        doc_start = jnp.where(place >= start, jnp.maximum(doc_start, start), doc_start)
        last_start = jnp.where(start <= SEQ - 1, jnp.maximum(last_start, start), last_start)
        start = start + docs_ref[j]
    inner_start = jnp.maximum(doc_start - chunk * LANES, -1)
    inner_float = inner_start.astype(f32)
    inner_last = jnp.broadcast_to(inner_float[:, LANES - 1 : LANES], (rows, LANES))
    to_end = chunk_end - cum
    entering = jnp.where(inner_start < 0, jnp.exp(cum), 0.0)
    leaving = jnp.where(token.astype(f32) >= inner_last, jnp.exp(to_end), 0.0)
    dev_entering = jnp.where(doc_start < 0, jnp.exp(prefix + cum), 0.0)
    dev_leaving = jnp.where(place >= last_start, jnp.exp(to_end + suffix), 0.0)
    for r, value in enumerate(
        (
            cum[:CHUNKS],
            cum[CHUNKS:],
            entering[:CHUNKS],
            entering[CHUNKS:],
            leaving[:CHUNKS],
            leaving[CHUNKS:],
            inner_float[:CHUNKS],
            inner_float[CHUNKS:],
        )
    ):
        rt_ref[pl.ds(r, CHUNKS, stride=8), :] = value
    zero = jnp.zeros((CHUNKS, LANES), f32)
    for r, value in enumerate(
        (
            dev_entering[:CHUNKS],
            dev_entering[CHUNKS:],
            dev_leaving[:CHUNKS],
            dev_leaving[CHUNKS:],
            zero,
            zero,
            zero,
            zero,
        )
    ):
        dt_ref[pl.ds(r, CHUNKS, stride=8), :] = value

    def step(k, acc):
        lanes = pl.ds(pl.multiple_of(k * LANES, LANES), LANES)
        rows_k = dt_ref[pl.ds(pl.multiple_of(k * 8, 8), 8), :]
        scaled = x_ref[:, lanes].astype(f32) * rows_of(rows_k[2:3], rows_k[3:4])
        return acc + dot_last(scaled.astype(bf16), write_ref[:, lanes])

    acc = lax.fori_loop(0, CHUNKS, step, jnp.zeros((HP, LANES), f32), unroll=4)
    msg_ref[0:HP, :] = acc
    through = jnp.concatenate(
        [
            jnp.broadcast_to(dev_entering[CHUNKS - 1 : CHUNKS, LANES - 1 : LANES], (1, LANES)),
            jnp.broadcast_to(dev_entering[rows - 1 : rows, LANES - 1 : LANES], (1, LANES)),
            jnp.zeros((6, LANES), f32),
        ],
        axis=0,
    )
    msg_ref[HP : HP + 8, :] = through


def chained(refs):
    state = refs[-1][0:HP, :]
    for ref in refs[-2::-1]:
        state = ref[0:HP, :] + rows_of(ref[HP : HP + 1, :], ref[HP + 1 : HP + 2, :]) * state
    return state


def forward_kernel(
    expert_ref,
    m1_ref,
    m2_ref,
    m3_ref,
    m4_ref,
    rt_ref,
    x_ref,
    write_ref,
    read_ref,
    ids_ref,
    pair_ref,
    msg_ref,
    rank_ref,
    weight_ref,
    first_ref,
    wide_ref,
    y_ref,
):
    earlier = earlier_mask()
    mine = expert_ref[0].astype(f32)
    is_first = ids_ref[0] == mine
    is_second = ids_ref[1] == mine
    picked = is_first | is_second
    rank = dot(jnp.where(picked, 1.0, 0.0).astype(bf16), earlier)
    rank = jnp.where(picked, rank, -1.0)
    route = jnp.where(is_first, ids_ref[2], jnp.where(is_second, ids_ref[3], 0.0))
    first = jnp.where(is_first, 1.0, 0.0)
    for c in range(CAP):
        here = rank == float(c)
        route_c = jnp.sum(jnp.where(here, route, 0.0), axis=1, keepdims=True)
        first_c = jnp.sum(jnp.where(here, first, 0.0), axis=1, keepdims=True)
        for par in range(2):
            at = (par * CAP + c) * PAIRS
            part = slice(par * PAIRS, (par + 1) * PAIRS)
            weight_ref[at : at + PAIRS, :] = jnp.broadcast_to(route_c[part], (PAIRS, LANES))
            first_ref[at : at + PAIRS, :] = jnp.broadcast_to(first_c[part], (PAIRS, LANES))

    row_i = lax.broadcasted_iota(i32, (LANES, LANES), 0)
    col_i = lax.broadcasted_iota(i32, (LANES, LANES), 1)
    causal = row_i <= col_i
    row_f = row_i.astype(f32)

    def step(k, state):
        lanes = pl.ds(pl.multiple_of(k * LANES, LANES), LANES)
        rows = rt_ref[pl.ds(pl.multiple_of(k * 8, 8), 8), :]
        cols = rows.T
        x = x_ref[:, lanes]
        write = write_ref[:, lanes]
        read = read_ref[:, lanes]
        scores = dot_first(write, read)
        valid = causal & (row_f >= rows[6:7, :])
        inside = []
        for h in range(2):
            gap = rows[h : h + 1, :] - cols[:, h : h + 1]
            pair = jnp.where(valid, jnp.exp(gap) * scores, 0.0).astype(bf16)
            pair_ref[pl.ds(pl.multiple_of((2 * k + h) * LANES, LANES), LANES), :] = pair
            inside.append(dot(x[h * HEAD : (h + 1) * HEAD, :], pair))
        carried = dot(state.astype(bf16), read) * rows_of(rows[2:3], rows[3:4])
        y_ref[:, lanes] = (jnp.concatenate(inside, axis=0) + carried).astype(bf16)
        scaled = (x.astype(f32) * rows_of(rows[4:5], rows[5:6])).astype(bf16)
        through = rows_of(
            jnp.broadcast_to(rows[2:3, LANES - 1 : LANES], (1, LANES)),
            jnp.broadcast_to(rows[3:4, LANES - 1 : LANES], (1, LANES)),
        )
        return through * state + dot_last(scaled, write)

    lax.fori_loop(0, CHUNKS, step, chained((m1_ref, m2_ref, m3_ref, m4_ref)), unroll=4)

    zero = jnp.zeros((HP, LANES), bf16)

    def dispatch(jp, carry):
        tables = []
        for par in range(2):
            j = par * PAIRS + jp
            table = rank_table(
                ids_ref[0, pl.ds(j, 1), :], ids_ref[1, pl.ds(j, 1), :], earlier
            )
            at = pl.multiple_of(jp * 64 + par * EXPERTS, EXPERTS)
            rank_ref[pl.ds(at, EXPERTS), :] = table
            tables.append(table)
        select = slot_onehot(jnp.concatenate(tables, axis=1))
        even = y_ref[:, pl.ds(pl.multiple_of(jp * 2 * LANES, LANES), LANES)]
        odd = y_ref[:, pl.ds(pl.multiple_of(jp * 2 * LANES + LANES, LANES), LANES)]
        both = jnp.concatenate(
            [jnp.concatenate([even, zero], axis=1), jnp.concatenate([zero, odd], axis=1)], axis=0
        )
        rows = dot_last(select, both)
        for c in range(CAP):
            wide_ref[pl.ds(c * PAIRS + jp, EXPERTS, stride=BLOCK), :] = rows[
                c * EXPERTS : (c + 1) * EXPERTS
            ]
        return carry

    lax.fori_loop(0, PAIRS, dispatch, 0, unroll=2)
    round_rows(msg_ref, wide_ref)


def arrived_grad_kernel(
    rows_ref, weight_ref, out_hbm, grad_ref, dhid_ref, wide_ref, scaled_ref, out_ref, sem
):
    fetch = pltpu.make_async_copy(out_hbm, out_ref, sem)
    fetch.start()
    round_rows(wide_ref, rows_ref)

    def unpack(fb, carry):
        lanes = pl.ds(pl.multiple_of(fb * LANES, LANES), LANES)
        for par in range(2):
            for c in range(CAP):
                at = (par * CAP + c) * PAIRS
                rows = wide_ref[
                    pl.ds(par * BLOCK + c * FBLOCKS + fb, PAIRS, stride=2 * BLOCK), :
                ]
                grad_ref[at : at + PAIRS, lanes] = rows.astype(bf16)
                scaled_ref[at : at + PAIRS, lanes] = (
                    rows * weight_ref[at : at + PAIRS, :]
                ).astype(bf16)
        return carry

    lax.fori_loop(0, FBLOCKS, unpack, 0, unroll=2)
    fetch.wait()

    def matmul(i, carry):
        lanes = pl.ds(pl.multiple_of(i * 256, 256), 256)
        dhid_ref[:, lanes] = dot(scaled_ref[...], out_ref[:, lanes])
        return carry

    lax.fori_loop(0, FF // 256, matmul, 0)


def expert_kernel(
    rows_ref,
    gain_ref,
    first_ref,
    grad_ref,
    dhid_ref,
    in_hbm,
    msg_ref,
    normed_ref,
    hidden_ref,
    y_ref,
    scaled_ref,
    dcat_ref,
    in_ref,
    sem,
):
    fetch = pltpu.make_async_copy(in_hbm, in_ref, sem)
    fetch.start()
    lane = lax.broadcasted_iota(i32, (BLOCK, LANES), 1)
    low = lane < 64

    def unpack(k, squares):
        lanes = pl.ds(pl.multiple_of(k * LANES, LANES), LANES)
        at = pl.multiple_of(k * 2 * BLOCK, BLOCK)
        a = rows_ref[pl.ds(at, BLOCK), :].astype(f32)
        b = rows_ref[pl.ds(at + BLOCK, BLOCK), :].astype(f32)
        even = jnp.where(low, a, pltpu.roll(b, 64, 1))
        odd = jnp.where(low, pltpu.roll(a, 64, 1), b)
        both = jnp.concatenate([even, odd], axis=0)
        y_ref[:, lanes] = both
        return squares + both * both

    squares = lax.fori_loop(0, FBLOCKS, unpack, jnp.zeros((SLOTS, LANES), f32))
    mean = jnp.sum(squares, axis=1, keepdims=True) * (1.0 / WIDTH)
    rscale = lax.rsqrt(mean + 1e-06)
    rscale_b = jnp.broadcast_to(rscale, (SLOTS, LANES))

    def scale(k, carry):
        lanes = pl.ds(pl.multiple_of(k * LANES, LANES), LANES)
        normed_ref[:, lanes] = (y_ref[:, lanes] * rscale_b * gain_ref[:, lanes]).astype(bf16)
        return carry

    lax.fori_loop(0, FBLOCKS, scale, 0)
    fetch.wait()

    def project(i, carry):
        lanes = pl.ds(pl.multiple_of(i * 256, 256), 256)
        lanes_up = pl.ds(pl.multiple_of(FF + i * 256, 256), 256)
        gate = dot(normed_ref[...], in_ref[:, lanes])
        up = dot(normed_ref[...], in_ref[:, lanes_up])
        sigmoid = 1.0 / (1.0 + jnp.exp(-gate))
        swish = gate * sigmoid
        hidden_ref[:, lanes] = (swish * up).astype(bf16)
        dhid = dhid_ref[:, lanes]
        dcat_ref[:, lanes] = (dhid * up * sigmoid * (1.0 + gate * (1.0 - sigmoid))).astype(bf16)
        dcat_ref[:, lanes_up] = (dhid * swish).astype(bf16)
        return carry

    lax.fori_loop(0, FF // 256, project, 0)
    first = first_ref[...]
    first2 = jnp.concatenate([first, first], axis=1)

    def back(i, acc):
        at = pl.multiple_of(i * 256, 256)
        lanes = pl.ds(at, 256)
        grad = dot_last(dcat_ref[...], in_ref[lanes, :]) + first2 * grad_ref[:, lanes].astype(f32)
        scaled = grad * gain_ref[:, lanes]
        scaled_ref[:, lanes] = scaled
        product = scaled * y_ref[:, lanes]
        return acc + product[:, :LANES] + product[:, LANES:]

    acc = lax.fori_loop(0, WIDTH // 256, back, jnp.zeros((SLOTS, LANES), f32))
    mean_grad = jnp.sum(acc, axis=1, keepdims=True) * (1.0 / WIDTH)
    pull = jnp.broadcast_to(rscale * rscale * rscale * mean_grad, (SLOTS, LANES))

    def pack(k, carry):
        lanes = pl.ds(pl.multiple_of(k * LANES, LANES), LANES)
        part = rscale_b * scaled_ref[:, lanes] - pull * y_ref[:, lanes]
        even, odd = part[:BLOCK], part[BLOCK:]
        row = pl.multiple_of(k * 2 * BLOCK, BLOCK)
        msg_ref[pl.ds(row, BLOCK), :] = jnp.where(low, even, pltpu.roll(odd, 64, 1)).astype(bf16)
        msg_ref[pl.ds(row + BLOCK, BLOCK), :] = jnp.where(low, pltpu.roll(even, 64, 1), odd).astype(
            bf16
        )
        return carry

    lax.fori_loop(0, FBLOCKS, pack, 0)


def expert_out_kernel(
    hidden_ref, normed_ref, weight_ref, first_ref, out_hbm, msg_ref, wide_ref, out_ref, sem
):
    fetch = pltpu.make_async_copy(out_hbm, out_ref, sem)
    fetch.start()
    weight = weight_ref[...]
    weight2 = jnp.concatenate([weight, weight], axis=1)
    first = first_ref[...]
    first2 = jnp.concatenate([first, first], axis=1)
    fetch.wait()

    def matmul(i, carry):
        lanes = pl.ds(pl.multiple_of(i * 256, 256), 256)
        result = dot_last(hidden_ref[...], out_ref[lanes, :])
        result = weight2 * result + first2 * normed_ref[:, lanes].astype(f32)
        for half in range(2):
            part = result[:, half * LANES : (half + 1) * LANES]
            fb = 2 * i + half
            for par in range(2):
                for c in range(CAP):
                    at = (par * CAP + c) * PAIRS
                    wide_ref[
                        pl.ds(par * BLOCK + c * FBLOCKS + fb, PAIRS, stride=2 * BLOCK), :
                    ] = part[at : at + PAIRS]
        return carry

    lax.fori_loop(0, WIDTH // 256, matmul, 0)
    round_rows(msg_ref, wide_ref)


def combine_kernel(ids_ref, rows_ref, out_ref, wide_ref):
    round_rows(wide_ref, rows_ref)
    select = slot_onehot(rank_table(ids_ref[0:1, :], ids_ref[1:2, :], earlier_mask()))

    def step(fb, carry):
        rows = jnp.concatenate(
            [
                wide_ref[pl.ds(c * FBLOCKS + fb, EXPERTS, stride=BLOCK), :].astype(bf16)
                for c in range(CAP)
            ],
            axis=0,
        )
        at = pl.multiple_of(fb * LANES, LANES)
        out_ref[pl.ds(at, LANES), :] = dot_first(rows, select).astype(bf16)
        return carry

    lax.fori_loop(0, FBLOCKS, step, 0, unroll=4)


def grad_kernel(rows_ref, rank_ref, read_ref, dt_ref, out_ref, msg_ref, wide_ref):
    round_rows(wide_ref, rows_ref)

    def step(jp, acc):
        at = pl.multiple_of(jp * 64, 64)
        ranks = rank_ref[pl.ds(at, 64), :]
        select = slot_onehot(jnp.concatenate([ranks[:EXPERTS], ranks[EXPERTS:]], axis=1))
        rows = jnp.concatenate(
            [
                wide_ref[pl.ds(c * PAIRS + jp, EXPERTS, stride=BLOCK), :].astype(bf16)
                for c in range(CAP)
            ],
            axis=0,
        )
        both = dot_first(rows, select)
        for par in range(2):
            lanes = pl.ds(pl.multiple_of((2 * jp + par) * LANES, LANES), LANES)
            grad = both[par * HP : (par + 1) * HP, par * LANES : (par + 1) * LANES].astype(bf16)
            out_ref[:, lanes] = grad
            rows_k = dt_ref[pl.ds(pl.multiple_of((2 * jp + par) * 8, 8), 8), :]
            weighted = (grad.astype(f32) * rows_of(rows_k[0:1], rows_k[1:2])).astype(bf16)
            acc = acc + dot_last(weighted, read_ref[:, lanes])
        return acc

    msg_ref[0:HP, :] = lax.fori_loop(0, PAIRS, step, jnp.zeros((HP, LANES), f32), unroll=2)
    last = dt_ref[(CHUNKS - 1) * 8 : CHUNKS * 8, :]
    msg_ref[HP : HP + 8, :] = jnp.broadcast_to(last[:, LANES - 1 : LANES], (8, LANES))


def backward_kernel(
    m1_ref, m2_ref, m3_ref, m4_ref, rt_ref, grad_ref, write_ref, read_ref, pair_ref, out_ref
):
    def step(i, state):
        k = CHUNKS - 1 - i
        lanes = pl.ds(pl.multiple_of(k * LANES, LANES), LANES)
        rows = rt_ref[pl.ds(pl.multiple_of(k * 8, 8), 8), :]
        grad = grad_ref[:, lanes]
        write = write_ref[:, lanes]
        read = read_ref[:, lanes]
        inside = []
        for h in range(2):
            pair = pair_ref[pl.ds(pl.multiple_of((2 * k + h) * LANES, LANES), LANES), :]
            inside.append(dot_last(grad[h * HEAD : (h + 1) * HEAD, :], pair))
        carried = dot(state.astype(bf16), write) * rows_of(rows[4:5], rows[5:6])
        out_ref[:, lanes] = (jnp.concatenate(inside, axis=0) + carried).astype(bf16)
        scaled = (grad.astype(f32) * rows_of(rows[2:3], rows[3:4])).astype(bf16)
        through = rows_of(
            jnp.broadcast_to(rows[2:3, LANES - 1 : LANES], (1, LANES)),
            jnp.broadcast_to(rows[3:4, LANES - 1 : LANES], (1, LANES)),
        )
        return through * state + dot_last(scaled, read)

    lax.fori_loop(0, CHUNKS, step, chained((m1_ref, m2_ref, m3_ref, m4_ref)), unroll=4)


def sent_along(value, by):
    size = lax.axis_size("ctx")
    pairs = [(i, i + by) for i in range(size) if 0 <= i + by < size]
    return lax.ppermute(value, "ctx", pairs)


def exchanged(rows):
    blocks = rows.reshape(EXPERTS, BLOCK, LANES)
    return lax.all_to_all(blocks, "exp", split_axis=0, concat_axis=0, tiled=True).reshape(
        ROWS, LANES
    )


def per_device(
    features,
    write_vectors,
    read_vectors,
    log_decay,
    doc_lengths,
    expert_ids,
    route_weights,
    norm_gain,
    expert_in,
    expert_out,
    out_grad,
):
    me_ctx = lax.axis_index("ctx")
    me_exp = lax.axis_index("exp")
    wide = pltpu.VMEM((ROWS, LANES), f32)
    ids_own = expert_ids.T.astype(f32)
    tokens_own = jnp.concatenate([ids_own, route_weights.T], axis=0)
    tokens = lax.all_to_all(
        jnp.broadcast_to(tokens_own[None], (EXPERTS, 4, LANES)), "exp", 0, 0, tiled=True
    )
    tokens = tokens.reshape(PAIRS, 2, 4, LANES).transpose(2, 1, 0, 3).reshape(4, CHUNKS, LANES)

    (grad_out_rows,) = call(
        grad_rows_kernel,
        [((ROWS, LANES), bf16)],
        (ids_own, out_grad),
        [VM, VM],
        [wide],
        flops=2 * SLOTS * LANES * WIDTH,
        moved=4 << 20,
        name="grad_rows",
    )
    grad_in_rows = exchanged(grad_out_rows)

    weight_in = lax.all_gather(expert_in, "ctx", axis=1, tiled=True)[0]
    weight_out = lax.all_gather(expert_out, "ctx", axis=1, tiled=True)[0]
    rt, dt, message = call(
        tables_kernel,
        [((CHUNKS * 8, LANES), f32), ((CHUNKS * 8, LANES), f32), ((HP + 8, LANES), f32)],
        (
            doc_lengths,
            (me_ctx * SEQ).astype(i32).reshape(1),
            log_decay.reshape(2 * CHUNKS, LANES),
            features,
            write_vectors,
        ),
        [SM, SM, VM, VM, VM],
        flops=2 * HP * LANES * SEQ,
        moved=3 << 20,
        name="shard_state",
    )
    before = [sent_along(message, d) for d in range(1, REACH + 1)]
    pairs, y_out_rows, ranks, slot_weight, slot_first = call(
        forward_kernel,
        [
            ((2 * CHUNKS * LANES, LANES), bf16),
            ((ROWS, LANES), bf16),
            ((2 * CHUNKS // 2 * EXPERTS, LANES), f32),
            ((SLOTS, LANES), f32),
            ((SLOTS, LANES), f32),
        ],
        (
            me_exp.astype(i32).reshape(1),
            *before,
            rt,
            features,
            write_vectors,
            read_vectors,
            tokens,
        ),
        [SM] + [VM] * 9,
        [wide, pltpu.VMEM((HP, SEQ), bf16)],
        flops=8 * HP * LANES * SEQ,
        moved=9 << 20,
        name="mixer_forward",
    )
    y_in_rows = exchanged(y_out_rows)

    grad_slots, d_hidden = call(
        arrived_grad_kernel,
        [((SLOTS, WIDTH), bf16), ((SLOTS, FF), f32)],
        (grad_in_rows, slot_weight, weight_out),
        [VM, VM, HBM],
        [wide, pltpu.VMEM((SLOTS, WIDTH), bf16), pltpu.VMEM((WIDTH, FF), bf16), pltpu.SemaphoreType.DMA],
        flops=2 * SLOTS * FF * WIDTH,
        moved=8 << 20,
        name="hidden_grad",
    )
    back_out_rows, normed, hidden = call(
        expert_kernel,
        [
            ((ROWS, LANES), bf16),
            ((SLOTS, WIDTH), bf16),
            ((SLOTS, FF), bf16),
        ],
        (y_in_rows, norm_gain.reshape(1, WIDTH), slot_first, grad_slots, d_hidden, weight_in),
        [VM, VM, VM, VM, VM, HBM],
        [
            pltpu.VMEM((SLOTS, WIDTH), f32),
            pltpu.VMEM((SLOTS, WIDTH), f32),
            pltpu.VMEM((SLOTS, 2 * FF), bf16),
            pltpu.VMEM((WIDTH, 2 * FF), bf16),
            pltpu.SemaphoreType.DMA,
        ],
        flops=8 * SLOTS * FF * WIDTH,
        moved=14 << 20,
        name="expert",
    )
    back_in_rows = exchanged(back_out_rows)

    (result_rows,) = call(
        expert_out_kernel,
        [((ROWS, LANES), bf16)],
        (hidden, normed, slot_weight, slot_first, weight_out),
        [VM, VM, VM, VM, HBM],
        [wide, pltpu.VMEM((WIDTH, FF), bf16), pltpu.SemaphoreType.DMA],
        flops=2 * SLOTS * FF * WIDTH,
        moved=8 << 20,
        name="expert_out",
    )
    returned_rows = exchanged(result_rows)

    y_grad, back_message = call(
        grad_kernel,
        [((HP, SEQ), bf16), ((HP + 8, LANES), f32)],
        (back_in_rows, ranks, read_vectors, dt),
        [VM] * 4,
        [wide],
        flops=8 * HP * LANES * SEQ,
        moved=6 << 20,
        name="mixer_grad",
    )
    after = [sent_along(back_message, -d) for d in range(1, REACH + 1)]
    (input_grad,) = call(
        backward_kernel,
        [((HP, SEQ), bf16)],
        (*after, rt, y_grad, write_vectors, read_vectors, pairs),
        [VM] * 9,
        flops=8 * HP * LANES * SEQ,
        moved=6 << 20,
        name="mixer_backward",
    )
    returned_rows, input_grad = lax.optimization_barrier((returned_rows, input_grad))
    (block_out,) = call(
        combine_kernel,
        [((WIDTH, LANES), bf16)],
        (ids_own, returned_rows),
        [VM, VM],
        [wide],
        flops=2 * SLOTS * LANES * WIDTH,
        moved=4 << 20,
        name="combine",
    )
    return (block_out, input_grad)


def solution(mesh):
    placed = (
        P("exp", "ctx"),
        P(None, "ctx"),
        P(None, "ctx"),
        P("exp", "ctx"),
        P(),
        P(("ctx", "exp"), None),
        P(("ctx", "exp"), None),
        P(),
        P("exp", "ctx", None),
        P("exp", "ctx", None),
        P(None, ("ctx", "exp")),
    )
    return jax.shard_map(
        per_device,
        mesh=mesh,
        in_specs=placed,
        out_specs=(P(None, ("ctx", "exp")), P("exp", "ctx")),
        check_vma=False,
    )
```

```python
import jax
import jax.numpy as jnp
from jax import lax
from jax.experimental import pallas as pl
from jax.experimental.pallas import tpu as pltpu
from jax.sharding import PartitionSpec as P

f32 = jnp.float32
bf16 = jnp.bfloat16
i32 = jnp.int32

LANES = 128
SEQ = 4096
CHUNKS = SEQ // LANES
PAIRS = CHUNKS // 2
HP = 64
HEAD = 32
EXPERTS = 32
CHIPS = 16
CAP = 10
SLOTS = EXPERTS * CAP
BLOCK = CAP * PAIRS
ROWS = EXPERTS * BLOCK
WIDTH = 2048
FF = 768
FBLOCKS = WIDTH // LANES
REACH = 4
VMEM = 60 * 1024 * 1024

LAST = (((1,), (1,)), ((), ()))
FIRST = (((0,), (0,)), ((), ()))


def dot(a, b):
    return jnp.dot(a, b, preferred_element_type=f32)


def dot_last(a, b):
    return lax.dot_general(a, b, LAST, preferred_element_type=f32)


def dot_first(a, b):
    return lax.dot_general(a, b, FIRST, preferred_element_type=f32)


def split3(value):
    high = value.astype(bf16)
    rest = value - high.astype(f32)
    middle = rest.astype(bf16)
    low = (rest - middle.astype(f32)).astype(bf16)
    return high, middle, low


def rows_of(first, second):
    return jnp.concatenate(
        [jnp.broadcast_to(first, (HEAD, LANES)), jnp.broadcast_to(second, (HEAD, LANES))], axis=0
    )


def earlier_mask():
    row = lax.broadcasted_iota(i32, (LANES, LANES), 0)
    col = lax.broadcasted_iota(i32, (LANES, LANES), 1)
    return jnp.where(row < col, 1.0, 0.0).astype(bf16)


def rank_table(first_ids, second_ids, earlier, experts=EXPERTS, core=None):
    expert = lax.broadcasted_iota(i32, (experts, LANES), 0)
    if core is not None:
        expert = 2 * expert + core
    expert = expert.astype(f32)
    picked = (expert == first_ids) | (expert == second_ids)
    rank = dot(jnp.where(picked, 1.0, 0.0).astype(bf16), earlier)
    return jnp.where(picked, rank, -1.0)


def slot_onehot(ranks):
    return jnp.concatenate(
        [jnp.where(ranks == float(c), 1.0, 0.0).astype(bf16) for c in range(CAP)], axis=0
    )


def round_rows(dst_ref, src_ref):
    def step(i, carry):
        at = pl.ds(pl.multiple_of(i * BLOCK, BLOCK), BLOCK)
        dst_ref[at, :] = src_ref[at, :].astype(dst_ref.dtype)
        return carry

    lax.fori_loop(0, ROWS // BLOCK, step, 0, unroll=4)


def call(kernel, outs, args, in_specs, scratch=(), flops=0, moved=0, name=None):
    vm = pl.BlockSpec(memory_space=pltpu.VMEM)
    return pl.pallas_call(
        kernel,
        out_shape=tuple(jax.ShapeDtypeStruct(shape, kind) for shape, kind in outs),
        in_specs=in_specs,
        out_specs=tuple(vm for _ in outs),
        scratch_shapes=list(scratch),
        compiler_params=pltpu.CompilerParams(vmem_limit_bytes=VMEM),
        cost_estimate=pl.CostEstimate(flops=flops, bytes_accessed=moved, transcendentals=0),
        name=name,
    )(*args)


VM = pl.BlockSpec(memory_space=pltpu.VMEM)
SM = pl.BlockSpec(memory_space=pltpu.SMEM)
HBM = pl.BlockSpec(memory_space=pl.ANY)


def grad_rows_kernel(core_ref, own_ids_ref, their_ids_ref, own_ref, their_ref, out_ref, wide_ref):
    core = core_ref[0]
    earlier = earlier_mask()

    def select_of(ids_ref):
        return slot_onehot(rank_table(ids_ref[0:1, :], ids_ref[1:2, :], earlier, CHIPS, core))

    own_select, their_select = select_of(own_ids_ref), select_of(their_ids_ref)

    def step(fb, carry):
        feats = pl.ds(pl.multiple_of(fb * LANES, LANES), LANES)
        for select, grad_ref, side in (
            (own_select, own_ref, core),
            (their_select, their_ref, 1 - core),
        ):
            rows = dot_last(select, grad_ref[feats, :])
            for c in range(CAP):
                wide_ref[pl.ds(side * BLOCK + c * FBLOCKS + fb, CHIPS, stride=2 * BLOCK), :] = rows[
                    c * CHIPS : (c + 1) * CHIPS
                ]
        return carry

    lax.fori_loop(0, FBLOCKS, step, 0, unroll=4)
    round_rows(out_ref, wide_ref)


def tables_kernel(docs_ref, base_ref, decay_ref, x_ref, write_ref, rt_ref, dt_ref, msg_ref):
    decay = decay_ref[...]
    row_i = lax.broadcasted_iota(i32, (LANES, LANES), 0)
    col_i = lax.broadcasted_iota(i32, (LANES, LANES), 1)
    upto = jnp.where(row_i <= col_i, 1.0, 0.0).astype(bf16)
    cum = sum(dot(part, upto) for part in split3(decay))
    rows = 2 * CHUNKS
    chunk_end = jnp.broadcast_to(cum[:, LANES - 1 : LANES], (rows, LANES))
    row_j = lax.broadcasted_iota(i32, (rows, rows), 0)
    col_j = lax.broadcasted_iota(i32, (rows, rows), 1)
    same_head = (row_j >= CHUNKS) == (col_j >= CHUNKS)
    before = jnp.where(same_head & (col_j < row_j), 1.0, 0.0).astype(bf16)
    after = jnp.where(same_head & (col_j > row_j), 1.0, 0.0).astype(bf16)
    parts = split3(chunk_end)
    prefix = sum(dot(before, part) for part in parts)
    suffix = sum(dot(after, part) for part in parts)
    chunk = lax.broadcasted_iota(i32, (rows, LANES), 0)
    chunk = jnp.where(chunk >= CHUNKS, chunk - CHUNKS, chunk)
    token = lax.broadcasted_iota(i32, (rows, LANES), 1)
    place = chunk * LANES + token
    base = base_ref[0]
    doc_start = jnp.full((rows, LANES), -(1 << 20), i32)
    last_start = jnp.int32(-(1 << 20))
    start = -base
    for j in range(docs_ref.shape[0]):
        doc_start = jnp.where(place >= start, jnp.maximum(doc_start, start), doc_start)
        last_start = jnp.where(start <= SEQ - 1, jnp.maximum(last_start, start), last_start)
        start = start + docs_ref[j]
    inner_start = jnp.maximum(doc_start - chunk * LANES, -1)
    inner_float = inner_start.astype(f32)
    inner_last = jnp.broadcast_to(inner_float[:, LANES - 1 : LANES], (rows, LANES))
    to_end = chunk_end - cum
    entering = jnp.where(inner_start < 0, jnp.exp(cum), 0.0)
    leaving = jnp.where(token.astype(f32) >= inner_last, jnp.exp(to_end), 0.0)
    dev_entering = jnp.where(doc_start < 0, jnp.exp(prefix + cum), 0.0)
    dev_leaving = jnp.where(place >= last_start, jnp.exp(to_end + suffix), 0.0)
    for r, value in enumerate(
        (
            cum[:CHUNKS],
            cum[CHUNKS:],
            entering[:CHUNKS],
            entering[CHUNKS:],
            leaving[:CHUNKS],
            leaving[CHUNKS:],
            inner_float[:CHUNKS],
            inner_float[CHUNKS:],
        )
    ):
        rt_ref[pl.ds(r, CHUNKS, stride=8), :] = value
    zero = jnp.zeros((CHUNKS, LANES), f32)
    for r, value in enumerate(
        (
            dev_entering[:CHUNKS],
            dev_entering[CHUNKS:],
            dev_leaving[:CHUNKS],
            dev_leaving[CHUNKS:],
            zero,
            zero,
            zero,
            zero,
        )
    ):
        dt_ref[pl.ds(r, CHUNKS, stride=8), :] = value

    def step(k, acc):
        lanes = pl.ds(pl.multiple_of(k * LANES, LANES), LANES)
        rows_k = dt_ref[pl.ds(pl.multiple_of(k * 8, 8), 8), :]
        scaled = x_ref[:, lanes].astype(f32) * rows_of(rows_k[2:3], rows_k[3:4])
        return acc + dot_last(scaled.astype(bf16), write_ref[:, lanes])

    acc = lax.fori_loop(0, CHUNKS, step, jnp.zeros((HP, LANES), f32), unroll=4)
    msg_ref[0:HP, :] = acc
    through = jnp.concatenate(
        [
            jnp.broadcast_to(dev_entering[CHUNKS - 1 : CHUNKS, LANES - 1 : LANES], (1, LANES)),
            jnp.broadcast_to(dev_entering[rows - 1 : rows, LANES - 1 : LANES], (1, LANES)),
            jnp.zeros((6, LANES), f32),
        ],
        axis=0,
    )
    msg_ref[HP : HP + 8, :] = through


def chained(refs):
    state = refs[-1][0:HP, :]
    for ref in refs[-2::-1]:
        state = ref[0:HP, :] + rows_of(ref[HP : HP + 1, :], ref[HP + 1 : HP + 2, :]) * state
    return state


def forward_kernel(
    m1_ref, m2_ref, m3_ref, m4_ref, rt_ref, x_ref, write_ref, read_ref, y_ref, pair_ref
):
    row_i = lax.broadcasted_iota(i32, (LANES, LANES), 0)
    col_i = lax.broadcasted_iota(i32, (LANES, LANES), 1)
    causal = row_i <= col_i
    row_f = row_i.astype(f32)

    def step(k, state):
        lanes = pl.ds(pl.multiple_of(k * LANES, LANES), LANES)
        rows = rt_ref[pl.ds(pl.multiple_of(k * 8, 8), 8), :]
        cols = rows.T
        x = x_ref[:, lanes]
        write = write_ref[:, lanes]
        read = read_ref[:, lanes]
        scores = dot_first(write, read)
        valid = causal & (row_f >= rows[6:7, :])
        inside = []
        for h in range(2):
            gap = rows[h : h + 1, :] - cols[:, h : h + 1]
            pair = jnp.where(valid, jnp.exp(gap) * scores, 0.0).astype(bf16)
            pair_ref[pl.ds(pl.multiple_of((2 * k + h) * LANES, LANES), LANES), :] = pair
            inside.append(dot(x[h * HEAD : (h + 1) * HEAD, :], pair))
        carried = dot(state.astype(bf16), read) * rows_of(rows[2:3], rows[3:4])
        y_ref[:, lanes] = (jnp.concatenate(inside, axis=0) + carried).astype(bf16)
        scaled = (x.astype(f32) * rows_of(rows[4:5], rows[5:6])).astype(bf16)
        through = rows_of(
            jnp.broadcast_to(rows[2:3, LANES - 1 : LANES], (1, LANES)),
            jnp.broadcast_to(rows[3:4, LANES - 1 : LANES], (1, LANES)),
        )
        return through * state + dot_last(scaled, write)

    lax.fori_loop(0, CHUNKS, step, chained((m1_ref, m2_ref, m3_ref, m4_ref)), unroll=4)


def dispatch_kernel(
    expert_ref, own_ref, their_ref, ids_ref, msg_ref, rank_ref, weight_ref, first_ref, wide_ref
):
    core = lax.rem(expert_ref[0], 2)
    earlier = earlier_mask()
    mine = expert_ref[0].astype(f32)
    is_first = ids_ref[0] == mine
    is_second = ids_ref[1] == mine
    picked = is_first | is_second
    rank = dot(jnp.where(picked, 1.0, 0.0).astype(bf16), earlier)
    rank = jnp.where(picked, rank, -1.0)
    route = jnp.where(is_first, ids_ref[2], jnp.where(is_second, ids_ref[3], 0.0))
    first = jnp.where(is_first, 1.0, 0.0)
    for c in range(CAP):
        here = rank == float(c)
        route_c = jnp.sum(jnp.where(here, route, 0.0), axis=1, keepdims=True)
        first_c = jnp.sum(jnp.where(here, first, 0.0), axis=1, keepdims=True)
        for par in range(2):
            at = (par * CAP + c) * PAIRS
            part = slice(par * PAIRS, (par + 1) * PAIRS)
            weight_ref[at : at + PAIRS, :] = jnp.broadcast_to(route_c[part], (PAIRS, LANES))
            first_ref[at : at + PAIRS, :] = jnp.broadcast_to(first_c[part], (PAIRS, LANES))

    def step(jp, carry):
        for par in range(2):
            j = par * PAIRS + jp
            table = rank_table(
                ids_ref[0, pl.ds(j, 1), :], ids_ref[1, pl.ds(j, 1), :], earlier, CHIPS, core
            )
            rank_ref[pl.ds(pl.multiple_of((2 * jp + par) * CHIPS, CHIPS), CHIPS), :] = table
            lanes = pl.ds(pl.multiple_of((2 * jp + par) * LANES, LANES), LANES)
            own = own_ref[:, lanes]
            their = their_ref[:, lanes]
            both = jnp.concatenate(
                [jnp.where(core == 0, own, their), jnp.where(core == 0, their, own)], axis=0
            )
            rows = dot_last(slot_onehot(table), both)
            for c in range(CAP):
                at = par * BLOCK + c * PAIRS + jp
                wide_ref[pl.ds(at, CHIPS, stride=2 * BLOCK), :] = rows[c * CHIPS : (c + 1) * CHIPS]
        return carry

    lax.fori_loop(0, PAIRS, step, 0, unroll=2)
    round_rows(msg_ref, wide_ref)


def arrived_grad_kernel(
    rows_ref, weight_ref, out_hbm, grad_ref, dhid_ref, wide_ref, scaled_ref, out_ref, sem
):
    fetch = pltpu.make_async_copy(out_hbm, out_ref, sem)
    fetch.start()
    round_rows(wide_ref, rows_ref)

    def unpack(fb, carry):
        lanes = pl.ds(pl.multiple_of(fb * LANES, LANES), LANES)
        for par in range(2):
            for c in range(CAP):
                at = (par * CAP + c) * PAIRS
                rows = wide_ref[
                    pl.ds(par * BLOCK + c * FBLOCKS + fb, PAIRS, stride=2 * BLOCK), :
                ]
                grad_ref[at : at + PAIRS, lanes] = rows.astype(bf16)
                scaled_ref[at : at + PAIRS, lanes] = (
                    rows * weight_ref[at : at + PAIRS, :]
                ).astype(bf16)
        return carry

    lax.fori_loop(0, FBLOCKS, unpack, 0, unroll=2)
    fetch.wait()

    def matmul(i, carry):
        lanes = pl.ds(pl.multiple_of(i * 256, 256), 256)
        dhid_ref[:, lanes] = dot(scaled_ref[...], out_ref[:, lanes])
        return carry

    lax.fori_loop(0, FF // 256, matmul, 0)


def expert_kernel(
    rows_ref,
    gain_ref,
    first_ref,
    grad_ref,
    dhid_ref,
    in_hbm,
    msg_ref,
    normed_ref,
    hidden_ref,
    y_ref,
    scaled_ref,
    dcat_ref,
    in_ref,
    sem,
):
    fetch = pltpu.make_async_copy(in_hbm, in_ref, sem)
    fetch.start()

    def unpack(k, squares):
        lanes = pl.ds(pl.multiple_of(k * LANES, LANES), LANES)
        y = rows_ref[pl.ds(pl.multiple_of(k * SLOTS, SLOTS), SLOTS), :].astype(f32)
        y_ref[:, lanes] = y
        return squares + y * y

    squares = lax.fori_loop(0, FBLOCKS, unpack, jnp.zeros((SLOTS, LANES), f32), unroll=2)
    mean = jnp.sum(squares, axis=1, keepdims=True) * (1.0 / WIDTH)
    rscale = lax.rsqrt(mean + 1e-06)
    rscale_b = jnp.broadcast_to(rscale, (SLOTS, LANES))

    def scale(k, carry):
        lanes = pl.ds(pl.multiple_of(k * LANES, LANES), LANES)
        normed_ref[:, lanes] = (y_ref[:, lanes] * rscale_b * gain_ref[:, lanes]).astype(bf16)
        return carry

    lax.fori_loop(0, FBLOCKS, scale, 0, unroll=4)
    fetch.wait()

    def project(i, carry):
        lanes = pl.ds(pl.multiple_of(i * 256, 256), 256)
        lanes_up = pl.ds(pl.multiple_of(FF + i * 256, 256), 256)
        gate = dot(normed_ref[...], in_ref[:, lanes])
        up = dot(normed_ref[...], in_ref[:, lanes_up])
        sigmoid = 1.0 / (1.0 + jnp.exp(-gate))
        swish = gate * sigmoid
        hidden_ref[:, lanes] = (swish * up).astype(bf16)
        dhid = dhid_ref[:, lanes]
        dcat_ref[:, lanes] = (dhid * up * sigmoid * (1.0 + gate * (1.0 - sigmoid))).astype(bf16)
        dcat_ref[:, lanes_up] = (dhid * swish).astype(bf16)
        return carry

    lax.fori_loop(0, FF // 256, project, 0)
    first = first_ref[...]
    first2 = jnp.concatenate([first, first], axis=1)

    def back(i, acc):
        at = pl.multiple_of(i * 256, 256)
        lanes = pl.ds(at, 256)
        grad = dot_last(dcat_ref[...], in_ref[lanes, :]) + first2 * grad_ref[:, lanes].astype(f32)
        scaled = grad * gain_ref[:, lanes]
        scaled_ref[:, lanes] = scaled
        product = scaled * y_ref[:, lanes]
        return acc + product[:, :LANES] + product[:, LANES:]

    acc = lax.fori_loop(0, WIDTH // 256, back, jnp.zeros((SLOTS, LANES), f32))
    mean_grad = jnp.sum(acc, axis=1, keepdims=True) * (1.0 / WIDTH)
    pull = jnp.broadcast_to(rscale * rscale * rscale * mean_grad, (SLOTS, LANES))

    def pack(k, carry):
        lanes = pl.ds(pl.multiple_of(k * LANES, LANES), LANES)
        part = rscale_b * scaled_ref[:, lanes] - pull * y_ref[:, lanes]
        msg_ref[pl.ds(pl.multiple_of(k * SLOTS, SLOTS), SLOTS), :] = part.astype(bf16)
        return carry

    lax.fori_loop(0, FBLOCKS, pack, 0, unroll=4)


def expert_out_kernel(
    hidden_ref, normed_ref, weight_ref, first_ref, out_hbm, msg_ref, wide_ref, out_ref, sem
):
    fetch = pltpu.make_async_copy(out_hbm, out_ref, sem)
    fetch.start()
    weight = weight_ref[...]
    weight2 = jnp.concatenate([weight, weight], axis=1)
    first = first_ref[...]
    first2 = jnp.concatenate([first, first], axis=1)
    fetch.wait()

    def matmul(i, carry):
        lanes = pl.ds(pl.multiple_of(i * 256, 256), 256)
        result = dot_last(hidden_ref[...], out_ref[lanes, :])
        result = weight2 * result + first2 * normed_ref[:, lanes].astype(f32)
        for half in range(2):
            part = result[:, half * LANES : (half + 1) * LANES]
            fb = 2 * i + half
            for par in range(2):
                for c in range(CAP):
                    at = (par * CAP + c) * PAIRS
                    wide_ref[
                        pl.ds(par * BLOCK + c * FBLOCKS + fb, PAIRS, stride=2 * BLOCK), :
                    ] = part[at : at + PAIRS]
        return carry

    lax.fori_loop(0, WIDTH // 256, matmul, 0)
    round_rows(msg_ref, wide_ref)


def combine_kernel(ids_ref, rows_ref, out_ref, wide_ref):
    round_rows(wide_ref, rows_ref)
    select = slot_onehot(rank_table(ids_ref[0:1, :], ids_ref[1:2, :], earlier_mask()))

    def step(fb, carry):
        rows = jnp.concatenate(
            [
                wide_ref[pl.ds(c * FBLOCKS + fb, EXPERTS, stride=BLOCK), :].astype(bf16)
                for c in range(CAP)
            ],
            axis=0,
        )
        at = pl.multiple_of(fb * LANES, LANES)
        out_ref[pl.ds(at, LANES), :] = dot_first(rows, select).astype(bf16)
        return carry

    lax.fori_loop(0, FBLOCKS, step, 0, unroll=4)


def slot_sums_kernel(core_ref, rows_ref, rank_ref, own_ref, their_ref, wide_ref):
    round_rows(wide_ref, rows_ref)
    core = core_ref[0]

    def step(jp, carry):
        for par in range(2):
            ranks = rank_ref[pl.ds(pl.multiple_of((2 * jp + par) * CHIPS, CHIPS), CHIPS), :]
            rows = jnp.concatenate(
                [
                    wide_ref[
                        pl.ds(par * BLOCK + c * PAIRS + jp, CHIPS, stride=2 * BLOCK), :
                    ].astype(bf16)
                    for c in range(CAP)
                ],
                axis=0,
            )
            sums = dot_first(rows, slot_onehot(ranks))
            low, high = sums[:HP], sums[HP:]
            lanes = pl.ds(pl.multiple_of((2 * jp + par) * LANES, LANES), LANES)
            own_ref[:, lanes] = jnp.where(core == 0, low, high)
            their_ref[:, lanes] = jnp.where(core == 0, high, low).astype(bf16)
        return carry

    lax.fori_loop(0, PAIRS, step, 0, unroll=2)


def grad_kernel(own_ref, their_ref, read_ref, dt_ref, out_ref, msg_ref):
    def step(k, acc):
        lanes = pl.ds(pl.multiple_of(k * LANES, LANES), LANES)
        grad = (own_ref[:, lanes] + their_ref[:, lanes].astype(f32)).astype(bf16)
        out_ref[:, lanes] = grad
        rows_k = dt_ref[pl.ds(pl.multiple_of(k * 8, 8), 8), :]
        weighted = (grad.astype(f32) * rows_of(rows_k[0:1], rows_k[1:2])).astype(bf16)
        return acc + dot_last(weighted, read_ref[:, lanes])

    acc = lax.fori_loop(0, CHUNKS, step, jnp.zeros((HP, LANES), f32), unroll=4)
    msg_ref[0:HP, :] = acc
    last = dt_ref[(CHUNKS - 1) * 8 : CHUNKS * 8, :]
    msg_ref[HP : HP + 8, :] = jnp.broadcast_to(last[:, LANES - 1 : LANES], (8, LANES))


def backward_kernel(
    m1_ref, m2_ref, m3_ref, m4_ref, rt_ref, grad_ref, write_ref, read_ref, pair_ref, out_ref
):
    def step(i, state):
        k = CHUNKS - 1 - i
        lanes = pl.ds(pl.multiple_of(k * LANES, LANES), LANES)
        rows = rt_ref[pl.ds(pl.multiple_of(k * 8, 8), 8), :]
        grad = grad_ref[:, lanes]
        write = write_ref[:, lanes]
        read = read_ref[:, lanes]
        inside = []
        for h in range(2):
            pair = pair_ref[pl.ds(pl.multiple_of((2 * k + h) * LANES, LANES), LANES), :]
            inside.append(dot_last(grad[h * HEAD : (h + 1) * HEAD, :], pair))
        carried = dot(state.astype(bf16), write) * rows_of(rows[4:5], rows[5:6])
        out_ref[:, lanes] = (jnp.concatenate(inside, axis=0) + carried).astype(bf16)
        scaled = (grad.astype(f32) * rows_of(rows[2:3], rows[3:4])).astype(bf16)
        through = rows_of(
            jnp.broadcast_to(rows[2:3, LANES - 1 : LANES], (1, LANES)),
            jnp.broadcast_to(rows[3:4, LANES - 1 : LANES], (1, LANES)),
        )
        return through * state + dot_last(scaled, read)

    lax.fori_loop(0, CHUNKS, step, chained((m1_ref, m2_ref, m3_ref, m4_ref)), unroll=4)


def sent_along(value, by):
    size = lax.axis_size("ctx")
    pairs = [(i, i + by) for i in range(size) if 0 <= i + by < size]
    return lax.ppermute(value, "ctx", pairs)


def exchanged(rows):
    blocks = rows.reshape(EXPERTS, BLOCK, LANES)
    return lax.all_to_all(blocks, "exp", split_axis=0, concat_axis=0, tiled=True).reshape(
        ROWS, LANES
    )


def exchanged_by_core(rows):
    blocks = rows.reshape(CHIPS, SLOTS, LANES)
    groups = [list(range(core, EXPERTS, 2)) for core in range(2)]
    return lax.all_to_all(
        blocks, "exp", split_axis=0, concat_axis=0, tiled=True, axis_index_groups=groups
    ).reshape(ROWS, LANES)


def from_other_core(value):
    return lax.ppermute(value, "exp", [(i, i ^ 1) for i in range(EXPERTS)])


def per_device(
    features,
    write_vectors,
    read_vectors,
    log_decay,
    doc_lengths,
    expert_ids,
    route_weights,
    norm_gain,
    expert_in,
    expert_out,
    out_grad,
):
    me_ctx = lax.axis_index("ctx")
    me_exp = lax.axis_index("exp")
    wide = pltpu.VMEM((ROWS, LANES), f32)
    ids_own = expert_ids.T.astype(f32)
    tokens_own = jnp.concatenate([ids_own, route_weights.T], axis=0)
    tokens = lax.all_to_all(
        jnp.broadcast_to(tokens_own[None], (EXPERTS, 4, LANES)), "exp", 0, 0, tiled=True
    )
    tokens = tokens.reshape(PAIRS, 2, 4, LANES).transpose(2, 1, 0, 3).reshape(4, CHUNKS, LANES)

    me_core = lax.rem(me_exp, 2).astype(i32).reshape(1)

    their_ids = from_other_core(ids_own)
    their_grad = from_other_core(out_grad)
    (grad_out_rows,) = call(
        grad_rows_kernel,
        [((ROWS, LANES), bf16)],
        (me_core, ids_own, their_ids, out_grad, their_grad),
        [SM] + [VM] * 4,
        [wide],
        flops=2 * SLOTS * LANES * WIDTH,
        moved=4 << 20,
        name="grad_rows",
    )
    grad_in_rows = exchanged_by_core(grad_out_rows)

    weight_in = lax.all_gather(expert_in, "ctx", axis=1, tiled=True)[0]
    weight_out = lax.all_gather(expert_out, "ctx", axis=1, tiled=True)[0]
    rt, dt, message = call(
        tables_kernel,
        [((CHUNKS * 8, LANES), f32), ((CHUNKS * 8, LANES), f32), ((HP + 8, LANES), f32)],
        (
            doc_lengths,
            (me_ctx * SEQ).astype(i32).reshape(1),
            log_decay.reshape(2 * CHUNKS, LANES),
            features,
            write_vectors,
        ),
        [SM, SM, VM, VM, VM],
        flops=2 * HP * LANES * SEQ,
        moved=3 << 20,
        name="shard_state",
    )
    before = [sent_along(message, d) for d in range(1, REACH + 1)]
    y_own, pairs = call(
        forward_kernel,
        [((HP, SEQ), bf16), ((2 * CHUNKS * LANES, LANES), bf16)],
        (*before, rt, features, write_vectors, read_vectors),
        [VM] * 8,
        flops=8 * HP * LANES * SEQ,
        moved=9 << 20,
        name="mixer_forward",
    )
    y_their = from_other_core(y_own)
    y_out_rows, ranks, slot_weight, slot_first = call(
        dispatch_kernel,
        [
            ((ROWS, LANES), bf16),
            ((CHUNKS * CHIPS, LANES), f32),
            ((SLOTS, LANES), f32),
            ((SLOTS, LANES), f32),
        ],
        (me_exp.astype(i32).reshape(1), y_own, y_their, tokens),
        [SM] + [VM] * 3,
        [wide],
        flops=4 * HP * SLOTS * SEQ,
        moved=4 << 20,
        name="dispatch",
    )
    y_in_rows = exchanged_by_core(y_out_rows)

    grad_slots, d_hidden = call(
        arrived_grad_kernel,
        [((SLOTS, WIDTH), bf16), ((SLOTS, FF), f32)],
        (grad_in_rows, slot_weight, weight_out),
        [VM, VM, HBM],
        [wide, pltpu.VMEM((SLOTS, WIDTH), bf16), pltpu.VMEM((WIDTH, FF), bf16), pltpu.SemaphoreType.DMA],
        flops=2 * SLOTS * FF * WIDTH,
        moved=8 << 20,
        name="hidden_grad",
    )
    back_out_rows, normed, hidden = call(
        expert_kernel,
        [
            ((ROWS, LANES), bf16),
            ((SLOTS, WIDTH), bf16),
            ((SLOTS, FF), bf16),
        ],
        (y_in_rows, norm_gain.reshape(1, WIDTH), slot_first, grad_slots, d_hidden, weight_in),
        [VM, VM, VM, VM, VM, HBM],
        [
            pltpu.VMEM((SLOTS, WIDTH), f32),
            pltpu.VMEM((SLOTS, WIDTH), f32),
            pltpu.VMEM((SLOTS, 2 * FF), bf16),
            pltpu.VMEM((WIDTH, 2 * FF), bf16),
            pltpu.SemaphoreType.DMA,
        ],
        flops=8 * SLOTS * FF * WIDTH,
        moved=14 << 20,
        name="expert",
    )
    back_in_rows = exchanged_by_core(back_out_rows)

    (result_rows,) = call(
        expert_out_kernel,
        [((ROWS, LANES), bf16)],
        (hidden, normed, slot_weight, slot_first, weight_out),
        [VM, VM, VM, VM, HBM],
        [wide, pltpu.VMEM((WIDTH, FF), bf16), pltpu.SemaphoreType.DMA],
        flops=2 * SLOTS * FF * WIDTH,
        moved=8 << 20,
        name="expert_out",
    )
    returned_rows = exchanged(result_rows)

    own_sums, their_sums = call(
        slot_sums_kernel,
        [((HP, SEQ), f32), ((HP, SEQ), bf16)],
        (me_core, back_in_rows, ranks),
        [SM, VM, VM],
        [wide],
        flops=4 * HP * SLOTS * SEQ,
        moved=4 << 20,
        name="slot_sums",
    )
    y_grad, back_message = call(
        grad_kernel,
        [((HP, SEQ), bf16), ((HP + 8, LANES), f32)],
        (own_sums, from_other_core(their_sums), read_vectors, dt),
        [VM] * 4,
        flops=8 * HP * LANES * SEQ,
        moved=6 << 20,
        name="mixer_grad",
    )
    after = [sent_along(back_message, -d) for d in range(1, REACH + 1)]
    (input_grad,) = call(
        backward_kernel,
        [((HP, SEQ), bf16)],
        (*after, rt, y_grad, write_vectors, read_vectors, pairs),
        [VM] * 9,
        flops=8 * HP * LANES * SEQ,
        moved=6 << 20,
        name="mixer_backward",
    )
    returned_rows, input_grad = lax.optimization_barrier((returned_rows, input_grad))
    (block_out,) = call(
        combine_kernel,
        [((WIDTH, LANES), bf16)],
        (ids_own, returned_rows),
        [VM, VM],
        [wide],
        flops=2 * SLOTS * LANES * WIDTH,
        moved=4 << 20,
        name="combine",
    )
    return (block_out, input_grad)


def solution(mesh):
    placed = (
        P("exp", "ctx"),
        P(None, "ctx"),
        P(None, "ctx"),
        P("exp", "ctx"),
        P(),
        P(("ctx", "exp"), None),
        P(("ctx", "exp"), None),
        P(),
        P("exp", "ctx", None),
        P("exp", "ctx", None),
        P(None, ("ctx", "exp")),
    )
    return jax.shard_map(
        per_device,
        mesh=mesh,
        in_specs=placed,
        out_specs=(P(None, ("ctx", "exp")), P("exp", "ctx")),
        check_vma=False,
    )
```

```python
import jax
import jax.numpy as jnp
from jax import lax
from jax.experimental import pallas as pl
from jax.experimental.pallas import tpu as pltpu
from jax.sharding import PartitionSpec as P

f32 = jnp.float32
bf16 = jnp.bfloat16
i32 = jnp.int32

LANES = 128
SEQ = 4096
CHUNKS = SEQ // LANES
PAIRS = CHUNKS // 2
HP = 64
HEAD = 32
EXPERTS = 32
CHIPS = 16
CAP = 10
SLOTS = EXPERTS * CAP
BLOCK = CAP * PAIRS
ROWS = EXPERTS * BLOCK
WIDTH = 2048
FF = 768
FBLOCKS = WIDTH // LANES
REACH = 4
EARLY = 14
STEPS = (0, 8, 7, 9, 6, 10, 5, 11, 4, 12, 3, 13, 2, 14, 1, 15)
VMEM = 60 * 1024 * 1024
VMEM_PART = 40 * 1024 * 1024

LAST = (((1,), (1,)), ((), ()))
FIRST = (((0,), (0,)), ((), ()))


def dot(a, b):
    return jnp.dot(a, b, preferred_element_type=f32)


def dot_last(a, b):
    return lax.dot_general(a, b, LAST, preferred_element_type=f32)


def dot_first(a, b):
    return lax.dot_general(a, b, FIRST, preferred_element_type=f32)


def split3(value):
    high = value.astype(bf16)
    rest = value - high.astype(f32)
    middle = rest.astype(bf16)
    low = (rest - middle.astype(f32)).astype(bf16)
    return high, middle, low


def rows_of(first, second):
    return jnp.concatenate(
        [jnp.broadcast_to(first, (HEAD, LANES)), jnp.broadcast_to(second, (HEAD, LANES))], axis=0
    )


def earlier_mask():
    row = lax.broadcasted_iota(i32, (LANES, LANES), 0)
    col = lax.broadcasted_iota(i32, (LANES, LANES), 1)
    return jnp.where(row < col, 1.0, 0.0).astype(bf16)


def rank_table(first_ids, second_ids, earlier, experts=EXPERTS, core=None):
    expert = lax.broadcasted_iota(i32, (experts, LANES), 0)
    if core is not None:
        expert = 2 * expert + core
    expert = expert.astype(f32)
    picked = (expert == first_ids) | (expert == second_ids)
    rank = dot(jnp.where(picked, 1.0, 0.0).astype(bf16), earlier)
    return jnp.where(picked, rank, -1.0)


def slot_onehot(ranks):
    return jnp.concatenate(
        [jnp.where(ranks == float(c), 1.0, 0.0).astype(bf16) for c in range(CAP)], axis=0
    )


def round_rows(dst_ref, src_ref):
    def step(i, carry):
        at = pl.ds(pl.multiple_of(i * BLOCK, BLOCK), BLOCK)
        dst_ref[at, :] = src_ref[at, :].astype(dst_ref.dtype)
        return carry

    lax.fori_loop(0, ROWS // BLOCK, step, 0, unroll=4)


def send_rows(out_refs, wide_ref, chip):
    for d, ref in zip(STEPS, out_refs):
        at = pl.multiple_of(lax.rem(chip + d, CHIPS) * SLOTS, SLOTS)
        ref[...] = wide_ref[pl.ds(at, SLOTS), :].astype(ref.dtype)


def take_rows(wide_ref, in_refs, chip):
    for d, ref in zip(STEPS, in_refs):
        at = pl.multiple_of(lax.rem(chip + CHIPS - d, CHIPS) * SLOTS, SLOTS)
        wide_ref[pl.ds(at, SLOTS), :] = ref[...].astype(wide_ref.dtype)


def call(kernel, outs, args, in_specs, scratch=(), flops=0, moved=0, name=None, vmem=VMEM):
    vm = pl.BlockSpec(memory_space=pltpu.VMEM)
    return pl.pallas_call(
        kernel,
        out_shape=tuple(jax.ShapeDtypeStruct(shape, kind) for shape, kind in outs),
        in_specs=in_specs,
        out_specs=tuple(vm for _ in outs),
        scratch_shapes=list(scratch),
        compiler_params=pltpu.CompilerParams(vmem_limit_bytes=vmem),
        cost_estimate=pl.CostEstimate(flops=flops, bytes_accessed=moved, transcendentals=0),
        name=name,
    )(*args)


VM = pl.BlockSpec(memory_space=pltpu.VMEM)
SM = pl.BlockSpec(memory_space=pltpu.SMEM)
HBM = pl.BlockSpec(memory_space=pl.ANY)


def grad_rows_kernel(expert_ref, own_ids_ref, their_ids_ref, own_ref, their_ref, out_ref, wide_ref):
    core = lax.rem(expert_ref[0], 2)
    earlier = earlier_mask()

    def select_of(ids_ref):
        return slot_onehot(rank_table(ids_ref[0:1, :], ids_ref[1:2, :], earlier, CHIPS, core))

    own_select, their_select = select_of(own_ids_ref), select_of(their_ids_ref)

    def step(fb, carry):
        feats = pl.ds(pl.multiple_of(fb * LANES, LANES), LANES)
        for select, grad_ref, side in (
            (own_select, own_ref, core),
            (their_select, their_ref, 1 - core),
        ):
            rows = dot_last(select, grad_ref[feats, :])
            for c in range(CAP):
                wide_ref[pl.ds(side * BLOCK + c * FBLOCKS + fb, CHIPS, stride=2 * BLOCK), :] = rows[
                    c * CHIPS : (c + 1) * CHIPS
                ]
        return carry

    lax.fori_loop(0, FBLOCKS, step, 0, unroll=4)
    round_rows(out_ref, wide_ref)


def tables_kernel(docs_ref, base_ref, decay_ref, x_ref, write_ref, rt_ref, dt_ref, msg_ref):
    decay = decay_ref[...]
    row_i = lax.broadcasted_iota(i32, (LANES, LANES), 0)
    col_i = lax.broadcasted_iota(i32, (LANES, LANES), 1)
    upto = jnp.where(row_i <= col_i, 1.0, 0.0).astype(bf16)
    cum = sum(dot(part, upto) for part in split3(decay))
    rows = 2 * CHUNKS
    chunk_end = jnp.broadcast_to(cum[:, LANES - 1 : LANES], (rows, LANES))
    row_j = lax.broadcasted_iota(i32, (rows, rows), 0)
    col_j = lax.broadcasted_iota(i32, (rows, rows), 1)
    same_head = (row_j >= CHUNKS) == (col_j >= CHUNKS)
    before = jnp.where(same_head & (col_j < row_j), 1.0, 0.0).astype(bf16)
    after = jnp.where(same_head & (col_j > row_j), 1.0, 0.0).astype(bf16)
    parts = split3(chunk_end)
    prefix = sum(dot(before, part) for part in parts)
    suffix = sum(dot(after, part) for part in parts)
    chunk = lax.broadcasted_iota(i32, (rows, LANES), 0)
    chunk = jnp.where(chunk >= CHUNKS, chunk - CHUNKS, chunk)
    token = lax.broadcasted_iota(i32, (rows, LANES), 1)
    place = chunk * LANES + token
    base = base_ref[0]
    doc_start = jnp.full((rows, LANES), -(1 << 20), i32)
    last_start = jnp.int32(-(1 << 20))
    start = -base
    for j in range(docs_ref.shape[0]):
        doc_start = jnp.where(place >= start, jnp.maximum(doc_start, start), doc_start)
        last_start = jnp.where(start <= SEQ - 1, jnp.maximum(last_start, start), last_start)
        start = start + docs_ref[j]
    inner_start = jnp.maximum(doc_start - chunk * LANES, -1)
    inner_float = inner_start.astype(f32)
    inner_last = jnp.broadcast_to(inner_float[:, LANES - 1 : LANES], (rows, LANES))
    to_end = chunk_end - cum
    entering = jnp.where(inner_start < 0, jnp.exp(cum), 0.0)
    leaving = jnp.where(token.astype(f32) >= inner_last, jnp.exp(to_end), 0.0)
    dev_entering = jnp.where(doc_start < 0, jnp.exp(prefix + cum), 0.0)
    dev_leaving = jnp.where(place >= last_start, jnp.exp(to_end + suffix), 0.0)
    for r, value in enumerate(
        (
            cum[:CHUNKS],
            cum[CHUNKS:],
            entering[:CHUNKS],
            entering[CHUNKS:],
            leaving[:CHUNKS],
            leaving[CHUNKS:],
            inner_float[:CHUNKS],
            inner_float[CHUNKS:],
        )
    ):
        rt_ref[pl.ds(r, CHUNKS, stride=8), :] = value
    zero = jnp.zeros((CHUNKS, LANES), f32)
    for r, value in enumerate(
        (
            dev_entering[:CHUNKS],
            dev_entering[CHUNKS:],
            dev_leaving[:CHUNKS],
            dev_leaving[CHUNKS:],
            zero,
            zero,
            zero,
            zero,
        )
    ):
        dt_ref[pl.ds(r, CHUNKS, stride=8), :] = value

    def step(k, acc):
        lanes = pl.ds(pl.multiple_of(k * LANES, LANES), LANES)
        rows_k = dt_ref[pl.ds(pl.multiple_of(k * 8, 8), 8), :]
        scaled = x_ref[:, lanes].astype(f32) * rows_of(rows_k[2:3], rows_k[3:4])
        return acc + dot_last(scaled.astype(bf16), write_ref[:, lanes])

    acc = lax.fori_loop(0, CHUNKS, step, jnp.zeros((HP, LANES), f32), unroll=4)
    msg_ref[0:HP, :] = acc
    through = jnp.concatenate(
        [
            jnp.broadcast_to(dev_entering[CHUNKS - 1 : CHUNKS, LANES - 1 : LANES], (1, LANES)),
            jnp.broadcast_to(dev_entering[rows - 1 : rows, LANES - 1 : LANES], (1, LANES)),
            jnp.zeros((6, LANES), f32),
        ],
        axis=0,
    )
    msg_ref[HP : HP + 8, :] = through


def chained(refs):
    state = refs[-1][0:HP, :]
    for ref in refs[-2::-1]:
        state = ref[0:HP, :] + rows_of(ref[HP : HP + 1, :], ref[HP + 1 : HP + 2, :]) * state
    return state


def forward_kernel(
    m1_ref, m2_ref, m3_ref, m4_ref, rt_ref, x_ref, write_ref, read_ref, y_ref, pair_ref
):
    row_i = lax.broadcasted_iota(i32, (LANES, LANES), 0)
    col_i = lax.broadcasted_iota(i32, (LANES, LANES), 1)
    causal = row_i <= col_i
    row_f = row_i.astype(f32)

    def step(k, state):
        lanes = pl.ds(pl.multiple_of(k * LANES, LANES), LANES)
        rows = rt_ref[pl.ds(pl.multiple_of(k * 8, 8), 8), :]
        cols = rows.T
        x = x_ref[:, lanes]
        write = write_ref[:, lanes]
        read = read_ref[:, lanes]
        scores = dot_first(write, read)
        valid = causal & (row_f >= rows[6:7, :])
        inside = []
        for h in range(2):
            gap = rows[h : h + 1, :] - cols[:, h : h + 1]
            pair = jnp.where(valid, jnp.exp(gap) * scores, 0.0).astype(bf16)
            pair_ref[pl.ds(pl.multiple_of((2 * k + h) * LANES, LANES), LANES), :] = pair
            inside.append(dot(x[h * HEAD : (h + 1) * HEAD, :], pair))
        carried = dot(state.astype(bf16), read) * rows_of(rows[2:3], rows[3:4])
        y_ref[:, lanes] = (jnp.concatenate(inside, axis=0) + carried).astype(bf16)
        scaled = (x.astype(f32) * rows_of(rows[4:5], rows[5:6])).astype(bf16)
        through = rows_of(
            jnp.broadcast_to(rows[2:3, LANES - 1 : LANES], (1, LANES)),
            jnp.broadcast_to(rows[3:4, LANES - 1 : LANES], (1, LANES)),
        )
        return through * state + dot_last(scaled, write)

    lax.fori_loop(0, CHUNKS, step, chained((m1_ref, m2_ref, m3_ref, m4_ref)), unroll=4)


def dispatch_kernel(expert_ref, own_ref, their_ref, ids_ref, *refs):
    out_refs = refs[:CHIPS]
    rank_ref, weight_ref, first_ref, wide_ref = refs[CHIPS:]
    core = lax.rem(expert_ref[0], 2)
    earlier = earlier_mask()
    mine = expert_ref[0].astype(f32)
    is_first = ids_ref[0] == mine
    is_second = ids_ref[1] == mine
    picked = is_first | is_second
    rank = dot(jnp.where(picked, 1.0, 0.0).astype(bf16), earlier)
    rank = jnp.where(picked, rank, -1.0)
    route = jnp.where(is_first, ids_ref[2], jnp.where(is_second, ids_ref[3], 0.0))
    first = jnp.where(is_first, 1.0, 0.0)
    for c in range(CAP):
        here = rank == float(c)
        route_c = jnp.sum(jnp.where(here, route, 0.0), axis=1, keepdims=True)
        first_c = jnp.sum(jnp.where(here, first, 0.0), axis=1, keepdims=True)
        for par in range(2):
            at = (par * CAP + c) * PAIRS
            part = slice(par * PAIRS, (par + 1) * PAIRS)
            weight_ref[at : at + PAIRS, :] = jnp.broadcast_to(route_c[part], (PAIRS, LANES))
            first_ref[at : at + PAIRS, :] = jnp.broadcast_to(first_c[part], (PAIRS, LANES))

    def step(jp, carry):
        for par in range(2):
            j = par * PAIRS + jp
            table = rank_table(
                ids_ref[0, pl.ds(j, 1), :], ids_ref[1, pl.ds(j, 1), :], earlier, CHIPS, core
            )
            rank_ref[pl.ds(pl.multiple_of((2 * jp + par) * CHIPS, CHIPS), CHIPS), :] = table
            lanes = pl.ds(pl.multiple_of((2 * jp + par) * LANES, LANES), LANES)
            own = own_ref[:, lanes]
            their = their_ref[:, lanes]
            both = jnp.concatenate(
                [jnp.where(core == 0, own, their), jnp.where(core == 0, their, own)], axis=0
            )
            rows = dot_last(slot_onehot(table), both)
            for c in range(CAP):
                at = par * BLOCK + c * PAIRS + jp
                wide_ref[pl.ds(at, CHIPS, stride=2 * BLOCK), :] = rows[c * CHIPS : (c + 1) * CHIPS]
        return carry

    lax.fori_loop(0, PAIRS, step, 0, unroll=2)
    send_rows(out_refs, wide_ref, lax.div(expert_ref[0], 2))


def arrived_grad_kernel(
    rows_ref, weight_ref, out_hbm, grad_ref, dhid_ref, wide_ref, scaled_ref, out_ref, sem
):
    fetch = pltpu.make_async_copy(out_hbm, out_ref, sem)
    fetch.start()
    round_rows(wide_ref, rows_ref)

    def unpack(fb, carry):
        lanes = pl.ds(pl.multiple_of(fb * LANES, LANES), LANES)
        for par in range(2):
            for c in range(CAP):
                at = (par * CAP + c) * PAIRS
                rows = wide_ref[
                    pl.ds(par * BLOCK + c * FBLOCKS + fb, PAIRS, stride=2 * BLOCK), :
                ]
                grad_ref[at : at + PAIRS, lanes] = rows.astype(bf16)
                scaled_ref[at : at + PAIRS, lanes] = (
                    rows * weight_ref[at : at + PAIRS, :]
                ).astype(bf16)
        return carry

    lax.fori_loop(0, FBLOCKS, unpack, 0, unroll=2)
    fetch.wait()

    def matmul(i, carry):
        lanes = pl.ds(pl.multiple_of(i * 256, 256), 256)
        dhid_ref[:, lanes] = dot(scaled_ref[...], out_ref[:, lanes])
        return carry

    lax.fori_loop(0, FF // 256, matmul, 0)


def expert_kernel(expert_ref, *refs):
    rows_refs = refs[:CHIPS]
    gain_ref, first_ref, grad_ref, dhid_ref, in_hbm = refs[CHIPS : CHIPS + 5]
    out_refs = refs[CHIPS + 5 : 2 * CHIPS + 5]
    normed_ref, hidden_ref, y_ref, scaled_ref, dcat_ref, in_ref, sem = refs[2 * CHIPS + 5 :]
    chip = lax.div(expert_ref[0], 2)
    fetch = pltpu.make_async_copy(in_hbm, in_ref, sem)
    fetch.start()
    squares = jnp.zeros((SLOTS, LANES), f32)
    for d, rows_ref in zip(STEPS, rows_refs):
        at = pl.multiple_of(lax.rem(chip + CHIPS - d, CHIPS) * LANES, LANES)
        y = rows_ref[...].astype(f32)
        y_ref[:, pl.ds(at, LANES)] = y
        squares = squares + y * y
    mean = jnp.sum(squares, axis=1, keepdims=True) * (1.0 / WIDTH)
    rscale = lax.rsqrt(mean + 1e-06)
    rscale_b = jnp.broadcast_to(rscale, (SLOTS, LANES))

    def scale(k, carry):
        lanes = pl.ds(pl.multiple_of(k * LANES, LANES), LANES)
        normed_ref[:, lanes] = (y_ref[:, lanes] * rscale_b * gain_ref[:, lanes]).astype(bf16)
        return carry

    lax.fori_loop(0, FBLOCKS, scale, 0, unroll=4)
    fetch.wait()

    def project(i, carry):
        lanes = pl.ds(pl.multiple_of(i * 256, 256), 256)
        lanes_up = pl.ds(pl.multiple_of(FF + i * 256, 256), 256)
        gate = dot(normed_ref[...], in_ref[:, lanes])
        up = dot(normed_ref[...], in_ref[:, lanes_up])
        sigmoid = 1.0 / (1.0 + jnp.exp(-gate))
        swish = gate * sigmoid
        hidden_ref[:, lanes] = (swish * up).astype(bf16)
        dhid = dhid_ref[:, lanes]
        dcat_ref[:, lanes] = (dhid * up * sigmoid * (1.0 + gate * (1.0 - sigmoid))).astype(bf16)
        dcat_ref[:, lanes_up] = (dhid * swish).astype(bf16)
        return carry

    lax.fori_loop(0, FF // 256, project, 0)
    first = first_ref[...]
    first2 = jnp.concatenate([first, first], axis=1)

    def back(i, acc):
        at = pl.multiple_of(i * 256, 256)
        lanes = pl.ds(at, 256)
        grad = dot_last(dcat_ref[...], in_ref[lanes, :]) + first2 * grad_ref[:, lanes].astype(f32)
        scaled = grad * gain_ref[:, lanes]
        scaled_ref[:, lanes] = scaled
        product = scaled * y_ref[:, lanes]
        return acc + product[:, :LANES] + product[:, LANES:]

    acc = lax.fori_loop(0, WIDTH // 256, back, jnp.zeros((SLOTS, LANES), f32))
    mean_grad = jnp.sum(acc, axis=1, keepdims=True) * (1.0 / WIDTH)
    pull = jnp.broadcast_to(rscale * rscale * rscale * mean_grad, (SLOTS, LANES))

    for d, out_ref in zip(STEPS, out_refs):
        lanes = pl.ds(pl.multiple_of(lax.rem(chip + d, CHIPS) * LANES, LANES), LANES)
        part = rscale_b * scaled_ref[:, lanes] - pull * y_ref[:, lanes]
        out_ref[...] = part.astype(bf16)


def expert_out_kernel(
    hidden_ref, normed_ref, weight_ref, first_ref, out_hbm, msg_ref, wide_ref, out_ref, sem
):
    fetch = pltpu.make_async_copy(out_hbm, out_ref, sem)
    fetch.start()
    weight = weight_ref[...]
    weight2 = jnp.concatenate([weight, weight], axis=1)
    first = first_ref[...]
    first2 = jnp.concatenate([first, first], axis=1)
    fetch.wait()

    def matmul(i, carry):
        lanes = pl.ds(pl.multiple_of(i * 256, 256), 256)
        result = dot_last(hidden_ref[...], out_ref[lanes, :])
        result = weight2 * result + first2 * normed_ref[:, lanes].astype(f32)
        for half in range(2):
            part = result[:, half * LANES : (half + 1) * LANES]
            fb = 2 * i + half
            for par in range(2):
                for c in range(CAP):
                    at = (par * CAP + c) * PAIRS
                    wide_ref[
                        pl.ds(par * BLOCK + c * FBLOCKS + fb, PAIRS, stride=2 * BLOCK), :
                    ] = part[at : at + PAIRS]
        return carry

    lax.fori_loop(0, WIDTH // 256, matmul, 0)
    round_rows(msg_ref, wide_ref)


def combine_kernel(ids_ref, rows_ref, out_ref, wide_ref):
    round_rows(wide_ref, rows_ref)
    select = slot_onehot(rank_table(ids_ref[0:1, :], ids_ref[1:2, :], earlier_mask()))

    def step(fb, carry):
        rows = jnp.concatenate(
            [
                wide_ref[pl.ds(c * FBLOCKS + fb, EXPERTS, stride=BLOCK), :].astype(bf16)
                for c in range(CAP)
            ],
            axis=0,
        )
        at = pl.multiple_of(fb * LANES, LANES)
        out_ref[pl.ds(at, LANES), :] = dot_first(rows, select).astype(bf16)
        return carry

    lax.fori_loop(0, FBLOCKS, step, 0, unroll=4)


def slot_sums_kernel(expert_ref, *refs):
    in_refs = refs[:CHIPS]
    rank_ref, own_ref, their_ref, wide_ref = refs[CHIPS:]
    take_rows(wide_ref, in_refs, lax.div(expert_ref[0], 2))
    core = lax.rem(expert_ref[0], 2)

    def step(jp, carry):
        for par in range(2):
            ranks = rank_ref[pl.ds(pl.multiple_of((2 * jp + par) * CHIPS, CHIPS), CHIPS), :]
            rows = jnp.concatenate(
                [
                    wide_ref[
                        pl.ds(par * BLOCK + c * PAIRS + jp, CHIPS, stride=2 * BLOCK), :
                    ].astype(bf16)
                    for c in range(CAP)
                ],
                axis=0,
            )
            sums = dot_first(rows, slot_onehot(ranks))
            low, high = sums[:HP], sums[HP:]
            lanes = pl.ds(pl.multiple_of((2 * jp + par) * LANES, LANES), LANES)
            own_ref[:, lanes] = jnp.where(core == 0, low, high)
            their_ref[:, lanes] = jnp.where(core == 0, high, low).astype(bf16)
        return carry

    lax.fori_loop(0, PAIRS, step, 0, unroll=2)


def grad_kernel(own_ref, their_ref, read_ref, dt_ref, out_ref, msg_ref):
    def step(k, acc):
        lanes = pl.ds(pl.multiple_of(k * LANES, LANES), LANES)
        grad = (own_ref[:, lanes] + their_ref[:, lanes].astype(f32)).astype(bf16)
        out_ref[:, lanes] = grad
        rows_k = dt_ref[pl.ds(pl.multiple_of(k * 8, 8), 8), :]
        weighted = (grad.astype(f32) * rows_of(rows_k[0:1], rows_k[1:2])).astype(bf16)
        return acc + dot_last(weighted, read_ref[:, lanes])

    acc = lax.fori_loop(0, CHUNKS, step, jnp.zeros((HP, LANES), f32), unroll=4)
    msg_ref[0:HP, :] = acc
    last = dt_ref[(CHUNKS - 1) * 8 : CHUNKS * 8, :]
    msg_ref[HP : HP + 8, :] = jnp.broadcast_to(last[:, LANES - 1 : LANES], (8, LANES))


def backward_kernel(
    m1_ref, m2_ref, m3_ref, m4_ref, rt_ref, grad_ref, write_ref, read_ref, pair_ref, out_ref
):
    def step(i, state):
        k = CHUNKS - 1 - i
        lanes = pl.ds(pl.multiple_of(k * LANES, LANES), LANES)
        rows = rt_ref[pl.ds(pl.multiple_of(k * 8, 8), 8), :]
        grad = grad_ref[:, lanes]
        write = write_ref[:, lanes]
        read = read_ref[:, lanes]
        inside = []
        for h in range(2):
            pair = pair_ref[pl.ds(pl.multiple_of((2 * k + h) * LANES, LANES), LANES), :]
            inside.append(dot_last(grad[h * HEAD : (h + 1) * HEAD, :], pair))
        carried = dot(state.astype(bf16), write) * rows_of(rows[4:5], rows[5:6])
        out_ref[:, lanes] = (jnp.concatenate(inside, axis=0) + carried).astype(bf16)
        scaled = (grad.astype(f32) * rows_of(rows[2:3], rows[3:4])).astype(bf16)
        through = rows_of(
            jnp.broadcast_to(rows[2:3, LANES - 1 : LANES], (1, LANES)),
            jnp.broadcast_to(rows[3:4, LANES - 1 : LANES], (1, LANES)),
        )
        return through * state + dot_last(scaled, read)

    lax.fori_loop(0, CHUNKS, step, chained((m1_ref, m2_ref, m3_ref, m4_ref)), unroll=4)


def sent_along(value, by):
    size = lax.axis_size("ctx")
    pairs = [(i, i + by) for i in range(size) if 0 <= i + by < size]
    return lax.ppermute(value, "ctx", pairs)


def exchanged(rows):
    blocks = rows.reshape(EXPERTS, BLOCK, LANES)
    return lax.all_to_all(blocks, "exp", split_axis=0, concat_axis=0, tiled=True).reshape(
        ROWS, LANES
    )


def exchanged_by_core(rows):
    blocks = rows.reshape(CHIPS, SLOTS, LANES)
    groups = [list(range(core, EXPERTS, 2)) for core in range(2)]
    return lax.all_to_all(
        blocks, "exp", split_axis=0, concat_axis=0, tiled=True, axis_index_groups=groups
    ).reshape(ROWS, LANES)


def shifted(blocks):
    moved = [blocks[0]]
    for d, block in zip(STEPS[1:], blocks[1:]):
        pairs = [(i, (i + 2 * d) % EXPERTS) for i in range(EXPERTS)]
        moved.append(lax.ppermute(block, "exp", pairs))
    return moved


def from_other_core(value):
    return lax.ppermute(value, "exp", [(i, i ^ 1) for i in range(EXPERTS)])


def per_device(
    features,
    write_vectors,
    read_vectors,
    log_decay,
    doc_lengths,
    expert_ids,
    route_weights,
    norm_gain,
    expert_in,
    expert_out,
    out_grad,
):
    me_ctx = lax.axis_index("ctx")
    me_exp = lax.axis_index("exp")
    wide = pltpu.VMEM((ROWS, LANES), f32)
    ids_own = expert_ids.T.astype(f32)
    tokens_own = jnp.concatenate([ids_own, route_weights.T], axis=0)
    tokens = lax.all_to_all(
        jnp.broadcast_to(tokens_own[None], (EXPERTS, 4, LANES)), "exp", 0, 0, tiled=True
    )
    tokens = tokens.reshape(PAIRS, 2, 4, LANES).transpose(2, 1, 0, 3).reshape(4, CHUNKS, LANES)

    me = me_exp.astype(i32).reshape(1)
    parts = [((SLOTS, LANES), bf16)] * CHIPS

    their_ids = from_other_core(ids_own)
    their_grad = from_other_core(out_grad)
    (grad_out_rows,) = call(
        grad_rows_kernel,
        [((ROWS, LANES), bf16)],
        (me, ids_own, their_ids, out_grad, their_grad),
        [SM] + [VM] * 4,
        [wide],
        flops=2 * SLOTS * LANES * WIDTH,
        moved=4 << 20,
        name="grad_rows",
    )
    grad_in_rows = exchanged_by_core(grad_out_rows)

    weight_in = lax.all_gather(expert_in, "ctx", axis=1, tiled=True)[0]
    weight_out = lax.all_gather(expert_out, "ctx", axis=1, tiled=True)[0]
    rt, dt, message = call(
        tables_kernel,
        [((CHUNKS * 8, LANES), f32), ((CHUNKS * 8, LANES), f32), ((HP + 8, LANES), f32)],
        (
            doc_lengths,
            (me_ctx * SEQ).astype(i32).reshape(1),
            log_decay.reshape(2 * CHUNKS, LANES),
            features,
            write_vectors,
        ),
        [SM, SM, VM, VM, VM],
        flops=2 * HP * LANES * SEQ,
        moved=3 << 20,
        name="shard_state",
    )
    before = [sent_along(message, d) for d in range(1, REACH + 1)]
    y_own, pairs = call(
        forward_kernel,
        [((HP, SEQ), bf16), ((2 * CHUNKS * LANES, LANES), bf16)],
        (*before, rt, features, write_vectors, read_vectors),
        [VM] * 8,
        flops=8 * HP * LANES * SEQ,
        moved=9 << 20,
        name="mixer_forward",
    )
    y_their = from_other_core(y_own)
    *y_out_rows, ranks, slot_weight, slot_first = call(
        dispatch_kernel,
        [
            *parts,
            ((CHUNKS * CHIPS, LANES), f32),
            ((SLOTS, LANES), f32),
            ((SLOTS, LANES), f32),
        ],
        (me, y_own, y_their, tokens),
        [SM] + [VM] * 3,
        [wide],
        flops=4 * HP * SLOTS * SEQ,
        moved=4 << 20,
        name="dispatch",
    )
    y_in_rows = shifted(y_out_rows)

    grad_slots, d_hidden = call(
        arrived_grad_kernel,
        [((SLOTS, WIDTH), bf16), ((SLOTS, FF), f32)],
        (grad_in_rows, slot_weight, weight_out),
        [VM, VM, HBM],
        [wide, pltpu.VMEM((SLOTS, WIDTH), bf16), pltpu.VMEM((WIDTH, FF), bf16), pltpu.SemaphoreType.DMA],
        flops=2 * SLOTS * FF * WIDTH,
        moved=8 << 20,
        name="hidden_grad",
    )
    *back_out_rows, normed, hidden = call(
        expert_kernel,
        [
            *parts,
            ((SLOTS, WIDTH), bf16),
            ((SLOTS, FF), bf16),
        ],
        (
            me,
            *y_in_rows,
            norm_gain.reshape(1, WIDTH),
            slot_first,
            grad_slots,
            d_hidden,
            weight_in,
        ),
        [SM] + [VM] * (CHIPS + 4) + [HBM],
        [
            pltpu.VMEM((SLOTS, WIDTH), f32),
            pltpu.VMEM((SLOTS, WIDTH), f32),
            pltpu.VMEM((SLOTS, 2 * FF), bf16),
            pltpu.VMEM((WIDTH, 2 * FF), bf16),
            pltpu.SemaphoreType.DMA,
        ],
        flops=8 * SLOTS * FF * WIDTH,
        moved=14 << 20,
        name="expert",
        vmem=VMEM_PART,
    )
    back_in_rows = shifted(back_out_rows)

    (result_rows,) = call(
        expert_out_kernel,
        [((ROWS, LANES), bf16)],
        (hidden, normed, slot_weight, slot_first, weight_out),
        [VM, VM, VM, VM, HBM],
        [wide, pltpu.VMEM((WIDTH, FF), bf16), pltpu.SemaphoreType.DMA],
        flops=2 * SLOTS * FF * WIDTH,
        moved=8 << 20,
        name="expert_out",
    )
    early = slice(1, 1 + EARLY)
    result_rows, *first_in = lax.optimization_barrier(
        (result_rows, *back_in_rows[early])
    )
    back_in_rows[early] = first_in
    returned_rows = exchanged(result_rows)

    own_sums, their_sums = call(
        slot_sums_kernel,
        [((HP, SEQ), f32), ((HP, SEQ), bf16)],
        (me, *back_in_rows, ranks),
        [SM] + [VM] * (CHIPS + 1),
        [wide],
        flops=4 * HP * SLOTS * SEQ,
        moved=4 << 20,
        name="slot_sums",
        vmem=VMEM_PART,
    )
    y_grad, back_message = call(
        grad_kernel,
        [((HP, SEQ), bf16), ((HP + 8, LANES), f32)],
        (own_sums, from_other_core(their_sums), read_vectors, dt),
        [VM] * 4,
        flops=8 * HP * LANES * SEQ,
        moved=6 << 20,
        name="mixer_grad",
    )
    after = [sent_along(back_message, -d) for d in range(1, REACH + 1)]
    (input_grad,) = call(
        backward_kernel,
        [((HP, SEQ), bf16)],
        (*after, rt, y_grad, write_vectors, read_vectors, pairs),
        [VM] * 9,
        flops=8 * HP * LANES * SEQ,
        moved=6 << 20,
        name="mixer_backward",
    )
    returned_rows, input_grad = lax.optimization_barrier((returned_rows, input_grad))
    (block_out,) = call(
        combine_kernel,
        [((WIDTH, LANES), bf16)],
        (ids_own, returned_rows),
        [VM, VM],
        [wide],
        flops=2 * SLOTS * LANES * WIDTH,
        moved=4 << 20,
        name="combine",
    )
    return (block_out, input_grad)


def solution(mesh):
    placed = (
        P("exp", "ctx"),
        P(None, "ctx"),
        P(None, "ctx"),
        P("exp", "ctx"),
        P(),
        P(("ctx", "exp"), None),
        P(("ctx", "exp"), None),
        P(),
        P("exp", "ctx", None),
        P("exp", "ctx", None),
        P(None, ("ctx", "exp")),
    )
    return jax.shard_map(
        per_device,
        mesh=mesh,
        in_specs=placed,
        out_specs=(P(None, ("ctx", "exp")), P("exp", "ctx")),
        check_vma=False,
    )
```

```python
import jax
import jax.numpy as jnp
from jax import lax
from jax.experimental import pallas as pl
from jax.experimental.pallas import tpu as pltpu
from jax.sharding import PartitionSpec as P

f32 = jnp.float32
bf16 = jnp.bfloat16
i32 = jnp.int32

LANES = 128
SEQ = 4096
CHUNKS = SEQ // LANES
PAIRS = CHUNKS // 2
HP = 64
HEAD = 32
EXPERTS = 32
CHIPS = 16
CAP = 10
SLOTS = EXPERTS * CAP
BLOCK = CAP * PAIRS
ROWS = EXPERTS * BLOCK
WIDTH = 2048
FF = 768
FBLOCKS = WIDTH // LANES
REACH = 4
VMEM = 60 * 1024 * 1024
VMEM_PART = 50 * 1024 * 1024

LAST = (((1,), (1,)), ((), ()))
FIRST = (((0,), (0,)), ((), ()))


def dot(a, b):
    return jnp.dot(a, b, preferred_element_type=f32)


def dot_last(a, b):
    return lax.dot_general(a, b, LAST, preferred_element_type=f32)


def dot_first(a, b):
    return lax.dot_general(a, b, FIRST, preferred_element_type=f32)


def split3(value):
    high = value.astype(bf16)
    rest = value - high.astype(f32)
    middle = rest.astype(bf16)
    low = (rest - middle.astype(f32)).astype(bf16)
    return high, middle, low


def rows_of(first, second):
    return jnp.concatenate(
        [jnp.broadcast_to(first, (HEAD, LANES)), jnp.broadcast_to(second, (HEAD, LANES))], axis=0
    )


def earlier_mask():
    row = lax.broadcasted_iota(i32, (LANES, LANES), 0)
    col = lax.broadcasted_iota(i32, (LANES, LANES), 1)
    return jnp.where(row < col, 1.0, 0.0).astype(bf16)


def rank_table(first_ids, second_ids, earlier, experts=EXPERTS, core=None):
    expert = lax.broadcasted_iota(i32, (experts, LANES), 0)
    if core is not None:
        expert = 2 * expert + core
    expert = expert.astype(f32)
    picked = (expert == first_ids) | (expert == second_ids)
    rank = dot(jnp.where(picked, 1.0, 0.0).astype(bf16), earlier)
    return jnp.where(picked, rank, -1.0)


def slot_onehot(ranks):
    return jnp.concatenate(
        [jnp.where(ranks == float(c), 1.0, 0.0).astype(bf16) for c in range(CAP)], axis=0
    )


def round_rows(dst_ref, src_ref):
    def step(i, carry):
        at = pl.ds(pl.multiple_of(i * BLOCK, BLOCK), BLOCK)
        dst_ref[at, :] = src_ref[at, :].astype(dst_ref.dtype)
        return carry

    lax.fori_loop(0, ROWS // BLOCK, step, 0, unroll=4)


def call(kernel, outs, args, in_specs, scratch=(), flops=0, moved=0, name=None, vmem=VMEM, out_specs=None):
    vm = pl.BlockSpec(memory_space=pltpu.VMEM)
    return pl.pallas_call(
        kernel,
        out_shape=tuple(jax.ShapeDtypeStruct(shape, kind) for shape, kind in outs),
        in_specs=in_specs,
        out_specs=out_specs or tuple(vm for _ in outs),
        scratch_shapes=list(scratch),
        compiler_params=pltpu.CompilerParams(vmem_limit_bytes=vmem),
        cost_estimate=pl.CostEstimate(flops=flops, bytes_accessed=moved, transcendentals=0),
        name=name,
    )(*args)


VM = pl.BlockSpec(memory_space=pltpu.VMEM)
SM = pl.BlockSpec(memory_space=pltpu.SMEM)
HBM = pl.BlockSpec(memory_space=pltpu.HBM)


def grad_rows_kernel(core_ref, own_ids_ref, their_ids_ref, own_ref, their_ref, out_ref, wide_ref):
    core = core_ref[0]
    earlier = earlier_mask()

    def select_of(ids_ref):
        return slot_onehot(rank_table(ids_ref[0:1, :], ids_ref[1:2, :], earlier, CHIPS, core))

    own_select, their_select = select_of(own_ids_ref), select_of(their_ids_ref)

    def step(fb, carry):
        feats = pl.ds(pl.multiple_of(fb * LANES, LANES), LANES)
        for select, grad_ref, side in (
            (own_select, own_ref, core),
            (their_select, their_ref, 1 - core),
        ):
            rows = dot_last(select, grad_ref[feats, :])
            for c in range(CAP):
                wide_ref[pl.ds(side * BLOCK + c * FBLOCKS + fb, CHIPS, stride=2 * BLOCK), :] = rows[
                    c * CHIPS : (c + 1) * CHIPS
                ]
        return carry

    lax.fori_loop(0, FBLOCKS, step, 0, unroll=4)
    round_rows(out_ref, wide_ref)


def tables_kernel(docs_ref, base_ref, decay_ref, x_ref, write_ref, rt_ref, dt_ref, msg_ref):
    decay = decay_ref[...]
    row_i = lax.broadcasted_iota(i32, (LANES, LANES), 0)
    col_i = lax.broadcasted_iota(i32, (LANES, LANES), 1)
    upto = jnp.where(row_i <= col_i, 1.0, 0.0).astype(bf16)
    cum = sum(dot(part, upto) for part in split3(decay))
    rows = 2 * CHUNKS
    chunk_end = jnp.broadcast_to(cum[:, LANES - 1 : LANES], (rows, LANES))
    row_j = lax.broadcasted_iota(i32, (rows, rows), 0)
    col_j = lax.broadcasted_iota(i32, (rows, rows), 1)
    same_head = (row_j >= CHUNKS) == (col_j >= CHUNKS)
    before = jnp.where(same_head & (col_j < row_j), 1.0, 0.0).astype(bf16)
    after = jnp.where(same_head & (col_j > row_j), 1.0, 0.0).astype(bf16)
    parts = split3(chunk_end)
    prefix = sum(dot(before, part) for part in parts)
    suffix = sum(dot(after, part) for part in parts)
    chunk = lax.broadcasted_iota(i32, (rows, LANES), 0)
    chunk = jnp.where(chunk >= CHUNKS, chunk - CHUNKS, chunk)
    token = lax.broadcasted_iota(i32, (rows, LANES), 1)
    place = chunk * LANES + token
    base = base_ref[0]
    doc_start = jnp.full((rows, LANES), -(1 << 20), i32)
    last_start = jnp.int32(-(1 << 20))
    start = -base
    for j in range(docs_ref.shape[0]):
        doc_start = jnp.where(place >= start, jnp.maximum(doc_start, start), doc_start)
        last_start = jnp.where(start <= SEQ - 1, jnp.maximum(last_start, start), last_start)
        start = start + docs_ref[j]
    inner_start = jnp.maximum(doc_start - chunk * LANES, -1)
    inner_float = inner_start.astype(f32)
    inner_last = jnp.broadcast_to(inner_float[:, LANES - 1 : LANES], (rows, LANES))
    to_end = chunk_end - cum
    entering = jnp.where(inner_start < 0, jnp.exp(cum), 0.0)
    leaving = jnp.where(token.astype(f32) >= inner_last, jnp.exp(to_end), 0.0)
    dev_entering = jnp.where(doc_start < 0, jnp.exp(prefix + cum), 0.0)
    dev_leaving = jnp.where(place >= last_start, jnp.exp(to_end + suffix), 0.0)
    for r, value in enumerate(
        (
            cum[:CHUNKS],
            cum[CHUNKS:],
            entering[:CHUNKS],
            entering[CHUNKS:],
            leaving[:CHUNKS],
            leaving[CHUNKS:],
            inner_float[:CHUNKS],
            inner_float[CHUNKS:],
        )
    ):
        rt_ref[pl.ds(r, CHUNKS, stride=8), :] = value
    zero = jnp.zeros((CHUNKS, LANES), f32)
    for r, value in enumerate(
        (
            dev_entering[:CHUNKS],
            dev_entering[CHUNKS:],
            dev_leaving[:CHUNKS],
            dev_leaving[CHUNKS:],
            zero,
            zero,
            zero,
            zero,
        )
    ):
        dt_ref[pl.ds(r, CHUNKS, stride=8), :] = value

    def step(k, acc):
        lanes = pl.ds(pl.multiple_of(k * LANES, LANES), LANES)
        rows_k = dt_ref[pl.ds(pl.multiple_of(k * 8, 8), 8), :]
        scaled = x_ref[:, lanes].astype(f32) * rows_of(rows_k[2:3], rows_k[3:4])
        return acc + dot_last(scaled.astype(bf16), write_ref[:, lanes])

    acc = lax.fori_loop(0, CHUNKS, step, jnp.zeros((HP, LANES), f32), unroll=4)
    msg_ref[0:HP, :] = acc
    through = jnp.concatenate(
        [
            jnp.broadcast_to(dev_entering[CHUNKS - 1 : CHUNKS, LANES - 1 : LANES], (1, LANES)),
            jnp.broadcast_to(dev_entering[rows - 1 : rows, LANES - 1 : LANES], (1, LANES)),
            jnp.zeros((6, LANES), f32),
        ],
        axis=0,
    )
    msg_ref[HP : HP + 8, :] = through


def chained(refs):
    state = refs[-1][0:HP, :]
    for ref in refs[-2::-1]:
        state = ref[0:HP, :] + rows_of(ref[HP : HP + 1, :], ref[HP + 1 : HP + 2, :]) * state
    return state


def forward_kernel(
    m1_ref, m2_ref, m3_ref, m4_ref, rt_ref, x_ref, write_ref, read_ref, y_ref, pair_ref
):
    row_i = lax.broadcasted_iota(i32, (LANES, LANES), 0)
    col_i = lax.broadcasted_iota(i32, (LANES, LANES), 1)
    causal = row_i <= col_i
    row_f = row_i.astype(f32)

    def step(k, state):
        lanes = pl.ds(pl.multiple_of(k * LANES, LANES), LANES)
        rows = rt_ref[pl.ds(pl.multiple_of(k * 8, 8), 8), :]
        cols = rows.T
        x = x_ref[:, lanes]
        write = write_ref[:, lanes]
        read = read_ref[:, lanes]
        scores = dot_first(write, read)
        valid = causal & (row_f >= rows[6:7, :])
        inside = []
        for h in range(2):
            gap = rows[h : h + 1, :] - cols[:, h : h + 1]
            pair = jnp.where(valid, jnp.exp(gap) * scores, 0.0).astype(bf16)
            pair_ref[pl.ds(pl.multiple_of((2 * k + h) * LANES, LANES), LANES), :] = pair
            inside.append(dot(x[h * HEAD : (h + 1) * HEAD, :], pair))
        carried = dot(state.astype(bf16), read) * rows_of(rows[2:3], rows[3:4])
        y_ref[:, lanes] = (jnp.concatenate(inside, axis=0) + carried).astype(bf16)
        scaled = (x.astype(f32) * rows_of(rows[4:5], rows[5:6])).astype(bf16)
        through = rows_of(
            jnp.broadcast_to(rows[2:3, LANES - 1 : LANES], (1, LANES)),
            jnp.broadcast_to(rows[3:4, LANES - 1 : LANES], (1, LANES)),
        )
        return through * state + dot_last(scaled, write)

    lax.fori_loop(0, CHUNKS, step, chained((m1_ref, m2_ref, m3_ref, m4_ref)), unroll=4)


def dispatch_kernel(
    expert_ref, own_ref, their_ref, ids_ref, msg_ref, rank_ref, weight_ref, first_ref, wide_ref
):
    core = lax.rem(expert_ref[0], 2)
    earlier = earlier_mask()
    mine = expert_ref[0].astype(f32)
    is_first = ids_ref[0] == mine
    is_second = ids_ref[1] == mine
    picked = is_first | is_second
    rank = dot(jnp.where(picked, 1.0, 0.0).astype(bf16), earlier)
    rank = jnp.where(picked, rank, -1.0)
    route = jnp.where(is_first, ids_ref[2], jnp.where(is_second, ids_ref[3], 0.0))
    first = jnp.where(is_first, 1.0, 0.0)
    for c in range(CAP):
        here = rank == float(c)
        route_c = jnp.sum(jnp.where(here, route, 0.0), axis=1, keepdims=True)
        first_c = jnp.sum(jnp.where(here, first, 0.0), axis=1, keepdims=True)
        for par in range(2):
            at = (par * CAP + c) * PAIRS
            part = slice(par * PAIRS, (par + 1) * PAIRS)
            weight_ref[at : at + PAIRS, :] = jnp.broadcast_to(route_c[part], (PAIRS, LANES))
            first_ref[at : at + PAIRS, :] = jnp.broadcast_to(first_c[part], (PAIRS, LANES))

    def step(jp, carry):
        for par in range(2):
            j = par * PAIRS + jp
            table = rank_table(
                ids_ref[0, pl.ds(j, 1), :], ids_ref[1, pl.ds(j, 1), :], earlier, CHIPS, core
            )
            rank_ref[pl.ds(pl.multiple_of((2 * jp + par) * CHIPS, CHIPS), CHIPS), :] = table
            lanes = pl.ds(pl.multiple_of((2 * jp + par) * LANES, LANES), LANES)
            own = own_ref[:, lanes]
            their = their_ref[:, lanes]
            both = jnp.concatenate(
                [jnp.where(core == 0, own, their), jnp.where(core == 0, their, own)], axis=0
            )
            rows = dot_last(slot_onehot(table), both)
            for c in range(CAP):
                at = par * BLOCK + c * PAIRS + jp
                wide_ref[pl.ds(at, CHIPS, stride=2 * BLOCK), :] = rows[c * CHIPS : (c + 1) * CHIPS]
        return carry

    lax.fori_loop(0, PAIRS, step, 0, unroll=2)
    round_rows(msg_ref, wide_ref)


def arrived_grad_kernel(
    rows_ref, weight_ref, out_hbm, grad_ref, dhid_ref, wide_ref, scaled_ref, out_ref, sem
):
    fetch = pltpu.make_async_copy(out_hbm, out_ref, sem)
    fetch.start()
    round_rows(wide_ref, rows_ref)

    def unpack(fb, carry):
        lanes = pl.ds(pl.multiple_of(fb * LANES, LANES), LANES)
        for par in range(2):
            for c in range(CAP):
                at = (par * CAP + c) * PAIRS
                rows = wide_ref[
                    pl.ds(par * BLOCK + c * FBLOCKS + fb, PAIRS, stride=2 * BLOCK), :
                ]
                grad_ref[at : at + PAIRS, lanes] = rows.astype(bf16)
                scaled_ref[at : at + PAIRS, lanes] = (
                    rows * weight_ref[at : at + PAIRS, :]
                ).astype(bf16)
        return carry

    lax.fori_loop(0, FBLOCKS, unpack, 0, unroll=2)
    fetch.wait()

    def matmul(i, carry):
        lanes = pl.ds(pl.multiple_of(i * 256, 256), 256)
        dhid_ref[:, lanes] = dot(scaled_ref[...], out_ref[:, lanes])
        return carry

    lax.fori_loop(0, FF // 256, matmul, 0)


def expert_kernel(
    rows_ref,
    gain_ref,
    first_hbm,
    grad_hbm,
    dhid_hbm,
    in_hbm,
    msg_hbm,
    normed_hbm,
    hidden_hbm,
    y_ref,
    scaled_ref,
    dcat_ref,
    in_ref,
    first_ref,
    grad_ref,
    dhid_ref,
    normed_ref,
    hidden_ref,
    msg_ref,
    fetch_sems,
    store_sems,
    msg_sems,
):
    fetches = [
        pltpu.make_async_copy(src, dst, fetch_sems.at[i])
        for i, (src, dst) in enumerate(
            (
                (in_hbm, in_ref),
                (dhid_hbm, dhid_ref),
                (grad_hbm, grad_ref),
                (first_hbm, first_ref),
            )
        )
    ]
    for fetch in fetches:
        fetch.start()
    keep_normed = pltpu.make_async_copy(normed_ref, normed_hbm, store_sems.at[0])
    keep_hidden = pltpu.make_async_copy(hidden_ref, hidden_hbm, store_sems.at[1])

    def unpack(k, squares):
        lanes = pl.ds(pl.multiple_of(k * LANES, LANES), LANES)
        y = rows_ref[pl.ds(pl.multiple_of(k * SLOTS, SLOTS), SLOTS), :].astype(f32)
        y_ref[:, lanes] = y
        return squares + y * y

    squares = lax.fori_loop(0, FBLOCKS, unpack, jnp.zeros((SLOTS, LANES), f32), unroll=2)
    mean = jnp.sum(squares, axis=1, keepdims=True) * (1.0 / WIDTH)
    rscale = lax.rsqrt(mean + 1e-06)
    rscale_b = jnp.broadcast_to(rscale, (SLOTS, LANES))

    def scale(k, carry):
        lanes = pl.ds(pl.multiple_of(k * LANES, LANES), LANES)
        normed_ref[:, lanes] = (y_ref[:, lanes] * rscale_b * gain_ref[:, lanes]).astype(bf16)
        return carry

    lax.fori_loop(0, FBLOCKS, scale, 0, unroll=4)
    keep_normed.start()
    fetches[0].wait()
    fetches[1].wait()

    def project(i, carry):
        lanes = pl.ds(pl.multiple_of(i * 256, 256), 256)
        lanes_up = pl.ds(pl.multiple_of(FF + i * 256, 256), 256)
        gate = dot(normed_ref[...], in_ref[:, lanes])
        up = dot(normed_ref[...], in_ref[:, lanes_up])
        sigmoid = 1.0 / (1.0 + jnp.exp(-gate))
        swish = gate * sigmoid
        hidden_ref[:, lanes] = (swish * up).astype(bf16)
        dhid = dhid_ref[:, lanes]
        dcat_ref[:, lanes] = (dhid * up * sigmoid * (1.0 + gate * (1.0 - sigmoid))).astype(bf16)
        dcat_ref[:, lanes_up] = (dhid * swish).astype(bf16)
        return carry

    lax.fori_loop(0, FF // 256, project, 0, unroll=True)
    keep_hidden.start()
    fetches[2].wait()
    fetches[3].wait()
    first = first_ref[...]
    first2 = jnp.concatenate([first, first], axis=1)

    def back(i, acc):
        at = pl.multiple_of(i * 256, 256)
        lanes = pl.ds(at, 256)
        grad = dot_last(dcat_ref[...], in_ref[lanes, :]) + first2 * grad_ref[:, lanes].astype(f32)
        scaled = grad * gain_ref[:, lanes]
        scaled_ref[:, lanes] = scaled
        product = scaled * y_ref[:, lanes]
        return acc + product[:, :LANES] + product[:, LANES:]

    acc = lax.fori_loop(0, WIDTH // 256, back, jnp.zeros((SLOTS, LANES), f32), unroll=2)
    mean_grad = jnp.sum(acc, axis=1, keepdims=True) * (1.0 / WIDTH)
    pull = jnp.broadcast_to(rscale * rscale * rscale * mean_grad, (SLOTS, LANES))

    parts = 4
    sends = []
    for part in range(parts):
        for k in range(part * FBLOCKS // parts, (part + 1) * FBLOCKS // parts):
            lanes = slice(k * LANES, (k + 1) * LANES)
            msg_ref[k * SLOTS : (k + 1) * SLOTS, :] = (
                rscale_b * scaled_ref[:, lanes] - pull * y_ref[:, lanes]
            ).astype(bf16)
        rows = pl.ds(part * (ROWS // parts), ROWS // parts)
        sends.append(
            pltpu.make_async_copy(msg_ref.at[rows, :], msg_hbm.at[rows, :], msg_sems.at[part])
        )
        sends[-1].start()
    for copy in (keep_normed, keep_hidden, *sends):
        copy.wait()


def expert_out_kernel(
    expert_ref,
    hidden_ref,
    normed_ref,
    weight_ref,
    first_ref,
    out_hbm,
    own_ref,
    their_ref,
    wide_ref,
    out_ref,
    sem,
):
    fetch = pltpu.make_async_copy(out_hbm, out_ref, sem)
    fetch.start()
    core = lax.rem(expert_ref[0], 2)
    weight = weight_ref[...]
    weight2 = jnp.concatenate([weight, weight], axis=1)
    first = first_ref[...]
    first2 = jnp.concatenate([first, first], axis=1)
    fetch.wait()

    def matmul(i, carry):
        lanes = pl.ds(pl.multiple_of(i * 256, 256), 256)
        result = dot_last(hidden_ref[...], out_ref[lanes, :])
        result = weight2 * result + first2 * normed_ref[:, lanes].astype(f32)
        for half in range(2):
            part = result[:, half * LANES : (half + 1) * LANES]
            fb = 2 * i + half
            for par in range(2):
                for c in range(CAP):
                    at = (par * CAP + c) * PAIRS
                    wide_ref[
                        pl.ds(par * (ROWS // 2) + c * FBLOCKS + fb, PAIRS, stride=BLOCK), :
                    ] = part[at : at + PAIRS]
        return carry

    lax.fori_loop(0, WIDTH // 256, matmul, 0)
    half_rows = ROWS // 2

    def split(i, carry):
        at = pl.multiple_of(i * BLOCK, BLOCK)
        own_at = pl.multiple_of(core * half_rows + at, BLOCK)
        their_at = pl.multiple_of((1 - core) * half_rows + at, BLOCK)
        own_ref[pl.ds(at, BLOCK), :] = wide_ref[pl.ds(own_at, BLOCK), :].astype(bf16)
        their_ref[pl.ds(at, BLOCK), :] = wide_ref[pl.ds(their_at, BLOCK), :].astype(bf16)
        return carry

    lax.fori_loop(0, CHIPS, split, 0, unroll=2)


def combine_kernel(expert_ref, ids_ref, rows_ref, out_ref, wide_ref):
    round_rows(wide_ref, rows_ref)
    core = lax.rem(expert_ref[0], 2)
    earlier = earlier_mask()
    select = jnp.concatenate(
        [
            slot_onehot(rank_table(ids_ref[0:1, :], ids_ref[1:2, :], earlier, CHIPS, side))
            for side in (core, 1 - core)
        ],
        axis=0,
    )

    def step(fb, carry):
        rows = jnp.concatenate(
            [
                wide_ref[
                    pl.ds(side * BLOCK + c * FBLOCKS + fb, CHIPS, stride=2 * BLOCK), :
                ].astype(bf16)
                for side in range(2)
                for c in range(CAP)
            ],
            axis=0,
        )
        at = pl.multiple_of(fb * LANES, LANES)
        out_ref[pl.ds(at, LANES), :] = dot_first(rows, select).astype(bf16)
        return carry

    lax.fori_loop(0, FBLOCKS, step, 0, unroll=4)


def slot_sums_kernel(core_ref, rows_ref, rank_ref, own_ref, their_ref, wide_ref):
    round_rows(wide_ref, rows_ref)
    core = core_ref[0]

    def step(jp, carry):
        for par in range(2):
            ranks = rank_ref[pl.ds(pl.multiple_of((2 * jp + par) * CHIPS, CHIPS), CHIPS), :]
            rows = jnp.concatenate(
                [
                    wide_ref[
                        pl.ds(par * BLOCK + c * PAIRS + jp, CHIPS, stride=2 * BLOCK), :
                    ].astype(bf16)
                    for c in range(CAP)
                ],
                axis=0,
            )
            sums = dot_first(rows, slot_onehot(ranks))
            low, high = sums[:HP], sums[HP:]
            lanes = pl.ds(pl.multiple_of((2 * jp + par) * LANES, LANES), LANES)
            own_ref[:, lanes] = jnp.where(core == 0, low, high)
            their_ref[:, lanes] = jnp.where(core == 0, high, low).astype(bf16)
        return carry

    lax.fori_loop(0, PAIRS, step, 0, unroll=2)


def grad_kernel(own_ref, their_ref, read_ref, dt_ref, out_ref, msg_ref):
    def step(k, acc):
        lanes = pl.ds(pl.multiple_of(k * LANES, LANES), LANES)
        grad = (own_ref[:, lanes] + their_ref[:, lanes].astype(f32)).astype(bf16)
        out_ref[:, lanes] = grad
        rows_k = dt_ref[pl.ds(pl.multiple_of(k * 8, 8), 8), :]
        weighted = (grad.astype(f32) * rows_of(rows_k[0:1], rows_k[1:2])).astype(bf16)
        return acc + dot_last(weighted, read_ref[:, lanes])

    acc = lax.fori_loop(0, CHUNKS, step, jnp.zeros((HP, LANES), f32), unroll=4)
    msg_ref[0:HP, :] = acc
    last = dt_ref[(CHUNKS - 1) * 8 : CHUNKS * 8, :]
    msg_ref[HP : HP + 8, :] = jnp.broadcast_to(last[:, LANES - 1 : LANES], (8, LANES))


def backward_kernel(
    m1_ref, m2_ref, m3_ref, m4_ref, rt_ref, grad_ref, write_ref, read_ref, pair_ref, out_ref
):
    def step(i, state):
        k = CHUNKS - 1 - i
        lanes = pl.ds(pl.multiple_of(k * LANES, LANES), LANES)
        rows = rt_ref[pl.ds(pl.multiple_of(k * 8, 8), 8), :]
        grad = grad_ref[:, lanes]
        write = write_ref[:, lanes]
        read = read_ref[:, lanes]
        inside = []
        for h in range(2):
            pair = pair_ref[pl.ds(pl.multiple_of((2 * k + h) * LANES, LANES), LANES), :]
            inside.append(dot_last(grad[h * HEAD : (h + 1) * HEAD, :], pair))
        carried = dot(state.astype(bf16), write) * rows_of(rows[4:5], rows[5:6])
        out_ref[:, lanes] = (jnp.concatenate(inside, axis=0) + carried).astype(bf16)
        scaled = (grad.astype(f32) * rows_of(rows[2:3], rows[3:4])).astype(bf16)
        through = rows_of(
            jnp.broadcast_to(rows[2:3, LANES - 1 : LANES], (1, LANES)),
            jnp.broadcast_to(rows[3:4, LANES - 1 : LANES], (1, LANES)),
        )
        return through * state + dot_last(scaled, read)

    lax.fori_loop(0, CHUNKS, step, chained((m1_ref, m2_ref, m3_ref, m4_ref)), unroll=4)


def sent_along(value, by):
    size = lax.axis_size("ctx")
    pairs = [(i, i + by) for i in range(size) if 0 <= i + by < size]
    return lax.ppermute(value, "ctx", pairs)


def exchanged_by_core(rows):
    blocks = rows.reshape(CHIPS, SLOTS, LANES)
    groups = [list(range(core, EXPERTS, 2)) for core in range(2)]
    return lax.all_to_all(
        blocks, "exp", split_axis=0, concat_axis=0, tiled=True, axis_index_groups=groups
    ).reshape(ROWS, LANES)


def from_other_core(value):
    return lax.ppermute(value, "exp", [(i, i ^ 1) for i in range(EXPERTS)])


def per_device(
    features,
    write_vectors,
    read_vectors,
    log_decay,
    doc_lengths,
    expert_ids,
    route_weights,
    norm_gain,
    expert_in,
    expert_out,
    out_grad,
):
    me_ctx = lax.axis_index("ctx")
    me_exp = lax.axis_index("exp")
    wide = pltpu.VMEM((ROWS, LANES), f32)
    ids_own = expert_ids.T.astype(f32)
    tokens_own = jnp.concatenate([ids_own, route_weights.T], axis=0)
    tokens_sent = jnp.broadcast_to(tokens_own[None], (EXPERTS, 4, LANES))
    tokens_sent, expert_in, expert_out, out_grad, ids_own = lax.optimization_barrier(
        (tokens_sent, expert_in, expert_out, out_grad, ids_own)
    )
    tokens = lax.all_to_all(tokens_sent, "exp", 0, 0, tiled=True)
    tokens = tokens.reshape(PAIRS, 2, 4, LANES).transpose(2, 1, 0, 3).reshape(4, CHUNKS, LANES)

    me_core = lax.rem(me_exp, 2).astype(i32).reshape(1)
    me = me_exp.astype(i32).reshape(1)

    their_ids = from_other_core(ids_own)
    their_grad = from_other_core(out_grad)
    (grad_out_rows,) = call(
        grad_rows_kernel,
        [((ROWS, LANES), bf16)],
        (me_core, ids_own, their_ids, out_grad, their_grad),
        [SM] + [VM] * 4,
        [wide],
        flops=2 * SLOTS * LANES * WIDTH,
        moved=4 << 20,
        name="grad_rows",
    )
    grad_in_rows = exchanged_by_core(grad_out_rows)

    weight_in = lax.all_gather(expert_in, "ctx", axis=1, tiled=True)[0]
    weight_out = lax.all_gather(expert_out, "ctx", axis=1, tiled=True)[0]
    rt, dt, message = call(
        tables_kernel,
        [((CHUNKS * 8, LANES), f32), ((CHUNKS * 8, LANES), f32), ((HP + 8, LANES), f32)],
        (
            doc_lengths,
            (me_ctx * SEQ).astype(i32).reshape(1),
            log_decay.reshape(2 * CHUNKS, LANES),
            features,
            write_vectors,
        ),
        [SM, SM, VM, VM, VM],
        flops=2 * HP * LANES * SEQ,
        moved=3 << 20,
        name="shard_state",
    )
    before = [sent_along(message, d) for d in range(1, REACH + 1)]
    y_own, pairs = call(
        forward_kernel,
        [((HP, SEQ), bf16), ((2 * CHUNKS * LANES, LANES), bf16)],
        (*before, rt, features, write_vectors, read_vectors),
        [VM] * 8,
        flops=8 * HP * LANES * SEQ,
        moved=9 << 20,
        name="mixer_forward",
    )
    y_their = from_other_core(y_own)
    y_out_rows, ranks, slot_weight, slot_first = call(
        dispatch_kernel,
        [
            ((ROWS, LANES), bf16),
            ((CHUNKS * CHIPS, LANES), f32),
            ((SLOTS, LANES), f32),
            ((SLOTS, LANES), f32),
        ],
        (me, y_own, y_their, tokens),
        [SM] + [VM] * 3,
        [wide],
        flops=4 * HP * SLOTS * SEQ,
        moved=4 << 20,
        name="dispatch",
    )
    y_in_rows = exchanged_by_core(y_out_rows)

    grad_slots, d_hidden = call(
        arrived_grad_kernel,
        [((SLOTS, WIDTH), bf16), ((SLOTS, FF), f32)],
        (grad_in_rows, slot_weight, weight_out),
        [VM, VM, HBM],
        [wide, pltpu.VMEM((SLOTS, WIDTH), bf16), pltpu.VMEM((WIDTH, FF), bf16), pltpu.SemaphoreType.DMA],
        flops=2 * SLOTS * FF * WIDTH,
        moved=8 << 20,
        name="hidden_grad",
        vmem=VMEM_PART,
    )
    back_out_rows, normed, hidden = call(
        expert_kernel,
        [
            ((ROWS, LANES), bf16),
            ((SLOTS, WIDTH), bf16),
            ((SLOTS, FF), bf16),
        ],
        (y_in_rows, norm_gain.reshape(1, WIDTH), slot_first, grad_slots, d_hidden, weight_in),
        [VM, VM, HBM, HBM, HBM, HBM],
        [
            pltpu.VMEM((SLOTS, WIDTH), f32),
            pltpu.VMEM((SLOTS, WIDTH), f32),
            pltpu.VMEM((SLOTS, 2 * FF), bf16),
            pltpu.VMEM((WIDTH, 2 * FF), bf16),
            pltpu.VMEM((SLOTS, LANES), f32),
            pltpu.VMEM((SLOTS, WIDTH), bf16),
            pltpu.VMEM((SLOTS, FF), f32),
            pltpu.VMEM((SLOTS, WIDTH), bf16),
            pltpu.VMEM((SLOTS, FF), bf16),
            pltpu.VMEM((ROWS, LANES), bf16),
            pltpu.SemaphoreType.DMA((4,)),
            pltpu.SemaphoreType.DMA((2,)),
            pltpu.SemaphoreType.DMA((4,)),
        ],
        flops=8 * SLOTS * FF * WIDTH,
        moved=14 << 20,
        name="expert",
        out_specs=(HBM, HBM, HBM),
    )
    back_in_rows = exchanged_by_core(back_out_rows)

    own_rows, their_rows = call(
        expert_out_kernel,
        [((ROWS // 2, LANES), bf16)] * 2,
        (me, hidden, normed, slot_weight, slot_first, weight_out),
        [SM, VM, VM, VM, VM, HBM],
        [wide, pltpu.VMEM((WIDTH, FF), bf16), pltpu.SemaphoreType.DMA],
        flops=2 * SLOTS * FF * WIDTH,
        moved=8 << 20,
        name="expert_out",
    )
    result_rows = jnp.concatenate(
        [
            rows.reshape(CHIPS, BLOCK, LANES)
            for rows in (own_rows, from_other_core(their_rows))
        ],
        axis=1,
    ).reshape(ROWS, LANES)
    returned_rows = exchanged_by_core(result_rows)

    own_sums, their_sums = call(
        slot_sums_kernel,
        [((HP, SEQ), f32), ((HP, SEQ), bf16)],
        (me_core, back_in_rows, ranks),
        [SM, VM, VM],
        [wide],
        flops=4 * HP * SLOTS * SEQ,
        moved=4 << 20,
        name="slot_sums",
        vmem=VMEM_PART,
    )
    y_grad, back_message = call(
        grad_kernel,
        [((HP, SEQ), bf16), ((HP + 8, LANES), f32)],
        (own_sums, from_other_core(their_sums), read_vectors, dt),
        [VM] * 4,
        flops=8 * HP * LANES * SEQ,
        moved=6 << 20,
        name="mixer_grad",
    )
    after = [sent_along(back_message, -d) for d in range(1, REACH + 1)]
    (input_grad,) = call(
        backward_kernel,
        [((HP, SEQ), bf16)],
        (*after, rt, y_grad, write_vectors, read_vectors, pairs),
        [VM] * 9,
        flops=8 * HP * LANES * SEQ,
        moved=6 << 20,
        name="mixer_backward",
    )
    returned_rows, input_grad = lax.optimization_barrier((returned_rows, input_grad))
    (block_out,) = call(
        combine_kernel,
        [((WIDTH, LANES), bf16)],
        (me, ids_own, returned_rows),
        [SM, VM, VM],
        [wide],
        flops=2 * SLOTS * LANES * WIDTH,
        moved=4 << 20,
        name="combine",
        vmem=VMEM_PART,
    )
    return (block_out, input_grad)


def solution(mesh):
    placed = (
        P("exp", "ctx"),
        P(None, "ctx"),
        P(None, "ctx"),
        P("exp", "ctx"),
        P(),
        P(("ctx", "exp"), None),
        P(("ctx", "exp"), None),
        P(),
        P("exp", "ctx", None),
        P("exp", "ctx", None),
        P(None, ("ctx", "exp")),
    )
    return jax.shard_map(
        per_device,
        mesh=mesh,
        in_specs=placed,
        out_specs=(P(None, ("ctx", "exp")), P("exp", "ctx")),
        check_vma=False,
    )
```

```python
import jax
import jax.numpy as jnp
from jax import lax
from jax.experimental import pallas as pl
from jax.experimental.pallas import tpu as pltpu
from jax.sharding import PartitionSpec as P

f32 = jnp.float32
bf16 = jnp.bfloat16
i32 = jnp.int32

LANES = 128
SEQ = 4096
CHUNKS = SEQ // LANES
PAIRS = CHUNKS // 2
HP = 64
HEAD = 32
EXPERTS = 32
CHIPS = 16
CAP = 10
SLOTS = EXPERTS * CAP
BLOCK = CAP * PAIRS
ROWS = EXPERTS * BLOCK
WIDTH = 2048
FF = 768
FBLOCKS = WIDTH // LANES
REACH = 4
VMEM = 60 * 1024 * 1024
VMEM_PART = 50 * 1024 * 1024

LAST = (((1,), (1,)), ((), ()))
FIRST = (((0,), (0,)), ((), ()))


def dot(a, b):
    return jnp.dot(a, b, preferred_element_type=f32)


def dot_last(a, b):
    return lax.dot_general(a, b, LAST, preferred_element_type=f32)


def dot_first(a, b):
    return lax.dot_general(a, b, FIRST, preferred_element_type=f32)


def split3(value):
    high = value.astype(bf16)
    rest = value - high.astype(f32)
    middle = rest.astype(bf16)
    low = (rest - middle.astype(f32)).astype(bf16)
    return high, middle, low


def rows_of(first, second):
    return jnp.concatenate(
        [jnp.broadcast_to(first, (HEAD, LANES)), jnp.broadcast_to(second, (HEAD, LANES))], axis=0
    )


def earlier_mask():
    row = lax.broadcasted_iota(i32, (LANES, LANES), 0)
    col = lax.broadcasted_iota(i32, (LANES, LANES), 1)
    return jnp.where(row < col, 1.0, 0.0).astype(bf16)


def rank_table(first_ids, second_ids, earlier, experts=EXPERTS, core=None):
    expert = lax.broadcasted_iota(i32, (experts, LANES), 0)
    if core is not None:
        expert = 2 * expert + core
    expert = expert.astype(f32)
    picked = (expert == first_ids) | (expert == second_ids)
    rank = dot(jnp.where(picked, 1.0, 0.0).astype(bf16), earlier)
    return jnp.where(picked, rank, -1.0)


def slot_onehot(ranks):
    return jnp.concatenate(
        [jnp.where(ranks == float(c), 1.0, 0.0).astype(bf16) for c in range(CAP)], axis=0
    )


def round_rows(dst_ref, src_ref):
    def step(i, carry):
        at = pl.ds(pl.multiple_of(i * BLOCK, BLOCK), BLOCK)
        dst_ref[at, :] = src_ref[at, :].astype(dst_ref.dtype)
        return carry

    lax.fori_loop(0, ROWS // BLOCK, step, 0, unroll=4)


def call(kernel, outs, args, in_specs, scratch=(), flops=0, moved=0, name=None, vmem=VMEM, out_specs=None):
    vm = pl.BlockSpec(memory_space=pltpu.VMEM)
    return pl.pallas_call(
        kernel,
        out_shape=tuple(jax.ShapeDtypeStruct(shape, kind) for shape, kind in outs),
        in_specs=in_specs,
        out_specs=out_specs or tuple(vm for _ in outs),
        scratch_shapes=list(scratch),
        compiler_params=pltpu.CompilerParams(vmem_limit_bytes=vmem),
        cost_estimate=pl.CostEstimate(flops=flops, bytes_accessed=moved, transcendentals=0),
        name=name,
    )(*args)


VM = pl.BlockSpec(memory_space=pltpu.VMEM)
SM = pl.BlockSpec(memory_space=pltpu.SMEM)
HBM = pl.BlockSpec(memory_space=pltpu.HBM)


def grad_rows_kernel(core_ref, own_ids_ref, their_ids_ref, own_ref, their_ref, out_ref, wide_ref):
    core = core_ref[0]
    earlier = earlier_mask()

    def select_of(ids_ref):
        return slot_onehot(rank_table(ids_ref[0:1, :], ids_ref[1:2, :], earlier, CHIPS, core))

    own_select, their_select = select_of(own_ids_ref), select_of(their_ids_ref)

    def step(fb, carry):
        feats = pl.ds(pl.multiple_of(fb * LANES, LANES), LANES)
        for select, grad_ref, side in (
            (own_select, own_ref, core),
            (their_select, their_ref, 1 - core),
        ):
            rows = dot_last(select, grad_ref[feats, :])
            for c in range(CAP):
                wide_ref[pl.ds(side * BLOCK + c * FBLOCKS + fb, CHIPS, stride=2 * BLOCK), :] = rows[
                    c * CHIPS : (c + 1) * CHIPS
                ]
        return carry

    lax.fori_loop(0, FBLOCKS, step, 0, unroll=4)
    round_rows(out_ref, wide_ref)


def tables_kernel(docs_ref, base_ref, decay_ref, x_ref, write_ref, rt_ref, dt_ref, msg_ref):
    decay = decay_ref[...]
    row_i = lax.broadcasted_iota(i32, (LANES, LANES), 0)
    col_i = lax.broadcasted_iota(i32, (LANES, LANES), 1)
    upto = jnp.where(row_i <= col_i, 1.0, 0.0).astype(bf16)
    cum = sum(dot(part, upto) for part in split3(decay))
    rows = 2 * CHUNKS
    chunk_end = jnp.broadcast_to(cum[:, LANES - 1 : LANES], (rows, LANES))
    row_j = lax.broadcasted_iota(i32, (rows, rows), 0)
    col_j = lax.broadcasted_iota(i32, (rows, rows), 1)
    same_head = (row_j >= CHUNKS) == (col_j >= CHUNKS)
    before = jnp.where(same_head & (col_j < row_j), 1.0, 0.0).astype(bf16)
    after = jnp.where(same_head & (col_j > row_j), 1.0, 0.0).astype(bf16)
    parts = split3(chunk_end)
    prefix = sum(dot(before, part) for part in parts)
    suffix = sum(dot(after, part) for part in parts)
    chunk = lax.broadcasted_iota(i32, (rows, LANES), 0)
    chunk = jnp.where(chunk >= CHUNKS, chunk - CHUNKS, chunk)
    token = lax.broadcasted_iota(i32, (rows, LANES), 1)
    place = chunk * LANES + token
    base = base_ref[0]
    doc_start = jnp.full((rows, LANES), -(1 << 20), i32)
    last_start = jnp.int32(-(1 << 20))
    start = -base
    for j in range(docs_ref.shape[0]):
        doc_start = jnp.where(place >= start, jnp.maximum(doc_start, start), doc_start)
        last_start = jnp.where(start <= SEQ - 1, jnp.maximum(last_start, start), last_start)
        start = start + docs_ref[j]
    inner_start = jnp.maximum(doc_start - chunk * LANES, -1)
    inner_float = inner_start.astype(f32)
    inner_last = jnp.broadcast_to(inner_float[:, LANES - 1 : LANES], (rows, LANES))
    to_end = chunk_end - cum
    entering = jnp.where(inner_start < 0, jnp.exp(cum), 0.0)
    leaving = jnp.where(token.astype(f32) >= inner_last, jnp.exp(to_end), 0.0)
    dev_entering = jnp.where(doc_start < 0, jnp.exp(prefix + cum), 0.0)
    dev_leaving = jnp.where(place >= last_start, jnp.exp(to_end + suffix), 0.0)
    for r, value in enumerate(
        (
            cum[:CHUNKS],
            cum[CHUNKS:],
            entering[:CHUNKS],
            entering[CHUNKS:],
            leaving[:CHUNKS],
            leaving[CHUNKS:],
            inner_float[:CHUNKS],
            inner_float[CHUNKS:],
        )
    ):
        rt_ref[pl.ds(r, CHUNKS, stride=8), :] = value
    zero = jnp.zeros((CHUNKS, LANES), f32)
    for r, value in enumerate(
        (
            dev_entering[:CHUNKS],
            dev_entering[CHUNKS:],
            dev_leaving[:CHUNKS],
            dev_leaving[CHUNKS:],
            zero,
            zero,
            zero,
            zero,
        )
    ):
        dt_ref[pl.ds(r, CHUNKS, stride=8), :] = value

    def step(k, acc):
        lanes = pl.ds(pl.multiple_of(k * LANES, LANES), LANES)
        rows_k = dt_ref[pl.ds(pl.multiple_of(k * 8, 8), 8), :]
        scaled = x_ref[:, lanes].astype(f32) * rows_of(rows_k[2:3], rows_k[3:4])
        return acc + dot_last(scaled.astype(bf16), write_ref[:, lanes])

    acc = lax.fori_loop(0, CHUNKS, step, jnp.zeros((HP, LANES), f32), unroll=4)
    msg_ref[0:HP, :] = acc
    through = jnp.concatenate(
        [
            jnp.broadcast_to(dev_entering[CHUNKS - 1 : CHUNKS, LANES - 1 : LANES], (1, LANES)),
            jnp.broadcast_to(dev_entering[rows - 1 : rows, LANES - 1 : LANES], (1, LANES)),
            jnp.zeros((6, LANES), f32),
        ],
        axis=0,
    )
    msg_ref[HP : HP + 8, :] = through


def chained(refs):
    state = refs[-1][0:HP, :]
    for ref in refs[-2::-1]:
        state = ref[0:HP, :] + rows_of(ref[HP : HP + 1, :], ref[HP + 1 : HP + 2, :]) * state
    return state


def forward_kernel(
    m1_ref, m2_ref, m3_ref, m4_ref, rt_ref, x_ref, write_ref, read_ref, y_ref, pair_ref
):
    row_i = lax.broadcasted_iota(i32, (LANES, LANES), 0)
    col_i = lax.broadcasted_iota(i32, (LANES, LANES), 1)
    causal = row_i <= col_i
    row_f = row_i.astype(f32)

    def step(k, state):
        lanes = pl.ds(pl.multiple_of(k * LANES, LANES), LANES)
        rows = rt_ref[pl.ds(pl.multiple_of(k * 8, 8), 8), :]
        cols = rows.T
        x = x_ref[:, lanes]
        write = write_ref[:, lanes]
        read = read_ref[:, lanes]
        scores = dot_first(write, read)
        valid = causal & (row_f >= rows[6:7, :])
        inside = []
        for h in range(2):
            gap = rows[h : h + 1, :] - cols[:, h : h + 1]
            pair = jnp.where(valid, jnp.exp(gap) * scores, 0.0).astype(bf16)
            pair_ref[pl.ds(pl.multiple_of((2 * k + h) * LANES, LANES), LANES), :] = pair
            inside.append(dot(x[h * HEAD : (h + 1) * HEAD, :], pair))
        carried = dot(state.astype(bf16), read) * rows_of(rows[2:3], rows[3:4])
        y_ref[:, lanes] = (jnp.concatenate(inside, axis=0) + carried).astype(bf16)
        scaled = (x.astype(f32) * rows_of(rows[4:5], rows[5:6])).astype(bf16)
        through = rows_of(
            jnp.broadcast_to(rows[2:3, LANES - 1 : LANES], (1, LANES)),
            jnp.broadcast_to(rows[3:4, LANES - 1 : LANES], (1, LANES)),
        )
        return through * state + dot_last(scaled, write)

    lax.fori_loop(0, CHUNKS, step, chained((m1_ref, m2_ref, m3_ref, m4_ref)), unroll=4)


def dispatch_kernel(
    expert_ref, own_ref, their_ref, ids_ref, msg_ref, rank_ref, weight_ref, first_ref, wide_ref
):
    core = lax.rem(expert_ref[0], 2)
    earlier = earlier_mask()
    mine = expert_ref[0].astype(f32)
    is_first = ids_ref[0] == mine
    is_second = ids_ref[1] == mine
    picked = is_first | is_second
    rank = dot(jnp.where(picked, 1.0, 0.0).astype(bf16), earlier)
    rank = jnp.where(picked, rank, -1.0)
    route = jnp.where(is_first, ids_ref[2], jnp.where(is_second, ids_ref[3], 0.0))
    first = jnp.where(is_first, 1.0, 0.0)
    for c in range(CAP):
        here = rank == float(c)
        route_c = jnp.sum(jnp.where(here, route, 0.0), axis=1, keepdims=True)
        first_c = jnp.sum(jnp.where(here, first, 0.0), axis=1, keepdims=True)
        for par in range(2):
            at = (par * CAP + c) * PAIRS
            part = slice(par * PAIRS, (par + 1) * PAIRS)
            weight_ref[at : at + PAIRS, :] = jnp.broadcast_to(route_c[part], (PAIRS, LANES))
            first_ref[at : at + PAIRS, :] = jnp.broadcast_to(first_c[part], (PAIRS, LANES))

    def step(jp, carry):
        for par in range(2):
            j = par * PAIRS + jp
            table = rank_table(
                ids_ref[0, pl.ds(j, 1), :], ids_ref[1, pl.ds(j, 1), :], earlier, CHIPS, core
            )
            rank_ref[pl.ds(pl.multiple_of((2 * jp + par) * CHIPS, CHIPS), CHIPS), :] = table
            lanes = pl.ds(pl.multiple_of((2 * jp + par) * LANES, LANES), LANES)
            own = own_ref[:, lanes]
            their = their_ref[:, lanes]
            both = jnp.concatenate(
                [jnp.where(core == 0, own, their), jnp.where(core == 0, their, own)], axis=0
            )
            rows = dot_last(slot_onehot(table), both)
            for c in range(CAP):
                at = par * BLOCK + c * PAIRS + jp
                wide_ref[pl.ds(at, CHIPS, stride=2 * BLOCK), :] = rows[c * CHIPS : (c + 1) * CHIPS]
        return carry

    lax.fori_loop(0, PAIRS, step, 0, unroll=2)
    round_rows(msg_ref, wide_ref)


def arrived_grad_kernel(
    rows_ref, weight_ref, out_hbm, grad_ref, dhid_ref, wide_ref, scaled_ref, out_ref, sem
):
    fetch = pltpu.make_async_copy(out_hbm, out_ref, sem)
    fetch.start()
    round_rows(wide_ref, rows_ref)

    def unpack(fb, carry):
        lanes = pl.ds(pl.multiple_of(fb * LANES, LANES), LANES)
        for par in range(2):
            for c in range(CAP):
                at = (par * CAP + c) * PAIRS
                rows = wide_ref[
                    pl.ds(par * BLOCK + c * FBLOCKS + fb, PAIRS, stride=2 * BLOCK), :
                ]
                grad_ref[at : at + PAIRS, lanes] = rows.astype(bf16)
                scaled_ref[at : at + PAIRS, lanes] = (
                    rows * weight_ref[at : at + PAIRS, :]
                ).astype(bf16)
        return carry

    lax.fori_loop(0, FBLOCKS, unpack, 0, unroll=2)
    fetch.wait()

    def matmul(i, carry):
        lanes = pl.ds(pl.multiple_of(i * 256, 256), 256)
        dhid_ref[:, lanes] = dot(scaled_ref[...], out_ref[:, lanes])
        return carry

    lax.fori_loop(0, FF // 256, matmul, 0)


EXPERT_SPECS = [VM, VM, HBM, HBM, HBM, HBM]
EXPERT_SCRATCH = [
    pltpu.VMEM((SLOTS, WIDTH), f32),
    pltpu.VMEM((SLOTS, WIDTH), f32),
    pltpu.VMEM((SLOTS, 2 * FF), bf16),
    pltpu.VMEM((WIDTH, 2 * FF), bf16),
    pltpu.VMEM((SLOTS, LANES), f32),
    pltpu.VMEM((SLOTS, WIDTH), bf16),
    pltpu.VMEM((SLOTS, FF), f32),
    pltpu.VMEM((SLOTS, WIDTH), bf16),
    pltpu.VMEM((SLOTS, FF), bf16),
    pltpu.VMEM((ROWS, LANES), bf16),
    pltpu.SemaphoreType.DMA((4,)),
    pltpu.SemaphoreType.DMA,
    pltpu.SemaphoreType.DMA((4,)),
]


def expert_kernel(
    rows_ref,
    gain_ref,
    first_hbm,
    grad_hbm,
    dhid_hbm,
    in_hbm,
    msg_hbm,
    hidden_hbm,
    rscale_out_ref,
    y_ref,
    scaled_ref,
    dcat_ref,
    in_ref,
    first_ref,
    grad_ref,
    dhid_ref,
    gained_ref,
    hidden_ref,
    msg_ref,
    fetch_sems,
    store_sem,
    msg_sems,
):
    fetches = [
        pltpu.make_async_copy(src, dst, fetch_sems.at[i])
        for i, (src, dst) in enumerate(
            (
                (in_hbm, in_ref),
                (dhid_hbm, dhid_ref),
                (grad_hbm, grad_ref),
                (first_hbm, first_ref),
            )
        )
    ]
    for fetch in fetches:
        fetch.start()
    keep_hidden = pltpu.make_async_copy(hidden_ref, hidden_hbm, store_sem)

    def unpack(k, squares):
        lanes = pl.ds(pl.multiple_of(k * LANES, LANES), LANES)
        y = rows_ref[pl.ds(pl.multiple_of(k * SLOTS, SLOTS), SLOTS), :].astype(f32)
        y_ref[:, lanes] = y
        gained_ref[:, lanes] = (y * gain_ref[:, lanes]).astype(bf16)
        return squares + y * y

    squares = lax.fori_loop(0, FBLOCKS, unpack, jnp.zeros((SLOTS, LANES), f32), unroll=2)
    mean = jnp.sum(squares, axis=1, keepdims=True) * (1.0 / WIDTH)
    rscale = lax.rsqrt(mean + 1e-06)
    rscale_b = jnp.broadcast_to(rscale, (SLOTS, LANES))

    rscale_out_ref[...] = rscale_b
    rscale2 = jnp.concatenate([rscale_b, rscale_b], axis=1)
    fetches[0].wait()
    fetches[1].wait()

    def project(i, carry):
        lanes = pl.ds(pl.multiple_of(i * 256, 256), 256)
        lanes_up = pl.ds(pl.multiple_of(FF + i * 256, 256), 256)
        gate = rscale2 * dot(gained_ref[...], in_ref[:, lanes])
        up = rscale2 * dot(gained_ref[...], in_ref[:, lanes_up])
        sigmoid = 1.0 / (1.0 + jnp.exp(-gate))
        swish = gate * sigmoid
        hidden_ref[:, lanes] = (swish * up).astype(bf16)
        dhid = dhid_ref[:, lanes]
        dcat_ref[:, lanes] = (dhid * up * sigmoid * (1.0 + gate * (1.0 - sigmoid))).astype(bf16)
        dcat_ref[:, lanes_up] = (dhid * swish).astype(bf16)
        return carry

    lax.fori_loop(0, FF // 256, project, 0, unroll=True)
    keep_hidden.start()
    fetches[2].wait()
    fetches[3].wait()
    first = first_ref[...]
    first2 = jnp.concatenate([first, first], axis=1)

    def back(i, acc):
        at = pl.multiple_of(i * 256, 256)
        lanes = pl.ds(at, 256)
        grad = dot_last(dcat_ref[...], in_ref[lanes, :]) + first2 * grad_ref[:, lanes].astype(f32)
        scaled = grad * gain_ref[:, lanes]
        scaled_ref[:, lanes] = scaled
        product = scaled * y_ref[:, lanes]
        return acc + product[:, :LANES] + product[:, LANES:]

    acc = lax.fori_loop(0, WIDTH // 256, back, jnp.zeros((SLOTS, LANES), f32), unroll=8)
    mean_grad = jnp.sum(acc, axis=1, keepdims=True) * (1.0 / WIDTH)
    pull = jnp.broadcast_to(rscale * rscale * rscale * mean_grad, (SLOTS, LANES))

    parts = 4
    sends = []
    for part in range(parts):
        for k in range(part * FBLOCKS // parts, (part + 1) * FBLOCKS // parts):
            lanes = slice(k * LANES, (k + 1) * LANES)
            msg_ref[k * SLOTS : (k + 1) * SLOTS, :] = (
                rscale_b * scaled_ref[:, lanes] - pull * y_ref[:, lanes]
            ).astype(bf16)
        rows = pl.ds(part * (ROWS // parts), ROWS // parts)
        sends.append(
            pltpu.make_async_copy(msg_ref.at[rows, :], msg_hbm.at[rows, :], msg_sems.at[part])
        )
        sends[-1].start()
    for copy in (keep_hidden, *sends):
        copy.wait()


def expert_out_kernel(
    expert_ref,
    hidden_ref,
    rows_ref,
    rscale_ref,
    gain_ref,
    weight_ref,
    first_ref,
    out_hbm,
    own_ref,
    their_ref,
    wide_ref,
    out_ref,
    sem,
):
    fetch = pltpu.make_async_copy(out_hbm, out_ref, sem)
    fetch.start()
    core = lax.rem(expert_ref[0], 2)
    weight = weight_ref[...]
    weight2 = jnp.concatenate([weight, weight], axis=1)
    first = first_ref[...] * rscale_ref[...]
    fetch.wait()

    def matmul(i, carry):
        lanes = pl.ds(pl.multiple_of(i * 256, 256), 256)
        result = dot_last(hidden_ref[...], out_ref[lanes, :])
        result = weight2 * result
        for half in range(2):
            fb = 2 * i + half
            y = rows_ref[pl.ds(pl.multiple_of(fb * SLOTS, SLOTS), SLOTS), :].astype(f32)
            gain = gain_ref[:, pl.ds(pl.multiple_of(fb * LANES, LANES), LANES)]
            part = result[:, half * LANES : (half + 1) * LANES] + first * (y * gain)
            for par in range(2):
                for c in range(CAP):
                    at = (par * CAP + c) * PAIRS
                    wide_ref[
                        pl.ds(par * (ROWS // 2) + c * FBLOCKS + fb, PAIRS, stride=BLOCK), :
                    ] = part[at : at + PAIRS]
        return carry

    lax.fori_loop(0, WIDTH // 256, matmul, 0)
    half_rows = ROWS // 2

    def split(i, carry):
        at = pl.multiple_of(i * BLOCK, BLOCK)
        own_at = pl.multiple_of(core * half_rows + at, BLOCK)
        their_at = pl.multiple_of((1 - core) * half_rows + at, BLOCK)
        own_ref[pl.ds(at, BLOCK), :] = wide_ref[pl.ds(own_at, BLOCK), :].astype(bf16)
        their_ref[pl.ds(at, BLOCK), :] = wide_ref[pl.ds(their_at, BLOCK), :].astype(bf16)
        return carry

    lax.fori_loop(0, CHIPS, split, 0, unroll=2)


def combine_kernel(expert_ref, ids_ref, rows_ref, out_ref, wide_ref):
    round_rows(wide_ref, rows_ref)
    core = lax.rem(expert_ref[0], 2)
    earlier = earlier_mask()
    select = jnp.concatenate(
        [
            slot_onehot(rank_table(ids_ref[0:1, :], ids_ref[1:2, :], earlier, CHIPS, side))
            for side in (core, 1 - core)
        ],
        axis=0,
    )

    def step(fb, carry):
        rows = jnp.concatenate(
            [
                wide_ref[
                    pl.ds(side * BLOCK + c * FBLOCKS + fb, CHIPS, stride=2 * BLOCK), :
                ].astype(bf16)
                for side in range(2)
                for c in range(CAP)
            ],
            axis=0,
        )
        at = pl.multiple_of(fb * LANES, LANES)
        out_ref[pl.ds(at, LANES), :] = dot_first(rows, select).astype(bf16)
        return carry

    lax.fori_loop(0, FBLOCKS, step, 0, unroll=8)


def slot_sums_kernel(core_ref, rows_ref, rank_ref, own_ref, their_ref, wide_ref):
    round_rows(wide_ref, rows_ref)
    core = core_ref[0]

    def step(jp, carry):
        for par in range(2):
            ranks = rank_ref[pl.ds(pl.multiple_of((2 * jp + par) * CHIPS, CHIPS), CHIPS), :]
            rows = jnp.concatenate(
                [
                    wide_ref[
                        pl.ds(par * BLOCK + c * PAIRS + jp, CHIPS, stride=2 * BLOCK), :
                    ].astype(bf16)
                    for c in range(CAP)
                ],
                axis=0,
            )
            sums = dot_first(rows, slot_onehot(ranks))
            low, high = sums[:HP], sums[HP:]
            lanes = pl.ds(pl.multiple_of((2 * jp + par) * LANES, LANES), LANES)
            own_ref[:, lanes] = jnp.where(core == 0, low, high)
            their_ref[:, lanes] = jnp.where(core == 0, high, low).astype(bf16)
        return carry

    lax.fori_loop(0, PAIRS, step, 0, unroll=2)


def grad_kernel(own_ref, their_ref, read_ref, dt_ref, out_ref, msg_ref):
    def step(k, acc):
        lanes = pl.ds(pl.multiple_of(k * LANES, LANES), LANES)
        grad = (own_ref[:, lanes] + their_ref[:, lanes].astype(f32)).astype(bf16)
        out_ref[:, lanes] = grad
        rows_k = dt_ref[pl.ds(pl.multiple_of(k * 8, 8), 8), :]
        weighted = (grad.astype(f32) * rows_of(rows_k[0:1], rows_k[1:2])).astype(bf16)
        return acc + dot_last(weighted, read_ref[:, lanes])

    acc = lax.fori_loop(0, CHUNKS, step, jnp.zeros((HP, LANES), f32), unroll=4)
    msg_ref[0:HP, :] = acc
    last = dt_ref[(CHUNKS - 1) * 8 : CHUNKS * 8, :]
    msg_ref[HP : HP + 8, :] = jnp.broadcast_to(last[:, LANES - 1 : LANES], (8, LANES))


def backward_kernel(
    m1_ref, m2_ref, m3_ref, m4_ref, rt_ref, grad_ref, write_ref, read_ref, pair_ref, out_ref
):
    def step(i, state):
        k = CHUNKS - 1 - i
        lanes = pl.ds(pl.multiple_of(k * LANES, LANES), LANES)
        rows = rt_ref[pl.ds(pl.multiple_of(k * 8, 8), 8), :]
        grad = grad_ref[:, lanes]
        write = write_ref[:, lanes]
        read = read_ref[:, lanes]
        inside = []
        for h in range(2):
            pair = pair_ref[pl.ds(pl.multiple_of((2 * k + h) * LANES, LANES), LANES), :]
            inside.append(dot_last(grad[h * HEAD : (h + 1) * HEAD, :], pair))
        carried = dot(state.astype(bf16), write) * rows_of(rows[4:5], rows[5:6])
        out_ref[:, lanes] = (jnp.concatenate(inside, axis=0) + carried).astype(bf16)
        scaled = (grad.astype(f32) * rows_of(rows[2:3], rows[3:4])).astype(bf16)
        through = rows_of(
            jnp.broadcast_to(rows[2:3, LANES - 1 : LANES], (1, LANES)),
            jnp.broadcast_to(rows[3:4, LANES - 1 : LANES], (1, LANES)),
        )
        return through * state + dot_last(scaled, read)

    lax.fori_loop(0, CHUNKS, step, chained((m1_ref, m2_ref, m3_ref, m4_ref)), unroll=4)


def sent_along(value, by):
    size = lax.axis_size("ctx")
    pairs = [(i, i + by) for i in range(size) if 0 <= i + by < size]
    return lax.ppermute(value, "ctx", pairs)


def exchanged_by_core(rows):
    blocks = rows.reshape(CHIPS, SLOTS, LANES)
    groups = [list(range(core, EXPERTS, 2)) for core in range(2)]
    return lax.all_to_all(
        blocks, "exp", split_axis=0, concat_axis=0, tiled=True, axis_index_groups=groups
    ).reshape(ROWS, LANES)


def from_other_core(value):
    return lax.ppermute(value, "exp", [(i, i ^ 1) for i in range(EXPERTS)])


def per_device(
    features,
    write_vectors,
    read_vectors,
    log_decay,
    doc_lengths,
    expert_ids,
    route_weights,
    norm_gain,
    expert_in,
    expert_out,
    out_grad,
):
    me_ctx = lax.axis_index("ctx")
    me_exp = lax.axis_index("exp")
    wide = pltpu.VMEM((ROWS + SLOTS, LANES), f32)
    ids_own = expert_ids.T.astype(f32)
    tokens_sent = jnp.concatenate(
        [
            jnp.broadcast_to(ids_own[None], (EXPERTS, 2, LANES)),
            jnp.broadcast_to(route_weights.T[None], (EXPERTS, 2, LANES)),
        ],
        axis=1,
    )
    tokens_sent, expert_in, expert_out, out_grad, ids_own = lax.optimization_barrier(
        (tokens_sent, expert_in, expert_out, out_grad, ids_own)
    )
    tokens = lax.all_to_all(tokens_sent, "exp", 0, 0, tiled=True)
    tokens = tokens.reshape(PAIRS, 2, 4, LANES).transpose(2, 1, 0, 3).reshape(4, CHUNKS, LANES)

    me_core = lax.rem(me_exp, 2).astype(i32).reshape(1)
    me = me_exp.astype(i32).reshape(1)

    their_ids = from_other_core(ids_own)
    their_grad = from_other_core(out_grad)
    (grad_out_rows,) = call(
        grad_rows_kernel,
        [((ROWS, LANES), bf16)],
        (me_core, ids_own, their_ids, out_grad, their_grad),
        [SM] + [VM] * 4,
        [wide],
        flops=2 * SLOTS * LANES * WIDTH,
        moved=4 << 20,
        name="grad_rows",
    )
    grad_in_rows = exchanged_by_core(grad_out_rows)

    weight_in = lax.all_gather(expert_in, "ctx", axis=1, tiled=True)[0]
    weight_out = lax.all_gather(expert_out, "ctx", axis=1, tiled=True)[0]
    rt, dt, message = call(
        tables_kernel,
        [((CHUNKS * 8 + 8, LANES), f32), ((CHUNKS * 8 + 8, LANES), f32), ((HP + 8, LANES), f32)],
        (
            doc_lengths,
            (me_ctx * SEQ).astype(i32).reshape(1),
            log_decay.reshape(2 * CHUNKS, LANES),
            features,
            write_vectors,
        ),
        [SM, SM, VM, VM, VM],
        flops=2 * HP * LANES * SEQ,
        moved=3 << 20,
        name="shard_state",
    )
    before = [sent_along(message, d) for d in range(1, REACH + 1)]
    y_own, pairs = call(
        forward_kernel,
        [((HP, SEQ), bf16), ((2 * CHUNKS * LANES, LANES), bf16)],
        (*before, rt, features, write_vectors, read_vectors),
        [VM] * 8,
        flops=8 * HP * LANES * SEQ,
        moved=9 << 20,
        name="mixer_forward",
    )
    y_their = from_other_core(y_own)
    y_out_rows, ranks, slot_weight, slot_first = call(
        dispatch_kernel,
        [
            ((ROWS, LANES), bf16),
            ((CHUNKS * CHIPS, LANES), f32),
            ((SLOTS, LANES), f32),
            ((SLOTS, LANES), f32),
        ],
        (me, y_own, y_their, tokens),
        [SM] + [VM] * 3,
        [wide],
        flops=4 * HP * SLOTS * SEQ,
        moved=4 << 20,
        name="dispatch",
    )
    y_in_rows = exchanged_by_core(y_out_rows)

    grad_slots, d_hidden = call(
        arrived_grad_kernel,
        [((SLOTS, WIDTH), bf16), ((SLOTS, FF), f32)],
        (grad_in_rows, slot_weight, weight_out),
        [VM, VM, HBM],
        [wide, pltpu.VMEM((SLOTS, WIDTH), bf16), pltpu.VMEM((WIDTH, FF), bf16), pltpu.SemaphoreType.DMA],
        flops=2 * SLOTS * FF * WIDTH,
        moved=8 << 20,
        name="hidden_grad",
        vmem=VMEM_PART,
    )
    back_out_rows, hidden, rscale = call(
        expert_kernel,
        [
            ((ROWS, LANES), bf16),
            ((SLOTS, FF), bf16),
            ((SLOTS, LANES), f32),
        ],
        (y_in_rows, norm_gain.reshape(1, WIDTH), slot_first, grad_slots, d_hidden, weight_in),
        EXPERT_SPECS,
        EXPERT_SCRATCH,
        flops=8 * SLOTS * FF * WIDTH,
        moved=14 << 20,
        name="expert",
        out_specs=(HBM, HBM, VM),
    )
    back_in_rows = exchanged_by_core(back_out_rows)

    own_rows, their_rows = call(
        expert_out_kernel,
        [((ROWS // 2, LANES), bf16)] * 2,
        (
            me,
            hidden,
            y_in_rows,
            rscale,
            norm_gain.reshape(1, WIDTH),
            slot_weight,
            slot_first,
            weight_out,
        ),
        [SM] + [VM] * 6 + [HBM],
        [wide, pltpu.VMEM((WIDTH, FF), bf16), pltpu.SemaphoreType.DMA],
        flops=2 * SLOTS * FF * WIDTH,
        moved=8 << 20,
        name="expert_out",
    )
    result_rows = jnp.concatenate(
        [
            rows.reshape(CHIPS, BLOCK, LANES)
            for rows in (own_rows, from_other_core(their_rows))
        ],
        axis=1,
    ).reshape(ROWS, LANES)
    returned_rows = exchanged_by_core(result_rows)

    own_sums, their_sums = call(
        slot_sums_kernel,
        [((HP, SEQ), f32), ((HP, SEQ), bf16)],
        (me_core, back_in_rows, ranks),
        [SM, VM, VM],
        [wide],
        flops=4 * HP * SLOTS * SEQ,
        moved=4 << 20,
        name="slot_sums",
        vmem=VMEM_PART,
    )
    y_grad, back_message = call(
        grad_kernel,
        [((HP, SEQ), bf16), ((HP + 8, LANES), f32)],
        (own_sums, from_other_core(their_sums), read_vectors, dt),
        [VM] * 4,
        flops=8 * HP * LANES * SEQ,
        moved=6 << 20,
        name="mixer_grad",
    )
    after = [sent_along(back_message, -d) for d in range(1, REACH + 1)]
    (input_grad,) = call(
        backward_kernel,
        [((HP, SEQ), bf16)],
        (*after, rt, y_grad, write_vectors, read_vectors, pairs),
        [VM] * 9,
        flops=8 * HP * LANES * SEQ,
        moved=6 << 20,
        name="mixer_backward",
    )
    returned_rows, input_grad = lax.optimization_barrier((returned_rows, input_grad))
    (block_out,) = call(
        combine_kernel,
        [((WIDTH, LANES), bf16)],
        (me, ids_own, returned_rows),
        [SM, VM, VM],
        [wide],
        flops=2 * SLOTS * LANES * WIDTH,
        moved=4 << 20,
        name="combine",
        vmem=VMEM_PART,
    )
    return (block_out, input_grad)


def solution(mesh):
    placed = (
        P("exp", "ctx"),
        P(None, "ctx"),
        P(None, "ctx"),
        P("exp", "ctx"),
        P(),
        P(("ctx", "exp"), None),
        P(("ctx", "exp"), None),
        P(),
        P("exp", "ctx", None),
        P("exp", "ctx", None),
        P(None, ("ctx", "exp")),
    )
    return jax.shard_map(
        per_device,
        mesh=mesh,
        in_specs=placed,
        out_specs=(P(None, ("ctx", "exp")), P("exp", "ctx")),
        check_vma=False,
    )
```

```python
import jax
import jax.numpy as jnp
from jax import lax
from jax.experimental import pallas as pl
from jax.experimental.pallas import tpu as pltpu
from jax.sharding import PartitionSpec as P

f32 = jnp.float32
bf16 = jnp.bfloat16
i32 = jnp.int32

LANES = 128
SEQ = 4096
CHUNKS = SEQ // LANES
PAIRS = CHUNKS // 2
HP = 64
HEAD = 32
EXPERTS = 32
CHIPS = 16
CAP = 10
SLOTS = EXPERTS * CAP
BLOCK = CAP * PAIRS
ROWS = EXPERTS * BLOCK
WIDTH = 2048
FF = 768
FBLOCKS = WIDTH // LANES
REACH = 4
VMEM = 60 * 1024 * 1024
VMEM_PART = 50 * 1024 * 1024

LAST = (((1,), (1,)), ((), ()))
FIRST = (((0,), (0,)), ((), ()))


def dot(a, b):
    return jnp.dot(a, b, preferred_element_type=f32)


def dot_last(a, b):
    return lax.dot_general(a, b, LAST, preferred_element_type=f32)


def dot_first(a, b):
    return lax.dot_general(a, b, FIRST, preferred_element_type=f32)


def split3(value):
    high = value.astype(bf16)
    rest = value - high.astype(f32)
    middle = rest.astype(bf16)
    low = (rest - middle.astype(f32)).astype(bf16)
    return high, middle, low


def rows_of(first, second):
    return jnp.concatenate(
        [jnp.broadcast_to(first, (HEAD, LANES)), jnp.broadcast_to(second, (HEAD, LANES))], axis=0
    )


def earlier_mask():
    row = lax.broadcasted_iota(i32, (LANES, LANES), 0)
    col = lax.broadcasted_iota(i32, (LANES, LANES), 1)
    return jnp.where(row < col, 1.0, 0.0).astype(bf16)


def rank_table(first_ids, second_ids, earlier, experts=EXPERTS, core=None):
    expert = lax.broadcasted_iota(i32, (experts, LANES), 0)
    if core is not None:
        expert = 2 * expert + core
    expert = expert.astype(f32)
    picked = (expert == first_ids) | (expert == second_ids)
    rank = dot(jnp.where(picked, 1.0, 0.0).astype(bf16), earlier)
    return jnp.where(picked, rank, -1.0)


def slot_onehot(ranks):
    return jnp.concatenate(
        [jnp.where(ranks == float(c), 1.0, 0.0).astype(bf16) for c in range(CAP)], axis=0
    )


def round_rows(dst_ref, src_ref):
    def step(i, carry):
        at = pl.ds(pl.multiple_of(i * BLOCK, BLOCK), BLOCK)
        dst_ref[at, :] = src_ref[at, :].astype(dst_ref.dtype)
        return carry

    lax.fori_loop(0, ROWS // BLOCK, step, 0, unroll=4)


def call(kernel, outs, args, in_specs, scratch=(), flops=0, moved=0, name=None, vmem=VMEM, out_specs=None):
    vm = pl.BlockSpec(memory_space=pltpu.VMEM)
    return pl.pallas_call(
        kernel,
        out_shape=tuple(jax.ShapeDtypeStruct(shape, kind) for shape, kind in outs),
        in_specs=in_specs,
        out_specs=out_specs or tuple(vm for _ in outs),
        scratch_shapes=list(scratch),
        compiler_params=pltpu.CompilerParams(vmem_limit_bytes=vmem),
        cost_estimate=pl.CostEstimate(flops=flops, bytes_accessed=moved, transcendentals=0),
        name=name,
    )(*args)


VM = pl.BlockSpec(memory_space=pltpu.VMEM)
SM = pl.BlockSpec(memory_space=pltpu.SMEM)
HBM = pl.BlockSpec(memory_space=pltpu.HBM)


def grad_rows_kernel(core_ref, own_ids_ref, their_ids_ref, own_ref, their_ref, out_ref, wide_ref):
    core = core_ref[0]
    earlier = earlier_mask()

    def select_of(ids_ref):
        return slot_onehot(rank_table(ids_ref[0:1, :], ids_ref[1:2, :], earlier, CHIPS, core))

    own_select, their_select = select_of(own_ids_ref), select_of(their_ids_ref)

    def step(fb, carry):
        feats = pl.ds(pl.multiple_of(fb * LANES, LANES), LANES)
        for select, grad_ref, side in (
            (own_select, own_ref, core),
            (their_select, their_ref, 1 - core),
        ):
            rows = dot_last(select, grad_ref[feats, :])
            for c in range(CAP):
                wide_ref[pl.ds(side * BLOCK + c * FBLOCKS + fb, CHIPS, stride=2 * BLOCK), :] = rows[
                    c * CHIPS : (c + 1) * CHIPS
                ]
        return carry

    lax.fori_loop(0, FBLOCKS, step, 0, unroll=4)
    round_rows(out_ref, wide_ref)


def tables_kernel(docs_ref, base_ref, decay_ref, x_ref, write_ref, rt_ref, dt_ref, msg_ref):
    decay = decay_ref[...]
    row_i = lax.broadcasted_iota(i32, (LANES, LANES), 0)
    col_i = lax.broadcasted_iota(i32, (LANES, LANES), 1)
    upto = jnp.where(row_i <= col_i, 1.0, 0.0).astype(bf16)
    cum = sum(dot(part, upto) for part in split3(decay))
    rows = 2 * CHUNKS
    chunk_end = jnp.broadcast_to(cum[:, LANES - 1 : LANES], (rows, LANES))
    row_j = lax.broadcasted_iota(i32, (rows, rows), 0)
    col_j = lax.broadcasted_iota(i32, (rows, rows), 1)
    same_head = (row_j >= CHUNKS) == (col_j >= CHUNKS)
    before = jnp.where(same_head & (col_j < row_j), 1.0, 0.0).astype(bf16)
    after = jnp.where(same_head & (col_j > row_j), 1.0, 0.0).astype(bf16)
    parts = split3(chunk_end)
    prefix = sum(dot(before, part) for part in parts)
    suffix = sum(dot(after, part) for part in parts)
    chunk = lax.broadcasted_iota(i32, (rows, LANES), 0)
    chunk = jnp.where(chunk >= CHUNKS, chunk - CHUNKS, chunk)
    token = lax.broadcasted_iota(i32, (rows, LANES), 1)
    place = chunk * LANES + token
    base = base_ref[0]
    doc_start = jnp.full((rows, LANES), -(1 << 20), i32)
    last_start = jnp.int32(-(1 << 20))
    start = -base
    for j in range(docs_ref.shape[0]):
        doc_start = jnp.where(place >= start, jnp.maximum(doc_start, start), doc_start)
        last_start = jnp.where(start <= SEQ - 1, jnp.maximum(last_start, start), last_start)
        start = start + docs_ref[j]
    inner_start = jnp.maximum(doc_start - chunk * LANES, -1)
    inner_float = inner_start.astype(f32)
    inner_last = jnp.broadcast_to(inner_float[:, LANES - 1 : LANES], (rows, LANES))
    to_end = chunk_end - cum
    entering = jnp.where(inner_start < 0, jnp.exp(cum), 0.0)
    leaving = jnp.where(token.astype(f32) >= inner_last, jnp.exp(to_end), 0.0)
    dev_entering = jnp.where(doc_start < 0, jnp.exp(prefix + cum), 0.0)
    dev_leaving = jnp.where(place >= last_start, jnp.exp(to_end + suffix), 0.0)
    for r, value in enumerate(
        (
            cum[:CHUNKS],
            cum[CHUNKS:],
            entering[:CHUNKS],
            entering[CHUNKS:],
            leaving[:CHUNKS],
            leaving[CHUNKS:],
            inner_float[:CHUNKS],
            inner_float[CHUNKS:],
        )
    ):
        rt_ref[pl.ds(r, CHUNKS, stride=8), :] = value
    zero = jnp.zeros((CHUNKS, LANES), f32)
    for r, value in enumerate(
        (
            dev_entering[:CHUNKS],
            dev_entering[CHUNKS:],
            dev_leaving[:CHUNKS],
            dev_leaving[CHUNKS:],
            zero,
            zero,
            zero,
            zero,
        )
    ):
        dt_ref[pl.ds(r, CHUNKS, stride=8), :] = value

    def step(k, acc):
        lanes = pl.ds(pl.multiple_of(k * LANES, LANES), LANES)
        rows_k = dt_ref[pl.ds(pl.multiple_of(k * 8, 8), 8), :]
        scaled = x_ref[:, lanes].astype(f32) * rows_of(rows_k[2:3], rows_k[3:4])
        return acc + dot_last(scaled.astype(bf16), write_ref[:, lanes])

    acc = lax.fori_loop(0, CHUNKS, step, jnp.zeros((HP, LANES), f32), unroll=4)
    msg_ref[0:HP, :] = acc
    through = jnp.concatenate(
        [
            jnp.broadcast_to(dev_entering[CHUNKS - 1 : CHUNKS, LANES - 1 : LANES], (1, LANES)),
            jnp.broadcast_to(dev_entering[rows - 1 : rows, LANES - 1 : LANES], (1, LANES)),
            jnp.zeros((6, LANES), f32),
        ],
        axis=0,
    )
    msg_ref[HP : HP + 8, :] = through


def chained(refs):
    state = refs[-1][0:HP, :]
    for ref in refs[-2::-1]:
        state = ref[0:HP, :] + rows_of(ref[HP : HP + 1, :], ref[HP + 1 : HP + 2, :]) * state
    return state


def forward_kernel(
    m1_ref, m2_ref, m3_ref, m4_ref, rt_ref, x_ref, write_ref, read_ref, y_ref, pair_ref
):
    row_i = lax.broadcasted_iota(i32, (LANES, LANES), 0)
    col_i = lax.broadcasted_iota(i32, (LANES, LANES), 1)
    causal = row_i <= col_i
    row_f = row_i.astype(f32)

    def step(k, state):
        lanes = pl.ds(pl.multiple_of(k * LANES, LANES), LANES)
        rows = rt_ref[pl.ds(pl.multiple_of(k * 8, 8), 8), :]
        cols = rows.T
        x = x_ref[:, lanes]
        write = write_ref[:, lanes]
        read = read_ref[:, lanes]
        scores = dot_first(write, read)
        valid = causal & (row_f >= rows[6:7, :])
        inside = []
        for h in range(2):
            gap = rows[h : h + 1, :] - cols[:, h : h + 1]
            pair = jnp.where(valid, jnp.exp(gap) * scores, 0.0).astype(bf16)
            pair_ref[pl.ds(pl.multiple_of((2 * k + h) * LANES, LANES), LANES), :] = pair
            inside.append(dot(x[h * HEAD : (h + 1) * HEAD, :], pair))
        carried = dot(state.astype(bf16), read) * rows_of(rows[2:3], rows[3:4])
        y_ref[:, lanes] = (jnp.concatenate(inside, axis=0) + carried).astype(bf16)
        scaled = (x.astype(f32) * rows_of(rows[4:5], rows[5:6])).astype(bf16)
        through = rows_of(
            jnp.broadcast_to(rows[2:3, LANES - 1 : LANES], (1, LANES)),
            jnp.broadcast_to(rows[3:4, LANES - 1 : LANES], (1, LANES)),
        )
        return through * state + dot_last(scaled, write)

    lax.fori_loop(0, CHUNKS, step, chained((m1_ref, m2_ref, m3_ref, m4_ref)), unroll=4)


def dispatch_kernel(
    expert_ref, own_ref, their_ref, ids_ref, msg_ref, rank_ref, weight_ref, first_ref, wide_ref
):
    core = lax.rem(expert_ref[0], 2)
    earlier = earlier_mask()
    mine = expert_ref[0].astype(f32)
    is_first = ids_ref[0] == mine
    is_second = ids_ref[1] == mine
    picked = is_first | is_second
    rank = dot(jnp.where(picked, 1.0, 0.0).astype(bf16), earlier)
    rank = jnp.where(picked, rank, -1.0)
    route = jnp.where(is_first, ids_ref[2], jnp.where(is_second, ids_ref[3], 0.0))
    first = jnp.where(is_first, 1.0, 0.0)
    for c in range(CAP):
        here = rank == float(c)
        route_c = jnp.sum(jnp.where(here, route, 0.0), axis=1, keepdims=True)
        first_c = jnp.sum(jnp.where(here, first, 0.0), axis=1, keepdims=True)
        for par in range(2):
            at = (par * CAP + c) * PAIRS
            part = slice(par * PAIRS, (par + 1) * PAIRS)
            weight_ref[at : at + PAIRS, :] = jnp.broadcast_to(route_c[part], (PAIRS, LANES))
            first_ref[at : at + PAIRS, :] = jnp.broadcast_to(first_c[part], (PAIRS, LANES))

    def step(jp, carry):
        for par in range(2):
            j = par * PAIRS + jp
            table = rank_table(
                ids_ref[0, pl.ds(j, 1), :], ids_ref[1, pl.ds(j, 1), :], earlier, CHIPS, core
            )
            rank_ref[pl.ds(pl.multiple_of((2 * jp + par) * CHIPS, CHIPS), CHIPS), :] = table
            lanes = pl.ds(pl.multiple_of((2 * jp + par) * LANES, LANES), LANES)
            own = own_ref[:, lanes]
            their = their_ref[:, lanes]
            both = jnp.concatenate(
                [jnp.where(core == 0, own, their), jnp.where(core == 0, their, own)], axis=0
            )
            rows = dot_last(slot_onehot(table), both)
            for c in range(CAP):
                at = par * BLOCK + c * PAIRS + jp
                wide_ref[pl.ds(at, CHIPS, stride=2 * BLOCK), :] = rows[c * CHIPS : (c + 1) * CHIPS]
        return carry

    lax.fori_loop(0, PAIRS, step, 0, unroll=2)
    round_rows(msg_ref, wide_ref)


def arrived_grad_kernel(
    rows_ref, weight_ref, out_hbm, grad_ref, dhid_ref, wide_ref, scaled_ref, out_ref, sem
):
    fetch = pltpu.make_async_copy(out_hbm.at[:, pl.ds(2 * FF, FF)], out_ref, sem)
    fetch.start()
    round_rows(wide_ref, rows_ref)

    def unpack(fb, carry):
        lanes = pl.ds(pl.multiple_of(fb * LANES, LANES), LANES)
        for par in range(2):
            for c in range(CAP):
                at = (par * CAP + c) * PAIRS
                rows = wide_ref[
                    pl.ds(par * BLOCK + c * FBLOCKS + fb, PAIRS, stride=2 * BLOCK), :
                ]
                grad_ref[at : at + PAIRS, lanes] = rows.astype(bf16)
                scaled_ref[at : at + PAIRS, lanes] = (
                    rows * weight_ref[at : at + PAIRS, :]
                ).astype(bf16)
        return carry

    lax.fori_loop(0, FBLOCKS, unpack, 0, unroll=2)
    fetch.wait()

    def matmul(i, carry):
        lanes = pl.ds(pl.multiple_of(i * 256, 256), 256)
        dhid_ref[:, lanes] = dot(scaled_ref[...], out_ref[:, lanes])
        return carry

    lax.fori_loop(0, FF // 256, matmul, 0)


EXPERT_SPECS = [VM, VM, HBM, HBM, HBM, HBM]
EXPERT_SCRATCH = [
    pltpu.VMEM((SLOTS, WIDTH), f32),
    pltpu.VMEM((SLOTS, WIDTH), f32),
    pltpu.VMEM((SLOTS, 2 * FF), bf16),
    pltpu.VMEM((WIDTH, 2 * FF), bf16),
    pltpu.VMEM((SLOTS, LANES), f32),
    pltpu.VMEM((SLOTS, WIDTH), bf16),
    pltpu.VMEM((SLOTS, FF), f32),
    pltpu.VMEM((SLOTS, WIDTH), bf16),
    pltpu.VMEM((SLOTS, FF), bf16),
    pltpu.VMEM((ROWS, LANES), bf16),
    pltpu.SemaphoreType.DMA((4,)),
    pltpu.SemaphoreType.DMA,
    pltpu.SemaphoreType.DMA((4,)),
]


def expert_kernel(
    rows_ref,
    gain_ref,
    first_hbm,
    grad_hbm,
    dhid_hbm,
    in_hbm,
    msg_hbm,
    hidden_hbm,
    rscale_out_ref,
    y_ref,
    scaled_ref,
    dcat_ref,
    in_ref,
    first_ref,
    grad_ref,
    dhid_ref,
    gained_ref,
    hidden_ref,
    msg_ref,
    fetch_sems,
    store_sem,
    msg_sems,
):
    fetches = [
        pltpu.make_async_copy(src, dst, fetch_sems.at[i])
        for i, (src, dst) in enumerate(
            (
                (in_hbm.at[:, pl.ds(0, 2 * FF)], in_ref),
                (dhid_hbm, dhid_ref),
                (grad_hbm, grad_ref),
                (first_hbm, first_ref),
            )
        )
    ]
    for fetch in fetches:
        fetch.start()
    keep_hidden = pltpu.make_async_copy(hidden_ref, hidden_hbm, store_sem)

    def unpack(k, squares):
        lanes = pl.ds(pl.multiple_of(k * LANES, LANES), LANES)
        y = rows_ref[pl.ds(pl.multiple_of(k * SLOTS, SLOTS), SLOTS), :].astype(f32)
        y_ref[:, lanes] = y
        gained_ref[:, lanes] = (y * gain_ref[:, lanes]).astype(bf16)
        return squares + y * y

    squares = lax.fori_loop(0, FBLOCKS, unpack, jnp.zeros((SLOTS, LANES), f32), unroll=2)
    mean = jnp.sum(squares, axis=1, keepdims=True) * (1.0 / WIDTH)
    rscale = lax.rsqrt(mean + 1e-06)
    rscale_b = jnp.broadcast_to(rscale, (SLOTS, LANES))

    rscale_out_ref[...] = rscale_b
    rscale2 = jnp.concatenate([rscale_b, rscale_b], axis=1)
    fetches[0].wait()
    fetches[1].wait()

    def project(i, carry):
        lanes = pl.ds(pl.multiple_of(i * 256, 256), 256)
        lanes_up = pl.ds(pl.multiple_of(FF + i * 256, 256), 256)
        gate = rscale2 * dot(gained_ref[...], in_ref[:, lanes])
        up = rscale2 * dot(gained_ref[...], in_ref[:, lanes_up])
        sigmoid = 1.0 / (1.0 + jnp.exp(-gate))
        swish = gate * sigmoid
        hidden_ref[:, lanes] = (swish * up).astype(bf16)
        dhid = dhid_ref[:, lanes]
        dcat_ref[:, lanes] = (dhid * up * sigmoid * (1.0 + gate * (1.0 - sigmoid))).astype(bf16)
        dcat_ref[:, lanes_up] = (dhid * swish).astype(bf16)
        return carry

    lax.fori_loop(0, FF // 256, project, 0, unroll=True)
    keep_hidden.start()
    fetches[2].wait()
    fetches[3].wait()
    first = first_ref[...]
    first2 = jnp.concatenate([first, first], axis=1)

    def back(i, acc):
        at = pl.multiple_of(i * 256, 256)
        lanes = pl.ds(at, 256)
        grad = dot_last(dcat_ref[...], in_ref[lanes, :]) + first2 * grad_ref[:, lanes].astype(f32)
        scaled = grad * gain_ref[:, lanes]
        scaled_ref[:, lanes] = scaled
        product = scaled * y_ref[:, lanes]
        return acc + product[:, :LANES] + product[:, LANES:]

    acc = lax.fori_loop(0, WIDTH // 256, back, jnp.zeros((SLOTS, LANES), f32), unroll=8)
    mean_grad = jnp.sum(acc, axis=1, keepdims=True) * (1.0 / WIDTH)
    pull = jnp.broadcast_to(rscale * rscale * rscale * mean_grad, (SLOTS, LANES))

    parts = 4
    sends = []
    for part in range(parts):
        for k in range(part * FBLOCKS // parts, (part + 1) * FBLOCKS // parts):
            lanes = slice(k * LANES, (k + 1) * LANES)
            msg_ref[k * SLOTS : (k + 1) * SLOTS, :] = (
                rscale_b * scaled_ref[:, lanes] - pull * y_ref[:, lanes]
            ).astype(bf16)
        rows = pl.ds(part * (ROWS // parts), ROWS // parts)
        sends.append(
            pltpu.make_async_copy(msg_ref.at[rows, :], msg_hbm.at[rows, :], msg_sems.at[part])
        )
        sends[-1].start()
    for copy in (keep_hidden, *sends):
        copy.wait()


def expert_out_kernel(
    expert_ref,
    hidden_ref,
    rows_ref,
    rscale_ref,
    gain_ref,
    weight_ref,
    first_ref,
    out_hbm,
    own_ref,
    their_ref,
    wide_ref,
    out_ref,
    sem,
):
    fetch = pltpu.make_async_copy(out_hbm.at[:, pl.ds(2 * FF, FF)], out_ref, sem)
    fetch.start()
    core = lax.rem(expert_ref[0], 2)
    weight = weight_ref[...]
    weight2 = jnp.concatenate([weight, weight], axis=1)
    first = first_ref[...] * rscale_ref[...]
    fetch.wait()

    def matmul(i, carry):
        lanes = pl.ds(pl.multiple_of(i * 256, 256), 256)
        result = dot_last(hidden_ref[...], out_ref[lanes, :])
        result = weight2 * result
        for half in range(2):
            fb = 2 * i + half
            y = rows_ref[pl.ds(pl.multiple_of(fb * SLOTS, SLOTS), SLOTS), :].astype(f32)
            gain = gain_ref[:, pl.ds(pl.multiple_of(fb * LANES, LANES), LANES)]
            part = result[:, half * LANES : (half + 1) * LANES] + first * (y * gain)
            for par in range(2):
                for c in range(CAP):
                    at = (par * CAP + c) * PAIRS
                    wide_ref[
                        pl.ds(par * (ROWS // 2) + c * FBLOCKS + fb, PAIRS, stride=BLOCK), :
                    ] = part[at : at + PAIRS]
        return carry

    lax.fori_loop(0, WIDTH // 256, matmul, 0)
    half_rows = ROWS // 2

    def split(i, carry):
        at = pl.multiple_of(i * BLOCK, BLOCK)
        own_at = pl.multiple_of(core * half_rows + at, BLOCK)
        their_at = pl.multiple_of((1 - core) * half_rows + at, BLOCK)
        own_ref[pl.ds(at, BLOCK), :] = wide_ref[pl.ds(own_at, BLOCK), :].astype(bf16)
        their_ref[pl.ds(at, BLOCK), :] = wide_ref[pl.ds(their_at, BLOCK), :].astype(bf16)
        return carry

    lax.fori_loop(0, CHIPS, split, 0, unroll=2)


def combine_kernel(expert_ref, ids_ref, rows_ref, out_ref, wide_ref):
    round_rows(wide_ref, rows_ref)
    core = lax.rem(expert_ref[0], 2)
    earlier = earlier_mask()
    select = jnp.concatenate(
        [
            slot_onehot(rank_table(ids_ref[0:1, :], ids_ref[1:2, :], earlier, CHIPS, side))
            for side in (core, 1 - core)
        ],
        axis=0,
    )

    def step(fb, carry):
        rows = jnp.concatenate(
            [
                wide_ref[
                    pl.ds(side * BLOCK + c * FBLOCKS + fb, CHIPS, stride=2 * BLOCK), :
                ].astype(bf16)
                for side in range(2)
                for c in range(CAP)
            ],
            axis=0,
        )
        at = pl.multiple_of(fb * LANES, LANES)
        out_ref[pl.ds(at, LANES), :] = dot_first(rows, select).astype(bf16)
        return carry

    lax.fori_loop(0, FBLOCKS, step, 0, unroll=8)


def slot_sums_kernel(core_ref, rows_ref, rank_ref, own_ref, their_ref, wide_ref):
    round_rows(wide_ref, rows_ref)
    core = core_ref[0]

    def step(jp, carry):
        for par in range(2):
            ranks = rank_ref[pl.ds(pl.multiple_of((2 * jp + par) * CHIPS, CHIPS), CHIPS), :]
            rows = jnp.concatenate(
                [
                    wide_ref[
                        pl.ds(par * BLOCK + c * PAIRS + jp, CHIPS, stride=2 * BLOCK), :
                    ].astype(bf16)
                    for c in range(CAP)
                ],
                axis=0,
            )
            sums = dot_first(rows, slot_onehot(ranks))
            low, high = sums[:HP], sums[HP:]
            lanes = pl.ds(pl.multiple_of((2 * jp + par) * LANES, LANES), LANES)
            own_ref[:, lanes] = jnp.where(core == 0, low, high)
            their_ref[:, lanes] = jnp.where(core == 0, high, low).astype(bf16)
        return carry

    lax.fori_loop(0, PAIRS, step, 0, unroll=2)


def grad_kernel(own_ref, their_ref, read_ref, dt_ref, out_ref, msg_ref):
    def step(k, acc):
        lanes = pl.ds(pl.multiple_of(k * LANES, LANES), LANES)
        grad = (own_ref[:, lanes] + their_ref[:, lanes].astype(f32)).astype(bf16)
        out_ref[:, lanes] = grad
        rows_k = dt_ref[pl.ds(pl.multiple_of(k * 8, 8), 8), :]
        weighted = (grad.astype(f32) * rows_of(rows_k[0:1], rows_k[1:2])).astype(bf16)
        return acc + dot_last(weighted, read_ref[:, lanes])

    acc = lax.fori_loop(0, CHUNKS, step, jnp.zeros((HP, LANES), f32), unroll=4)
    msg_ref[0:HP, :] = acc
    last = dt_ref[(CHUNKS - 1) * 8 : CHUNKS * 8, :]
    msg_ref[HP : HP + 8, :] = jnp.broadcast_to(last[:, LANES - 1 : LANES], (8, LANES))


def backward_kernel(
    m1_ref, m2_ref, m3_ref, m4_ref, rt_ref, grad_ref, write_ref, read_ref, pair_ref, out_ref
):
    def step(i, state):
        k = CHUNKS - 1 - i
        lanes = pl.ds(pl.multiple_of(k * LANES, LANES), LANES)
        rows = rt_ref[pl.ds(pl.multiple_of(k * 8, 8), 8), :]
        grad = grad_ref[:, lanes]
        write = write_ref[:, lanes]
        read = read_ref[:, lanes]
        inside = []
        for h in range(2):
            pair = pair_ref[pl.ds(pl.multiple_of((2 * k + h) * LANES, LANES), LANES), :]
            inside.append(dot_last(grad[h * HEAD : (h + 1) * HEAD, :], pair))
        carried = dot(state.astype(bf16), write) * rows_of(rows[4:5], rows[5:6])
        out_ref[:, lanes] = (jnp.concatenate(inside, axis=0) + carried).astype(bf16)
        scaled = (grad.astype(f32) * rows_of(rows[2:3], rows[3:4])).astype(bf16)
        through = rows_of(
            jnp.broadcast_to(rows[2:3, LANES - 1 : LANES], (1, LANES)),
            jnp.broadcast_to(rows[3:4, LANES - 1 : LANES], (1, LANES)),
        )
        return through * state + dot_last(scaled, read)

    lax.fori_loop(0, CHUNKS, step, chained((m1_ref, m2_ref, m3_ref, m4_ref)), unroll=4)


def sent_along(value, by):
    size = lax.axis_size("ctx")
    pairs = [(i, i + by) for i in range(size) if 0 <= i + by < size]
    return lax.ppermute(value, "ctx", pairs)


def exchanged_by_core(rows):
    blocks = rows.reshape(CHIPS, SLOTS, LANES)
    groups = [list(range(core, EXPERTS, 2)) for core in range(2)]
    return lax.all_to_all(
        blocks, "exp", split_axis=0, concat_axis=0, tiled=True, axis_index_groups=groups
    ).reshape(ROWS, LANES)


def from_other_core(value):
    return lax.ppermute(value, "exp", [(i, i ^ 1) for i in range(EXPERTS)])


def per_device(
    features,
    write_vectors,
    read_vectors,
    log_decay,
    doc_lengths,
    expert_ids,
    route_weights,
    norm_gain,
    expert_in,
    expert_out,
    out_grad,
):
    me_ctx = lax.axis_index("ctx")
    me_exp = lax.axis_index("exp")
    wide = pltpu.VMEM((ROWS + SLOTS, LANES), f32)
    ids_own = expert_ids.T.astype(f32)
    tokens_sent = jnp.concatenate(
        [
            jnp.broadcast_to(ids_own[None], (EXPERTS, 2, LANES)),
            jnp.broadcast_to(route_weights.T[None], (EXPERTS, 2, LANES)),
        ],
        axis=1,
    )
    tokens_sent, expert_in, expert_out, out_grad, ids_own = lax.optimization_barrier(
        (tokens_sent, expert_in, expert_out, out_grad, ids_own)
    )
    tokens = lax.all_to_all(tokens_sent, "exp", 0, 0, tiled=True)
    tokens = tokens.reshape(PAIRS, 2, 4, LANES).transpose(2, 1, 0, 3).reshape(4, CHUNKS, LANES)

    me_core = lax.rem(me_exp, 2).astype(i32).reshape(1)
    me = me_exp.astype(i32).reshape(1)

    their_ids = from_other_core(ids_own)
    their_grad = from_other_core(out_grad)
    (grad_out_rows,) = call(
        grad_rows_kernel,
        [((ROWS, LANES), bf16)],
        (me_core, ids_own, their_ids, out_grad, their_grad),
        [SM] + [VM] * 4,
        [wide],
        flops=2 * SLOTS * LANES * WIDTH,
        moved=4 << 20,
        name="grad_rows",
    )

    grad_in_rows = exchanged_by_core(grad_out_rows)
    weights = lax.all_gather(
        jnp.concatenate([expert_in, expert_out], axis=2), "ctx", axis=1, tiled=True
    )[0]

    rt, dt, message = call(
        tables_kernel,
        [((CHUNKS * 8 + 8, LANES), f32), ((CHUNKS * 8 + 8, LANES), f32), ((HP + 8, LANES), f32)],
        (
            doc_lengths,
            (me_ctx * SEQ).astype(i32).reshape(1),
            log_decay.reshape(2 * CHUNKS, LANES),
            features,
            write_vectors,
        ),
        [SM, SM, VM, VM, VM],
        flops=2 * HP * LANES * SEQ,
        moved=3 << 20,
        name="shard_state",
    )
    before = [sent_along(message, d) for d in range(1, REACH + 1)]
    y_own, pairs = call(
        forward_kernel,
        [((HP, SEQ), bf16), ((2 * CHUNKS * LANES, LANES), bf16)],
        (*before, rt, features, write_vectors, read_vectors),
        [VM] * 8,
        flops=8 * HP * LANES * SEQ,
        moved=9 << 20,
        name="mixer_forward",
    )
    y_their = from_other_core(y_own)
    y_out_rows, ranks, slot_weight, slot_first = call(
        dispatch_kernel,
        [
            ((ROWS, LANES), bf16),
            ((CHUNKS * CHIPS, LANES), f32),
            ((SLOTS, LANES), f32),
            ((SLOTS, LANES), f32),
        ],
        (me, y_own, y_their, tokens),
        [SM] + [VM] * 3,
        [wide],
        flops=4 * HP * SLOTS * SEQ,
        moved=4 << 20,
        name="dispatch",
    )
    y_in_rows = exchanged_by_core(y_out_rows)

    grad_slots, d_hidden = call(
        arrived_grad_kernel,
        [((SLOTS, WIDTH), bf16), ((SLOTS, FF), f32)],
        (grad_in_rows, slot_weight, weights),
        [VM, VM, HBM],
        [wide, pltpu.VMEM((SLOTS, WIDTH), bf16), pltpu.VMEM((WIDTH, FF), bf16), pltpu.SemaphoreType.DMA],
        flops=2 * SLOTS * FF * WIDTH,
        moved=8 << 20,
        name="hidden_grad",
        vmem=VMEM_PART,
    )
    back_out_rows, hidden, rscale = call(
        expert_kernel,
        [
            ((ROWS, LANES), bf16),
            ((SLOTS, FF), bf16),
            ((SLOTS, LANES), f32),
        ],
        (y_in_rows, norm_gain.reshape(1, WIDTH), slot_first, grad_slots, d_hidden, weights),
        EXPERT_SPECS,
        EXPERT_SCRATCH,
        flops=8 * SLOTS * FF * WIDTH,
        moved=14 << 20,
        name="expert",
        out_specs=(HBM, HBM, VM),
    )
    back_in_rows = exchanged_by_core(back_out_rows)

    own_rows, their_rows = call(
        expert_out_kernel,
        [((ROWS // 2, LANES), bf16)] * 2,
        (
            me,
            hidden,
            y_in_rows,
            rscale,
            norm_gain.reshape(1, WIDTH),
            slot_weight,
            slot_first,
            weights,
        ),
        [SM] + [VM] * 6 + [HBM],
        [wide, pltpu.VMEM((WIDTH, FF), bf16), pltpu.SemaphoreType.DMA],
        flops=2 * SLOTS * FF * WIDTH,
        moved=8 << 20,
        name="expert_out",
    )
    result_rows = jnp.concatenate(
        [
            rows.reshape(CHIPS, BLOCK, LANES)
            for rows in (own_rows, from_other_core(their_rows))
        ],
        axis=1,
    ).reshape(ROWS, LANES)
    returned_rows = exchanged_by_core(result_rows)

    own_sums, their_sums = call(
        slot_sums_kernel,
        [((HP, SEQ), f32), ((HP, SEQ), bf16)],
        (me_core, back_in_rows, ranks),
        [SM, VM, VM],
        [wide],
        flops=4 * HP * SLOTS * SEQ,
        moved=4 << 20,
        name="slot_sums",
        vmem=VMEM_PART,
    )
    y_grad, back_message = call(
        grad_kernel,
        [((HP, SEQ), bf16), ((HP + 8, LANES), f32)],
        (own_sums, from_other_core(their_sums), read_vectors, dt),
        [VM] * 4,
        flops=8 * HP * LANES * SEQ,
        moved=6 << 20,
        name="mixer_grad",
    )
    after = [sent_along(back_message, -d) for d in range(1, REACH + 1)]
    (input_grad,) = call(
        backward_kernel,
        [((HP, SEQ), bf16)],
        (*after, rt, y_grad, write_vectors, read_vectors, pairs),
        [VM] * 9,
        flops=8 * HP * LANES * SEQ,
        moved=6 << 20,
        name="mixer_backward",
    )
    returned_rows, input_grad = lax.optimization_barrier((returned_rows, input_grad))
    (block_out,) = call(
        combine_kernel,
        [((WIDTH, LANES), bf16)],
        (me, ids_own, returned_rows),
        [SM, VM, VM],
        [wide],
        flops=2 * SLOTS * LANES * WIDTH,
        moved=4 << 20,
        name="combine",
        vmem=VMEM_PART,
    )
    return (block_out, input_grad)


def solution(mesh):
    placed = (
        P("exp", "ctx"),
        P(None, "ctx"),
        P(None, "ctx"),
        P("exp", "ctx"),
        P(),
        P(("ctx", "exp"), None),
        P(("ctx", "exp"), None),
        P(),
        P("exp", "ctx", None),
        P("exp", "ctx", None),
        P(None, ("ctx", "exp")),
    )
    return jax.shard_map(
        per_device,
        mesh=mesh,
        in_specs=placed,
        out_specs=(P(None, ("ctx", "exp")), P("exp", "ctx")),
        check_vma=False,
    )
```
